32 devices in a mesh: dp: 8 (over z, x), blk: 4 (over y, core).
Axes of the slice: x: 2, y: 2, z: 4, core: 2. Of those that a mesh axis runs over, the one named last changes fastest.
Arguments:
- block_input: bfloat16 [2, 32, 1024, 512], P(None, 'dp', 'blk'), may hold values from -6 to 6
- segment_ids: int32 [32, 1024], P('dp', 'blk'), may hold values from 0 to 3, as said below
- gain_one: float32 [512], replicated, may hold values from 0.5 to 1.5
- w_query: bfloat16 [512, 512], replicated, may hold values from -0.25 to 0.25
- w_key: bfloat16 [512, 512], replicated, may hold values from -0.25 to 0.25
- w_value: bfloat16 [512, 512], replicated, may hold values from -0.25 to 0.25
- w_out: bfloat16 [512, 512], replicated, may hold values from -1 to 1
- gain_two: float32 [512], replicated, may hold values from 0.5 to 1.5
- w_ctrl: bfloat16 [512, 2], replicated, may hold values from -0.1875 to 0.1875
- w_in: bfloat16 [2, 512, 2048], replicated, may hold values from -1.5 to 1.5
- w_back: bfloat16 [2, 2048, 512], replicated, may hold values from -3 to 3
- cotangent: bfloat16 [2, 32, 1024, 512], P(None, 'dp', 'blk'), may hold values from -6 to 6
Outputs:
- activations: bfloat16 [2, 32, 1024, 512], P(None, 'dp', 'blk')
- grad_input: bfloat16 [2, 32, 1024, 512], P(None, 'dp', 'blk')
- grad_gain_one: float32 [512], replicated
- grad_query: float32 [512, 512], replicated
- grad_key: float32 [512, 512], replicated
- grad_value: float32 [512, 512], replicated
- grad_out: float32 [512, 512], replicated
- grad_gain_two: float32 [512], replicated
- grad_ctrl: float32 [512, 2], replicated
- grad_in: float32 [2, 512, 2048], replicated
- grad_back: float32 [2, 2048, 512], replicated
The draws below stay inside these ranges and needn't reach their ends.
Inputs may be any that keep to these rules, and one draw needn't show every extreme that they name: `segment_ids`: ids start at 0 and never fall along a row; they rise by one at each document start, and document k >= 1 begins fewer than 128 positions away from k * 256.
All inputs are finite; a program needn't handle non-finite values.
Results may differ from the reference program's by a relative error of at most 0.03.
Values may be sent and summed in bfloat16 or wider, within the bound.
A program may use at most 256 MiB of HBM per device.

```python
import jax
import jax.numpy as jnp
from jax import lax

D = 512
HEADS = 8
HEAD_DIM = 64
FF = 2048
EXPERTS = 2
GROUP = 32
TOK_BLK = 256
MICRO = 2
LENGTH = 1024
SEQS = 32


def draw_segment_ids(key, part):
    key = jax.random.fold_in(key, 11)
    doc_count = LENGTH // TOK_BLK
    jitter = jax.random.randint(key, (SEQS, doc_count - 1), 1 - TOK_BLK // 2, TOK_BLK // 2)
    starts = (jnp.arange(1, doc_count, dtype=jnp.int32) * TOK_BLK)[None, :] + jitter
    position = jnp.arange(LENGTH, dtype=jnp.int32)
    crossed = (position[None, :, None] >= starts[:, None, :]).astype(jnp.int32)
    return jnp.sum(crossed, axis=-1).astype(jnp.int32)


def steps_of(stream_key, dims, shards, smallest, largest):
    loudness = 1.0
    for dim, shards_of in shards:
        steps = jax.random.uniform(jax.random.fold_in(jax.random.fold_in(stream_key, 6), dim), (shards_of,), jnp.float32, smallest / len(shards), largest / len(shards))
        loudness = loudness * jnp.repeat(jnp.exp(steps), dims[dim] // shards_of).reshape((-1,) + (1,) * (len(dims) - 1 - dim))
    return loudness


def centred(rng, dims, scale, limit, shards=(), kind=jnp.bfloat16):
    level = steps_of(rng, dims, shards, -0.22, 0.18) if shards else 1.0
    drawn = jax.random.normal(rng, dims, jnp.float32) * scale * level
    return jnp.minimum(jnp.maximum(drawn, -limit), limit).astype(kind)


def setup_inputs(seed: int = 0) -> dict:
    arg_keys = jax.random.split(jax.random.key(seed), 13)
    return {
        "block_input": centred(arg_keys[0], (MICRO, SEQS, LENGTH, D), 1.0, 6.0, ((1, 8), (2, 4))),
        "segment_ids": draw_segment_ids(jax.random.fold_in(arg_keys[12], 71), 0),
        "gain_one": jnp.clip(1.0 + 0.1 * jax.random.normal(arg_keys[2], (D,), jnp.float32), 0.5, 1.5),
        "w_query": centred(arg_keys[3], (D, D), D ** -0.5, 0.25),
        "w_key": centred(arg_keys[4], (D, D), D ** -0.5, 0.25),
        "w_value": centred(arg_keys[5], (D, D), D ** -0.5, 0.25),
        "w_out": centred(arg_keys[6], (D, D), (D // 16) ** -0.5, 1.0),
        "gain_two": jnp.clip(1.0 + 0.1 * jax.random.normal(arg_keys[7], (D,), jnp.float32), 0.5, 1.5),
        "w_ctrl": centred(arg_keys[8], (D, EXPERTS), (2 * D) ** -0.5, 0.1875),
        "w_in": centred(arg_keys[9], (EXPERTS, D, FF), (D // 32) ** -0.5, 1.5),
        "w_back": centred(arg_keys[10], (EXPERTS, FF, D), (max(FF // 512, 1)) ** -0.5, 3.0),
        "cotangent": centred(arg_keys[11], (MICRO, SEQS, LENGTH, D), 1.0, 6.0, ((1, 8), (2, 4))),
    }


@jax.custom_vjp
def low(v):
    return lax.optimization_barrier(v.astype(jnp.bfloat16)).astype(jnp.float32)

@jax.custom_vjp
def low_back(v):
    return v

def low_keep(v):
    return (low(v), None)

def low_pass(kept, grad):
    return (grad,)

def back_keep(v):
    return (v, None)

def back_low(kept, grad):
    return (low(grad),)
low.defvjp(low_keep, low_pass)
low_back.defvjp(back_keep, back_low)
EPSILON = 1e-05

def normalize(values, scale_gain):
    return values * lax.rsqrt(lax.optimization_barrier(jnp.mean(values * values, axis=-1, keepdims=True)) + EPSILON) * scale_gain

def layer_one(inputs, segments, params):
    gain_one, w_query, w_key, w_value, w_out, gain_two, w_ctrl, w_in, w_back = params
    highest = lax.Precision.HIGHEST
    length = inputs.shape[0]
    normed_one = low(normalize(inputs, gain_one))
    queries = low(low_back(jnp.dot(normed_one, w_query, precision=highest))).reshape(length, HEADS, HEAD_DIM)
    keys = low(low_back(jnp.dot(normed_one, w_key, precision=highest))).reshape(length, HEADS, HEAD_DIM)
    values = low(low_back(jnp.dot(normed_one, w_value, precision=highest))).reshape(length, HEADS, HEAD_DIM)
    scores = low_back(jnp.einsum('qhd,khd->hqk', queries, keys, precision=highest) * 0.125)
    position = jnp.arange(length)
    allowed = (position[None, :] <= position[:, None]) & (segments[None, :] == segments[:, None])
    scores = jnp.where(allowed[None], scores, -1000000000.0)
    probs = jax.nn.softmax(scores, axis=-1)
    attended = low_back(jnp.einsum('hqk,khd->qhd', low(probs), values, precision=highest)).reshape(length, D)
    branch = low_back(jnp.dot(low(attended), w_out, precision=highest))
    hidden_state = inputs + branch
    normed_two = low(normalize(hidden_state, gain_two))
    logits = low_back(jnp.dot(normed_two, w_ctrl, precision=highest))
    groups = length // GROUP
    gate = jax.nn.softmax(logits.reshape(groups, GROUP, EXPERTS), axis=1)
    grouped = normed_two.reshape(groups, GROUP, D)
    merged = low(low_back(jnp.einsum('gte,gtd->ged', low(gate), grouped, precision=highest)))
    inner = low_back(jnp.einsum('ged,edf->gef', merged, w_in, precision=highest))
    hidden_units = low(jax.nn.gelu(inner))
    expert_out = low_back(jnp.einsum('gef,efd->ged', hidden_units, w_back, precision=highest))
    mixed = jnp.einsum('gte,ged->gtd', gate, expert_out, precision=highest).reshape(length, D)
    return hidden_state + mixed

def reference(block_input, segment_ids, gain_one, w_query, w_key, w_value, w_out, gain_two, w_ctrl, w_in, w_back, cotangent):
    inputs = block_input.astype(jnp.float32)
    params = tuple((weight.astype(jnp.float32) for weight in (gain_one, w_query, w_key, w_value, w_out, gain_two, w_ctrl, w_in, w_back)))
    segments = jnp.stack([jnp.zeros_like(segment_ids), segment_ids]).reshape(MICRO * SEQS, LENGTH)

    def forward(inputs, params):
        flat = inputs.reshape(MICRO * SEQS, LENGTH, D)
        step_one = jax.checkpoint(lambda entry_pair: layer_one(entry_pair[0], entry_pair[1], params))
        return lax.map(step_one, (flat, segments)).reshape(inputs.shape)
    output, pull = jax.vjp(forward, inputs, params)
    grad_inputs, grads = pull(cotangent.astype(jnp.float32))
    return (output.astype(jnp.bfloat16), grad_inputs.astype(jnp.bfloat16), grads[0], grads[1], grads[2], grads[3], grads[4], grads[5], grads[6], grads[7], grads[8])
```

```python
import functools

import jax
import jax.numpy as jnp
from jax import lax
from jax.experimental import pallas as pl
from jax.experimental.pallas import tpu as pltpu
from jax.sharding import PartitionSpec as P

HEAD_DIM = 64
GROUP = 32
EPSILON = 1e-05
BLOCK = 256
CHUNK = 512
SCALE = 0.125
MASKED = -1e30
VMEM_LIMIT = 60 * 1024 * 1024
BF = jnp.bfloat16
F32 = jnp.float32


def dot(a, b, ca, cb):
    return lax.dot_general(a, b, (((ca,), (cb,)), ((), ())), preferred_element_type=F32)


def nn(a, b):
    return dot(a, b, 1, 0)


def nt(a, b):
    return dot(a, b, 1, 1)


def tn(a, b):
    return dot(a, b, 0, 0)


def key_range(packed, i):
    low = max(0, i * BLOCK - BLOCK - BLOCK // 2) if packed else 0
    return low, (i + 1) * BLOCK - low


def head_masks():
    lane = lax.broadcasted_iota(jnp.int32, (1, 2 * HEAD_DIM), 1)
    first = (lane < HEAD_DIM).astype(F32).astype(BF)
    return first, (lane >= HEAD_DIM).astype(F32).astype(BF)


def group_match(rows, tokens):
    row = lax.broadcasted_iota(jnp.int32, (rows, tokens), 0)
    col = lax.broadcasted_iota(jnp.int32, (rows, tokens), 1)
    return (row % (tokens // GROUP)) == (col // GROUP)


def fill_bias(bias_ref, start_ref, packed, i):
    low, count = key_range(packed, i)
    q_pos = i * BLOCK + lax.broadcasted_iota(jnp.int32, (1, BLOCK), 1)
    if packed:
        k_pos = low + lax.broadcasted_iota(jnp.int32, (count, BLOCK), 0)
        allowed = (k_pos <= q_pos) & (k_pos >= start_ref[...])
        bias_ref[0:count, :] = jnp.where(allowed, 0.0, MASKED)
    else:
        k_pos = i * BLOCK + lax.broadcasted_iota(jnp.int32, (BLOCK, BLOCK), 0)
        bias_ref[0:BLOCK, :] = jnp.where(k_pos <= q_pos, 0.0, MASKED)


def add_bias(scores, bias_ref, packed, count):
    if packed:
        return scores + bias_ref[0:count, :]
    last = scores[count - BLOCK :, :] + bias_ref[0:BLOCK, :]
    if count == BLOCK:
        return last
    return jnp.concatenate([scores[: count - BLOCK, :], last], axis=0)


def rms(values):
    return lax.rsqrt(jnp.mean(values * values, axis=-1, keepdims=True) + EPSILON)


def forward_kernel(
    packed, blocks, x_ref, start_ref, g1_ref, wqkv_ref, wkvt_ref, wo_ref, g2_ref, wc_ref,
    q_ref, k_ref, v_ref, kt_ref, ob_ref, lse_ref, h_ref, gate_ref, mg_ref,
    k_all, vt_all, bias,
):
    step = pl.program_id(0)
    width = x_ref.shape[1]
    pairs = width // (2 * HEAD_DIM)
    x = x_ref[...].astype(F32)
    n1 = (x * rms(x) * g1_ref[...]).astype(BF)
    qkv = nn(n1, wqkv_ref[...]).astype(BF)
    q_ref[...] = qkv[:, :width]
    k_ref[...] = qkv[:, width : 2 * width]
    v_ref[...] = qkv[:, 2 * width :]
    kvt = nt(wkvt_ref[...], n1).astype(BF)
    kt_ref[...] = kvt[:width]
    at = pl.multiple_of(step * BLOCK, BLOCK)
    k_all[pl.ds(at, BLOCK), :] = qkv[:, width : 2 * width]
    vt_all[:, pl.ds(at, BLOCK)] = kvt[width:]
    masks = head_masks()

    def attend(i):
        low, count = key_range(packed, i)
        fill_bias(bias, start_ref, packed, i)

        def pair(hp, carry):
            lanes = pl.ds(pl.multiple_of(hp * 2 * HEAD_DIM, 2 * HEAD_DIM), 2 * HEAD_DIM)
            q_pair = q_ref[:, lanes]
            k_pair = k_all[low : low + count, lanes]
            for h in range(2):
                scores = add_bias(nt(k_pair, q_pair * masks[h]), bias, packed, count)
                top = jnp.max(scores, axis=0, keepdims=True)
                p = jnp.exp((scores - top) * SCALE)
                total = jnp.sum(p, axis=0, keepdims=True)
                rows = pl.ds(pl.multiple_of(hp * 2 * HEAD_DIM + h * HEAD_DIM, HEAD_DIM), HEAD_DIM)
                o = nn(vt_all[rows, low : low + count], p.astype(BF))
                ob_ref[rows, :] = (o * (1.0 / total)).astype(BF)
                lse_ref[pl.ds(hp * 2 + h, 1), :] = top * SCALE + jnp.log(total)
            return carry

        lax.fori_loop(0, pairs, pair, 0)

    for i in range(blocks):
        pl.when(step == i)(functools.partial(attend, i))

    h = x + tn(ob_ref[...], wo_ref[...])
    h_ref[...] = h
    n2 = (h * rms(h) * g2_ref[...]).astype(BF)
    logits = nt(wc_ref[...], n2)
    rows = logits.shape[0]
    match = group_match(rows, BLOCK)
    logits = jnp.where(match, logits, MASKED)
    e = jnp.where(match, jnp.exp(logits - jnp.max(logits, axis=1, keepdims=True)), 0.0)
    gate = e / jnp.sum(e, axis=1, keepdims=True)
    gate_ref[...] = gate
    mg = nn(gate.astype(BF), n2).astype(BF).astype(F32)
    half = rows // mg_ref.shape[0]
    for j in range(mg_ref.shape[0]):
        mg_ref[j] = mg[j * half : (j + 1) * half]


def gelu_both(u):
    c = 0.7978845608028654
    t = jnp.tanh(c * (u + 0.044715 * (u * u * u)))
    act = 0.5 * u * (1.0 + t)
    slope = 0.5 * (1.0 + t) + 0.5 * u * (1.0 - t * t) * (c * (1.0 + 3 * 0.044715 * (u * u)))
    return act, slope


def experts_kernel(
    micros, blocks, *refs,
):
    mgs, gates = refs[:micros], refs[micros : 2 * micros]
    cot_ref, win_ref, wback_ref = refs[2 * micros : 2 * micros + 3]
    eo_ref, dmg_ref, mgb_ref, deob_ref, deo = refs[2 * micros + 3 :]
    e, c = pl.program_id(0), pl.program_id(1)
    per = BLOCK // GROUP
    n_exp = deo.shape[0]

    @pl.when((e == 0) & (c == 0))
    def _():
        for m in range(micros):
            for i in range(blocks):
                part = gates[m][:, i * BLOCK : (i + 1) * BLOCK].astype(BF)
                d = nn(part, cot_ref[m, i * BLOCK : (i + 1) * BLOCK, :])
                for j in range(n_exp):
                    at = (m * blocks + i) * per
                    deo[j, at : at + per, :] = d[j * per : (j + 1) * per]

    mg = jnp.concatenate([r[0] for r in mgs], axis=0).astype(BF)
    deo_b = deo[e].astype(BF)

    @pl.when(c == 0)
    def _():
        mgb_ref[0] = mg
        deob_ref[0] = deo_b

    act, slope = gelu_both(nn(mg, win_ref[0]))
    eo_part = nn(act.astype(BF), wback_ref[0])
    du = (slope * nt(deo_b, wback_ref[0])).astype(BF)
    dmg_part = nt(du, win_ref[0])

    @pl.when(c == 0)
    def _():
        eo_ref[0] = eo_part
        dmg_ref[0] = dmg_part

    @pl.when(c > 0)
    def _():
        eo_ref[0] += eo_part
        dmg_ref[0] += dmg_part


def backward_kernel(
    packed, blocks, first, x_ref, cot_ref, h_ref, gate_ref, eo_ref, dmg_ref, ob_ref, lse_ref,
    q_ref, k_ref, v_ref, kt_ref, start_ref, g1_ref, g2_ref, wc_ref, wqt_ref, wk_ref, wv_ref,
    wo_ref, *refs,
):
    if first:
        before, refs = None, refs
    else:
        before, refs = refs[:4], refs[4:]
    act_ref, gi_ref, gq_ref, gkv_ref, go_ref, small_ref, dk_acc, dv_acc, dqt, dob, dobt, delta, bias = refs
    step = pl.program_id(0)
    width = x_ref.shape[1]
    pairs = width // (2 * HEAD_DIM)
    heads = width // HEAD_DIM

    @pl.when(step == 0)
    def _():
        dk_acc[...] = jnp.zeros_like(dk_acc)
        dv_acc[...] = jnp.zeros_like(dv_acc)
        if first:
            for r in (gq_ref, gkv_ref, go_ref, small_ref):
                r[...] = jnp.zeros_like(r)
        else:
            for r, b in zip((gq_ref, gkv_ref, go_ref, small_ref), before):
                r[...] = b[...]

    h = h_ref[...]
    cot_b = cot_ref[...]
    dout = cot_b.astype(F32)
    r2 = rms(h)
    z = h * r2
    n2 = (z * g2_ref[...]).astype(BF)
    gate = gate_ref[...]
    rows = gate.shape[0]
    gate_b = gate.astype(BF)
    gate_low = (gate - gate_b.astype(F32)).astype(BF)
    eo = jnp.concatenate([eo_ref[j] for j in range(eo_ref.shape[0])], axis=0)
    dmg = jnp.concatenate([dmg_ref[j] for j in range(dmg_ref.shape[0])], axis=0).astype(BF)
    eo_b = eo.astype(BF)
    eo_low = (eo - eo_b.astype(F32)).astype(BF)
    mixed = tn(
        jnp.concatenate([gate_b, gate_low, gate_b], axis=0),
        jnp.concatenate([eo_b, eo_b, eo_low], axis=0),
    )
    act_ref[...] = (h + mixed).astype(BF)
    dw2 = nt(jnp.concatenate([eo_b, eo_low], axis=0), cot_b)
    dw = dw2[:rows] + dw2[rows:] + nt(dmg, n2)
    wdw = gate * dw
    dlog = (wdw - gate * jnp.sum(wdw, axis=1, keepdims=True)).astype(BF)
    dn2 = tn(
        jnp.concatenate([gate_b, dlog], axis=0),
        jnp.concatenate([dmg, wc_ref[...]], axis=0),
    )
    small_ref[0:rows, :] += nn(dlog, n2)
    dg2 = dn2 * z
    small_ref[rows : rows + 1, :] += jnp.sum(dg2, axis=0, keepdims=True)
    a = dn2 * g2_ref[...]
    dh = dout + r2 * (a - z * jnp.mean(a * z, axis=-1, keepdims=True))
    da = dh.astype(BF)
    dob[...] = nt(da, wo_ref[...]).astype(BF)
    dobt[...] = nt(wo_ref[...], da).astype(BF)
    go_ref[...] += nn(ob_ref[...], da)
    prod = dobt[...].astype(F32) * ob_ref[...].astype(F32)
    for hd in range(heads):
        delta[hd : hd + 1, :] = jnp.sum(
            prod[hd * HEAD_DIM : (hd + 1) * HEAD_DIM], axis=0, keepdims=True
        )
    masks = head_masks()

    def attend(i):
        low, count = key_range(packed, i)
        fill_bias(bias, start_ref, packed, i)
        keys = slice(low, low + count)

        def pair(hp, carry):
            lanes = pl.ds(pl.multiple_of(hp * 2 * HEAD_DIM, 2 * HEAD_DIM), 2 * HEAD_DIM)
            q_pair, dob_pair = q_ref[:, lanes], dob[:, lanes]
            k_pair, v_pair = k_ref[keys, lanes], v_ref[keys, lanes]
            dk_sum = dv_sum = None
            for h in range(2):
                qm, dm = q_pair * masks[h], dob_pair * masks[h]
                scores = add_bias(nt(k_pair, qm), bias, packed, count)
                p = jnp.exp(scores * SCALE - lse_ref[pl.ds(hp * 2 + h, 1), :])
                dp = nt(v_pair, dm)
                ds = (p * (dp - delta[pl.ds(hp * 2 + h, 1), :])).astype(BF)
                rows_h = pl.ds(pl.multiple_of(hp * 2 * HEAD_DIM + h * HEAD_DIM, HEAD_DIM), HEAD_DIM)
                dqt[rows_h, :] = (nn(kt_ref[rows_h, keys], ds) * SCALE).astype(BF)
                dk_part, dv_part = nn(ds, qm), nn(p.astype(BF), dm)
                dk_sum = dk_part if dk_sum is None else dk_sum + dk_part
                dv_sum = dv_part if dv_sum is None else dv_sum + dv_part
            dk_acc[keys, lanes] += dk_sum
            dv_acc[keys, lanes] += dv_sum
            return carry

        lax.fori_loop(0, pairs, pair, 0)

    for i in range(blocks):
        pl.when(step == blocks - 1 - i)(functools.partial(attend, i))

    at = pl.ds(pl.multiple_of((blocks - 1 - step) * BLOCK, BLOCK), BLOCK)
    dk = (dk_acc[at, :] * SCALE).astype(BF)
    dv = dv_acc[at, :].astype(BF)
    x = x_ref[...].astype(F32)
    r1 = rms(x)
    z1 = x * r1
    n1 = (z1 * g1_ref[...]).astype(BF)
    dq_t = dqt[...]
    dn1 = tn(dq_t, wqt_ref[...]) + nt(dk, wk_ref[...]) + nt(dv, wv_ref[...])
    gq_ref[...] += nn(dq_t, n1)
    gkv_ref[...] += tn(n1, jnp.concatenate([dk, dv], axis=1))
    small_ref[rows + 8 : rows + 9, :] += jnp.sum(dn1 * z1, axis=0, keepdims=True)
    b = dn1 * g1_ref[...]
    gi = dh + r1 * (b - z1 * jnp.mean(b * z1, axis=-1, keepdims=True))
    gi_ref[...] = gi.astype(BF)


def whole(shape):
    return pl.BlockSpec(shape, lambda *_: (0,) * len(shape))


def params(flag=None):
    return pltpu.CompilerParams(vmem_limit_bytes=VMEM_LIMIT)


def forward_call(packed, x, start, g1, wqkv, wkvt, wo, g2, wc):
    length, width = x.shape
    blocks = length // BLOCK
    rows = wc.shape[0]
    per = BLOCK // GROUP
    experts = rows // per
    row_block = pl.BlockSpec((BLOCK, width), lambda i: (i, 0))
    col_block = pl.BlockSpec((width, BLOCK), lambda i: (0, i))
    out = lambda shape, dtype: jax.ShapeDtypeStruct(shape, dtype)
    return pl.pallas_call(
        functools.partial(forward_kernel, packed, blocks),
        grid=(blocks,),
        in_specs=[
            row_block, pl.BlockSpec((1, BLOCK), lambda i: (0, i)), whole(g1.shape), whole(wqkv.shape),
            whole(wkvt.shape), whole(wo.shape), whole(g2.shape), whole(wc.shape),
        ],
        out_specs=[
            row_block, row_block, row_block, col_block, col_block,
            pl.BlockSpec((width // HEAD_DIM, BLOCK), lambda i: (0, i)),
            row_block,
            pl.BlockSpec((rows, BLOCK), lambda i: (0, i)),
            pl.BlockSpec((experts, per, width), lambda i: (0, i, 0)),
        ],
        out_shape=[
            out((length, width), BF), out((length, width), BF), out((length, width), BF),
            out((width, length), BF), out((width, length), BF),
            out((width // HEAD_DIM, length), F32),
            out((length, width), F32),
            out((rows, length), F32),
            out((experts, length // GROUP, width), F32),
        ],
        scratch_shapes=[
            pltpu.VMEM((length, width), BF), pltpu.VMEM((width, length), BF),
            pltpu.VMEM((length, BLOCK), F32),
        ],
        compiler_params=params(),
        name="attention_forward",
    )(x, start, g1, wqkv, wkvt, wo, g2, wc)


def experts_call(mgs, gates, cot, w_in, w_back):
    micros, length, width = cot.shape
    experts, _, ff = w_in.shape
    blocks = length // BLOCK
    groups = micros * length // GROUP
    chunk = min(CHUNK, ff)
    by_expert = lambda n: pl.BlockSpec((1, n, width), lambda e, c: (e, 0, 0))
    out = lambda dtype: jax.ShapeDtypeStruct((experts, groups, width), dtype)
    return pl.pallas_call(
        functools.partial(experts_kernel, micros, blocks),
        grid=(experts, ff // chunk),
        in_specs=[by_expert(length // GROUP)] * micros
        + [whole(gates[0].shape)] * micros
        + [
            whole(cot.shape),
            pl.BlockSpec((1, width, chunk), lambda e, c: (e, 0, c)),
            pl.BlockSpec((1, chunk, width), lambda e, c: (e, c, 0)),
        ],
        out_specs=[by_expert(groups)] * 4,
        out_shape=[out(F32), out(F32), out(BF), out(BF)],
        scratch_shapes=[pltpu.VMEM((experts, groups, width), F32)],
        compiler_params=params(),
        name="experts",
    )(*mgs, *gates, cot, w_in, w_back)


def backward_call(packed, micro, x, cot, h, gate, eo, dmg, ob, lse, q, k, v, kt, start, g1, g2, wc,
                  wqt, wk, wv, wo, before):
    length, width = x.shape
    blocks = length // BLOCK
    rows = wc.shape[0]
    per = BLOCK // GROUP
    experts = rows // per
    heads = width // HEAD_DIM
    first = before is None
    back = lambda i: blocks - 1 - i
    row_block = pl.BlockSpec((BLOCK, width), lambda i: (back(i), 0))
    col_block = lambda n: pl.BlockSpec((n, BLOCK), lambda i: (0, back(i)))
    group_block = pl.BlockSpec((experts, per, width), lambda i: (0, micro * blocks + back(i), 0))
    sums = [(width, width), (width, 2 * width), (width, width), (rows + 16, width)]
    out = lambda shape, dtype: jax.ShapeDtypeStruct(shape, dtype)
    return pl.pallas_call(
        functools.partial(backward_kernel, packed, blocks, first),
        grid=(blocks,),
        in_specs=[
            row_block, row_block, row_block, col_block(rows), group_block, group_block,
            col_block(width), col_block(heads), row_block, whole(k.shape), whole(v.shape),
            whole(kt.shape), col_block(1), whole(g1.shape), whole(g2.shape), whole(wc.shape),
            whole(wqt.shape), whole(wk.shape), whole(wv.shape), whole(wo.shape),
        ] + ([] if first else [whole(s) for s in sums]),
        out_specs=[row_block, row_block] + [whole(s) for s in sums],
        out_shape=[out((length, width), BF), out((length, width), BF)] + [out(s, F32) for s in sums],
        scratch_shapes=[
            pltpu.VMEM((length, width), F32), pltpu.VMEM((length, width), F32),
            pltpu.VMEM((width, BLOCK), BF), pltpu.VMEM((BLOCK, width), BF),
            pltpu.VMEM((width, BLOCK), BF), pltpu.VMEM((heads, BLOCK), F32),
            pltpu.VMEM((length, BLOCK), F32),
        ],
        compiler_params=params(),
        name="attention_backward",
    )(x, cot, h, gate, eo, dmg, ob, lse, q, k, v, kt, start, g1, g2, wc, wqt, wk, wv, wo,
      *([] if first else before))


def swap(value, axis, size, distance, stride=1):
    n = lax.axis_size(axis)
    return lax.ppermute(value, axis, [(i, i ^ (distance * stride)) for i in range(n)])


def take(value, index, axis=0):
    return lax.dynamic_index_in_dim(value, index, axis, keepdims=False)


def trade(pieces, axis, size, me):
    got = lax.dynamic_update_index_in_dim(jnp.zeros_like(pieces), take(pieces, me), me, 0)
    for d in range(1, size):
        came = swap(take(pieces, me ^ d), axis, size, d)
        got = lax.dynamic_update_index_in_dim(got, came, me ^ d, 0)
    return got


def local(block_input, segment_ids, gain_one, w_query, w_key, w_value, w_out, gain_two, w_ctrl,
          w_in, w_back, cotangent):
    micros, seqs, rows, width = block_input.shape
    experts, _, ff = w_in.shape
    nb = lax.axis_size("blk")
    nd = lax.axis_size("dp")
    blk, dp = lax.axis_index("blk"), lax.axis_index("dp")
    length = nb * rows
    per = BLOCK // GROUP

    def to_sequences(a):
        return trade(a, "blk", nb, blk).reshape(length, -1)

    def to_blocks(a):
        return trade(a.reshape(nb, rows, width), "blk", nb, blk)

    seg = to_sequences(segment_ids).reshape(1, length)
    start = jnp.sum((seg.reshape(length, 1) < seg).astype(jnp.int32), axis=0, keepdims=True)
    g1, g2 = gain_one.reshape(1, width), gain_two.reshape(1, width)
    wqkv = jnp.concatenate([w_query, w_key, w_value], axis=1)
    wkvt = jnp.concatenate([w_key, w_value], axis=1).T
    wqt = w_query.T
    wc = jnp.repeat(w_ctrl.T, per, axis=0)

    xs = [to_sequences(block_input[m]) for m in range(micros)]
    fwd = [
        forward_call(m > 0, xs[m], start, g1, wqkv, wkvt, w_out, g2, wc) for m in range(micros)
    ]
    cots = jnp.stack([to_sequences(cotangent[m]) for m in range(micros)])
    eo, dmg, mgb, deob = experts_call([f[8] for f in fwd], [f[7] for f in fwd], cots, w_in, w_back)

    grads = None
    acts, gis = [], []
    for m in range(micros):
        q, k, v, kt, ob, lse, h, gate, _ = fwd[m]
        act, gi, *grads = backward_call(
            m > 0, m, xs[m], cots[m], h, gate, eo, dmg, ob, lse, q, k, v, kt, start, g1, g2, wc,
            wqt, w_key, w_value, w_out, grads,
        )
        acts.append(to_blocks(act))
        gis.append(to_blocks(gi))
    gqt, gkv, go, small = grads

    slices = nb
    e_mine = blk % experts
    pair = jnp.stack([mgb, deob])
    keep = take(pair, e_mine, 1)
    came = swap(take(pair, 1 - e_mine, 1), "blk", nb, 1)
    mine = jnp.stack([keep, came])
    sets = [mine]
    for far in (0, 1):
        for d in range(0, nb, 2):
            if far == 0 and d == 0:
                continue
            if far:
                moved = lax.ppermute(
                    mine, ("dp", "blk"),
                    [(i * nb + j, (i ^ 1) * nb + (j ^ d)) for i in range(nd) for j in range(nb)],
                )
            else:
                moved = swap(mine, "blk", nb, d)
            sets.append(moved)
    both = jnp.stack(sets)
    mg_all = both[:, :, 0].reshape(-1, width)
    deo_all = both[:, :, 1].reshape(-1, width)
    part = (dp % 2) * (nb // 2) + blk // 2
    cut = ff // slices
    win_cut = lax.dynamic_slice(w_in, (e_mine, 0, part * cut), (1, width, cut))[0]
    wback_cut = lax.dynamic_slice(w_back, (e_mine, part * cut, 0), (1, cut, width))[0]
    act, slope = gelu_both(nn(mg_all, win_cut))
    du = (slope * nt(deo_all, wback_cut)).astype(BF)
    g_in = tn(mg_all, du)
    g_back = tn(act.astype(BF), deo_all)
    planes = nd // 2
    plane = dp // 2

    def plane_swap(a, d):
        return lax.ppermute(a, "dp", [(i, i ^ (2 * d)) for i in range(nd)])

    ours = jnp.stack([g_in, g_back]).reshape(2, planes, width // planes, cut).astype(F32)
    total = take(ours, plane, 1)
    for d in range(1, planes):
        total = total + plane_swap(take(ours, plane ^ d, 1).astype(BF), d).astype(F32)
    got = jnp.zeros((planes,) + total.shape, BF)
    got = lax.dynamic_update_index_in_dim(got, total.astype(BF), plane, 0)
    for d in range(1, planes):
        got = lax.dynamic_update_index_in_dim(got, plane_swap(total.astype(BF), d), plane ^ d, 0)
    piece = jnp.transpose(got, (1, 0, 2, 3)).reshape(2, width, cut)
    full = jnp.zeros((2 * nb, 2, width, cut), BF)
    place = (dp % 2) * nb + blk
    full = lax.dynamic_update_index_in_dim(full, piece, place, 0)
    for far in (0, 1):
        for d in range(nb):
            if far == 0 and d == 0:
                continue
            moved = lax.ppermute(
                piece, ("dp", "blk"),
                [(i * nb + j, (i ^ far) * nb + (j ^ d)) for i in range(nd) for j in range(nb)],
            )
            full = lax.dynamic_update_index_in_dim(full, moved, ((dp % 2) ^ far) * nb + (blk ^ d), 0)
    full = full.reshape(2, nb // 2, 2, 2, width, cut).astype(F32)
    grad_in = jnp.transpose(full[:, :, :, 0], (2, 3, 0, 1, 4)).reshape(experts, width, ff)
    grad_back = jnp.transpose(full[:, :, :, 1], (2, 0, 1, 3, 4)).reshape(experts, ff, width)

    flat = jnp.concatenate([gqt, gkv[:, :width], gkv[:, width:], go], axis=0)
    def reduce_scatter(a, size, me, move):
        a = a.reshape(size, a.shape[0] // size, width)
        total = take(a, me)
        for d in range(1, size):
            total = total + move(take(a, me ^ d).astype(BF), d).astype(F32)
        return total

    def gather(a, size, me, move):
        got = jnp.zeros((size,) + a.shape, a.dtype)
        got = lax.dynamic_update_index_in_dim(got, a, me, 0)
        for d in range(1, size):
            got = lax.dynamic_update_index_in_dim(got, move(a, d), me ^ d, 0)
        return got.reshape(-1, width)

    def add_all(a, size, move):
        total = a
        for d in range(1, size):
            total = total + move(a, d)
        return total

    by_core = lambda a, d: swap(a, "blk", nb, d)
    def by_plane(a, d):
        far, d = d % 2, (d // 2) * 2
        return lax.ppermute(
            a, ("dp", "blk"),
            [(i * nb + j, (i ^ far) * nb + (j ^ d)) for i in range(nd) for j in range(nb)],
        )
    stages = [(2, blk % 2, by_core), (nb, (blk // 2) * 2 + dp % 2, by_plane), (planes, plane, plane_swap)]
    for s in stages:
        flat = reduce_scatter(flat, *s)
        small = add_all(small, s[0], s[2])
    flat = flat.astype(BF)
    for s in reversed(stages):
        flat = gather(flat, *s)
    flat = flat.astype(F32).reshape(4, width, width)
    ctrl = jnp.sum(small[: experts * per].reshape(experts, per, width), axis=1).T
    return (
        jnp.stack(acts), jnp.stack(gis), small[experts * per + 8], flat[0].T, flat[1], flat[2],
        flat[3], small[experts * per], ctrl, grad_in, grad_back,
    )


def solution(mesh):
    data = P(None, "dp", "blk", None)
    in_specs = (data, P("dp", "blk")) + (P(),) * 9 + (data,)
    out_specs = (data, data) + (P(),) * 9
    return jax.shard_map(local, mesh=mesh, in_specs=in_specs, out_specs=out_specs, check_vma=False)
```

```python
import functools

import jax
import jax.numpy as jnp
from jax import lax
from jax.experimental import pallas as pl
from jax.experimental.pallas import tpu as pltpu
from jax.sharding import PartitionSpec as P

HEAD_DIM = 64
GROUP = 32
EPSILON = 1e-05
BLOCK = 256
CHUNK = 512
SCALE = 0.125
MASKED = -1e30
VMEM_LIMIT = 60 * 1024 * 1024
BF = jnp.bfloat16
F32 = jnp.float32
MESH = pl.DeviceIdType.MESH


def dot(a, b, ca, cb):
    return lax.dot_general(a, b, (((ca,), (cb,)), ((), ())), preferred_element_type=F32)


def nn(a, b):
    return dot(a, b, 1, 0)


def nt(a, b):
    return dot(a, b, 1, 1)


def tn(a, b):
    return dot(a, b, 0, 0)


def key_range(packed, i):
    low = max(0, i * BLOCK - BLOCK - BLOCK // 2) if packed else 0
    return low, (i + 1) * BLOCK - low


def head_masks():
    lane = lax.broadcasted_iota(jnp.int32, (1, 2 * HEAD_DIM), 1)
    first = (lane < HEAD_DIM).astype(F32).astype(BF)
    return first, (lane >= HEAD_DIM).astype(F32).astype(BF)


def group_match(rows, tokens):
    row = lax.broadcasted_iota(jnp.int32, (rows, tokens), 0)
    col = lax.broadcasted_iota(jnp.int32, (rows, tokens), 1)
    return (row % (tokens // GROUP)) == (col // GROUP)


def fill_bias(bias_ref, start_ref, packed, i):
    low, count = key_range(packed, i)
    q_pos = i * BLOCK + lax.broadcasted_iota(jnp.int32, (1, BLOCK), 1)
    if packed:
        k_pos = low + lax.broadcasted_iota(jnp.int32, (count, BLOCK), 0)
        allowed = (k_pos <= q_pos) & (k_pos >= start_ref[...])
        bias_ref[0:count, :] = jnp.where(allowed, 0.0, MASKED)
    else:
        k_pos = i * BLOCK + lax.broadcasted_iota(jnp.int32, (BLOCK, BLOCK), 0)
        bias_ref[0:BLOCK, :] = jnp.where(k_pos <= q_pos, 0.0, MASKED)


def add_bias(scores, bias_ref, packed, count):
    if packed:
        return scores + bias_ref[0:count, :]
    last = scores[count - BLOCK :, :] + bias_ref[0:BLOCK, :]
    if count == BLOCK:
        return last
    return jnp.concatenate([scores[: count - BLOCK, :], last], axis=0)


def rms(values):
    return lax.rsqrt(jnp.mean(values * values, axis=-1, keepdims=True) + EPSILON)


def peer(axis, me, d):
    return {axis: me ^ d}


def arrive(partners):
    barrier = pltpu.get_barrier_semaphore()
    for p in partners:
        pl.semaphore_signal(barrier, inc=1, device_id=p, device_id_type=MESH)
    pl.semaphore_wait(barrier, len(partners))


def remote(src, dst, sems, k, where):
    return pltpu.make_async_remote_copy(
        src_ref=src, dst_ref=dst, send_sem=sems[0].at[k], recv_sem=sems[1].at[k],
        device_id=where, device_id_type=MESH,
    )


class Exchange:
    def __init__(self, nb, src, dst, own, sems, base):
        self.nb, self.src, self.dst, self.own, self.sems, self.base = nb, src, dst, own, sems, base
        self.me = lax.axis_index("blk")

    def local(self):
        return pltpu.make_async_copy(
            self.src.at[self.me], self.dst.at[self.me], self.own.at[self.base]
        )

    def copy(self, d):
        return remote(
            self.src.at[self.me ^ d], self.dst.at[self.me], self.sems,
            self.base * (self.nb - 1) + d - 1, peer("blk", self.me, d),
        )

    def start(self):
        self.local().start()
        for d in range(1, self.nb):
            self.copy(d).start()

    def wait(self):
        self.local().wait()
        for d in range(1, self.nb):
            self.copy(d).wait()


def forward_kernel(packed, blocks, nb, moves, *refs):
    if packed:
        x_ref, refs = refs[0], refs[1:]
    else:
        x_src, refs = refs[0], refs[1:]
    start_ref, g1_ref, wqkv_ref, wkvt_ref, wo_ref, g2_ref, wc_ref = refs[:7]
    srcs, refs = refs[7 : 7 + moves], refs[7 + moves :]
    q_ref, k_ref, v_ref, kt_ref, ob_ref, lse_ref, h_ref, gate_ref, mg_ref = refs[:9]
    dsts, refs = refs[9 : 9 + moves], refs[9 + moves :]
    if not packed:
        x_out, refs = refs[0], refs[1:]
    vt_all, bias, own, send_sem, recv_sem = refs[:5]
    sems = (send_sem, recv_sem)
    step = pl.program_id(0)
    width = q_ref.shape[1]
    pairs = width // (2 * HEAD_DIM)
    me = lax.axis_index("blk")
    later = [Exchange(nb, s, t, own, sems, n) for n, (s, t) in enumerate(zip(srcs, dsts))]
    if not packed:
        x_all = refs[5]
        first = Exchange(nb, x_src, x_all, own, sems, moves)
        keep = pltpu.make_async_copy(x_all, x_out, own.at[moves + 1])

    @pl.when(step == 0)
    def _():
        if not packed:
            first.local().start()
        arrive([peer("blk", me, d) for d in range(1, nb)])
        for d in range(1, nb):
            if not packed:
                first.copy(d).start()
        if packed:
            for x in later:
                x.start()

    @pl.when(step < blocks)
    def _():
        if packed:
            block = step
            x = x_ref[pl.ds(pl.multiple_of(block * BLOCK, BLOCK), BLOCK), :]
        else:
            block = me ^ step
            pl.when(step == 0)(first.local().wait)
            for d in range(1, nb):
                pl.when(step == d)(first.copy(d).wait_recv)
            x = x_all[block]
        x = x.astype(F32)
        n1 = (x * rms(x) * g1_ref[...]).astype(BF)
        qkv = nn(n1, wqkv_ref[...]).astype(BF)
        at = pl.ds(pl.multiple_of(block * BLOCK, BLOCK), BLOCK)
        q_ref[at, :] = qkv[:, :width]
        k_ref[at, :] = qkv[:, width : 2 * width]
        v_ref[at, :] = qkv[:, 2 * width :]
        kvt = nt(wkvt_ref[...], n1).astype(BF)
        kt_ref[:, at] = kvt[:width]
        vt_all[:, at] = kvt[width:]

    if not packed:
        @pl.when(step == nb - 1)
        def _():
            for x in later:
                x.start()
            keep.start()

    masks = head_masks()

    def attend(i):
        low, count = key_range(packed, i)
        fill_bias(bias, start_ref, packed, i)

        def pair(hp, carry):
            lanes = pl.ds(pl.multiple_of(hp * 2 * HEAD_DIM, 2 * HEAD_DIM), 2 * HEAD_DIM)
            q_pair = q_ref[i * BLOCK : (i + 1) * BLOCK, lanes]
            k_pair = k_ref[low : low + count, lanes]
            for h in range(2):
                scores = add_bias(nt(k_pair, q_pair * masks[h]), bias, packed, count)
                top = jnp.max(scores, axis=0, keepdims=True)
                p = jnp.exp((scores - top) * SCALE)
                total = jnp.sum(p, axis=0, keepdims=True)
                rows = pl.ds(pl.multiple_of(hp * 2 * HEAD_DIM + h * HEAD_DIM, HEAD_DIM), HEAD_DIM)
                o = nn(vt_all[rows, low : low + count], p.astype(BF))
                ob_ref[rows, :] = (o * (1.0 / total)).astype(BF)
                lse_ref[pl.ds(hp * 2 + h, 1), :] = top * SCALE + jnp.log(total)
            return carry

        lax.fori_loop(0, pairs, pair, 0)

    for i in range(blocks):
        pl.when(step == blocks + i)(functools.partial(attend, i))

    @pl.when(step >= blocks)
    def _():
        if packed:
            x = x_ref[pl.ds(pl.multiple_of((step - blocks) * BLOCK, BLOCK), BLOCK), :]
        else:
            x = x_all[step - blocks]
        h = x.astype(F32) + tn(ob_ref[...], wo_ref[...])
        h_ref[...] = h
        n2 = (h * rms(h) * g2_ref[...]).astype(BF)
        logits = nt(wc_ref[...], n2)
        rows = logits.shape[0]
        match = group_match(rows, BLOCK)
        logits = jnp.where(match, logits, MASKED)
        e = jnp.where(match, jnp.exp(logits - jnp.max(logits, axis=1, keepdims=True)), 0.0)
        gate = e / jnp.sum(e, axis=1, keepdims=True)
        gate_ref[...] = gate
        mg = nn(gate.astype(BF), n2).astype(BF).astype(F32)
        half = rows // mg_ref.shape[0]
        for j in range(mg_ref.shape[0]):
            mg_ref[j] = mg[j * half : (j + 1) * half]

    @pl.when(step == 2 * blocks - 1)
    def _():
        if not packed:
            keep.wait()
            for d in range(1, nb):
                first.copy(d).wait_send()
        for x in later:
            x.wait()


def gelu_both(u):
    c = 0.7978845608028654
    t = jnp.tanh(c * (u + 0.044715 * (u * u * u)))
    act = 0.5 * u * (1.0 + t)
    slope = 0.5 * (1.0 + t) + 0.5 * u * (1.0 - t * t) * (c * (1.0 + 3 * 0.044715 * (u * u)))
    return act, slope


def same_plane(far, d):
    return {"dp": lax.axis_index("dp") ^ far, "blk": lax.axis_index("blk") ^ d}


def plane_steps(nb):
    return [(far, d) for far in (0, 1) for d in range(0, nb, 2) if far or d]


def experts_kernel(micros, blocks, nb, *refs):
    mgs, gates = refs[:micros], refs[micros : 2 * micros]
    cot_ref, win_ref, wback_ref = refs[2 * micros : 2 * micros + 3]
    eo_ref, dmg_ref, all_ref, factors, mine, gathered, send_sem, recv_sem = refs[2 * micros + 3 :]
    sems = (send_sem, recv_sem)
    e, c = pl.program_id(0), pl.program_id(1)
    at = e * pl.num_programs(1) + c
    last = pl.num_programs(0) * pl.num_programs(1) - 1
    per = BLOCK // GROUP
    n_exp = factors.shape[0]
    groups = micros * blocks * per
    blk = lax.axis_index("blk")
    kind = blk % n_exp
    steps = plane_steps(nb)

    def core_copy():
        return remote(factors.at[1 - kind], mine.at[1], sems, 0, peer("blk", blk, 1))

    def plane_copy(n):
        return remote(mine, gathered.at[n], sems, 1 + n, same_plane(*steps[n]))

    @pl.when(at == 0)
    def _():
        for j in range(n_exp):
            factors[j, 0] = jnp.concatenate([r[j] for r in mgs], axis=0).astype(BF)
            parts = []
            for m in range(micros):
                for i in range(blocks):
                    part = gates[m][:, i * BLOCK : (i + 1) * BLOCK].astype(BF)
                    d = nn(part, cot_ref[m, i * BLOCK : (i + 1) * BLOCK, :])
                    parts.append(d[j * per : (j + 1) * per])
            factors[j, 1] = jnp.concatenate(parts, axis=0).astype(BF)
        arrive([peer("blk", blk, 1)] + [same_plane(*s) for s in steps])
        core_copy().start()
        mine[0] = factors[kind]

    mg, deo = factors[e, 0], factors[e, 1]
    act, slope = gelu_both(nn(mg, win_ref[0]))
    eo_part = nn(act.astype(BF), wback_ref[0])
    du = (slope * nt(deo, wback_ref[0])).astype(BF)
    dmg_part = nt(du, win_ref[0])

    @pl.when(c == 0)
    def _():
        eo_ref[0] = eo_part
        dmg_ref[0] = dmg_part

    @pl.when(c > 0)
    def _():
        eo_ref[0] += eo_part
        dmg_ref[0] += dmg_part

    @pl.when(at == 2)
    def _():
        core_copy().wait()
        for n in range(len(steps)):
            plane_copy(n).start()

    @pl.when(at == last)
    def _():
        for n in range(len(steps)):
            plane_copy(n).wait()
        for n in range(len(steps) + 1):
            piece = mine[...] if n == 0 else gathered[n - 1]
            for f in range(2):
                for j in range(2):
                    rows = slice((2 * n + j) * groups, (2 * n + j + 1) * groups)
                    all_ref[f, rows, :] = piece[j, f]


class Return:
    def __init__(self, nb, buf, out, own, sems, base):
        self.nb, self.buf, self.out, self.own, self.sems, self.base = nb, buf, out, own, sems, base
        self.me = lax.axis_index("blk")

    def local(self):
        return pltpu.make_async_copy(
            self.buf.at[self.me], self.out.at[self.me], self.own.at[self.base]
        )

    def copy(self, d):
        return remote(
            self.buf.at[self.me ^ d], self.out.at[self.me], self.sems,
            self.base * (self.nb - 1) + d - 1, peer("blk", self.me, d),
        )

    def start(self, i):
        pl.when(i == self.me)(self.local().start)
        for d in range(1, self.nb):
            pl.when(i == (self.me ^ d))(self.copy(d).start)

    def wait(self):
        self.local().wait()
        for d in range(1, self.nb):
            self.copy(d).wait()


def other_plane(d):
    return {"dp": lax.axis_index("dp") ^ (2 * d)}


def pair_sum(parts):
    while len(parts) > 1:
        parts = [parts[n] + parts[n + 1] for n in range(0, len(parts), 2)]
    return parts[0]


def my_part():
    return lax.axis_index("blk") // 2 + (lax.axis_size("blk") // 2) * (lax.axis_index("dp") % 2)


def backward_kernel(packed, blocks, nb, planes, first, x_ref, cot_ref, h_ref, gate_ref, eo_ref, dmg_ref,
                    ob_ref, lse_ref, q_ref, k_ref, v_ref, kt_ref, start_ref, g1_ref, g2_ref, wc_ref,
                    wqt_ref, wk_ref, wv_ref, wo_ref, *refs):
    if first:
        (factors, win_hbm, wback_hbm), refs = refs[:3], refs[3:]
        (act_ref, gi_ref, gall_ref, small_ref, piece_ref), refs = refs[:5], refs[5:]
    else:
        before, refs = refs[:2], refs[2:]
        (act_ref, gi_ref, gall_ref, small_ref), refs = refs[:4], refs[4:]
    dk_acc, dv_acc, dqt, dob, dobt, delta, bias, act_buf, gi_buf, own, send_sem, recv_sem = refs[:12]
    sems = (send_sem, recv_sem)
    step = pl.program_id(0)
    block = blocks - 1 - step
    width = x_ref.shape[1]
    pairs = width // (2 * HEAD_DIM)
    heads = width // HEAD_DIM
    me = lax.axis_index("blk")
    act_out = Return(nb, act_buf, act_ref, own, sems, 0)
    gi_out = Return(nb, gi_buf, gi_ref, own, sems, 1)
    if first:
        win, wback, ours, theirs, load_sem, send_z, recv_z = refs[12:]
        kind, part, plane = me % 2, my_part(), lax.axis_index("dp") // 2
        cut = win.shape[1]
        columns = pl.ds(pl.multiple_of(part * cut, cut), cut)
        loads = [
            pltpu.make_async_copy(win_hbm.at[kind, :, columns], win, load_sem.at[0]),
            pltpu.make_async_copy(wback_hbm.at[kind, columns, :], wback, load_sem.at[1]),
        ]

        def plane_copy(d):
            return remote(ours.at[plane ^ d], theirs.at[d - 1], (send_z, recv_z), d - 1, other_plane(d))

    @pl.when(step == 0)
    def _():
        partners = [peer("blk", me, d) for d in range(1, nb)]
        if first:
            partners += [other_plane(d) for d in range(1, planes)]
            for c in loads:
                c.start()
        arrive(partners)
        dk_acc[...] = jnp.zeros_like(dk_acc)
        dv_acc[...] = jnp.zeros_like(dv_acc)
        if first:
            gall_ref[...] = jnp.zeros_like(gall_ref)
            small_ref[...] = jnp.zeros_like(small_ref)
            for c in loads:
                c.wait()
            mg, deo = factors[0], factors[1]
            act, slope = gelu_both(nn(mg, win[...]))
            du = (slope * nt(deo, wback[...])).astype(BF)
            rows = width // planes
            g_in = tn(mg, du).astype(BF)
            for n in range(planes):
                ours[n, 0] = g_in[n * rows : (n + 1) * rows]
            rows = cut // planes
            g_back = tn(act.astype(BF), deo).astype(BF)
            for n in range(planes):
                ours[n, 1] = g_back[n * rows : (n + 1) * rows]
            for d in range(1, planes):
                plane_copy(d).start()
        else:
            gall_ref[...] = before[0][...]
            small_ref[...] = before[1][...]

    h = h_ref[...]
    cot_b = cot_ref[...]
    dout = cot_b.astype(F32)
    r2 = rms(h)
    z = h * r2
    n2 = (z * g2_ref[...]).astype(BF)
    gate = gate_ref[...]
    rows = gate.shape[0]
    gate_b = gate.astype(BF)
    gate_low = (gate - gate_b.astype(F32)).astype(BF)
    eo = jnp.concatenate([eo_ref[j] for j in range(eo_ref.shape[0])], axis=0)
    dmg = jnp.concatenate([dmg_ref[j] for j in range(dmg_ref.shape[0])], axis=0).astype(BF)
    eo_b = eo.astype(BF)
    eo_low = (eo - eo_b.astype(F32)).astype(BF)
    mixed = tn(
        jnp.concatenate([gate_b, gate_low, gate_b], axis=0),
        jnp.concatenate([eo_b, eo_b, eo_low], axis=0),
    )
    act_buf[block] = (h + mixed).astype(BF)
    act_out.start(block)
    dw2 = nt(jnp.concatenate([eo_b, eo_low], axis=0), cot_b)
    dw = dw2[:rows] + dw2[rows:] + nt(dmg, n2)
    wdw = gate * dw
    dlog = (wdw - gate * jnp.sum(wdw, axis=1, keepdims=True)).astype(BF)
    dn2 = tn(
        jnp.concatenate([gate_b, dlog], axis=0),
        jnp.concatenate([dmg, wc_ref[...]], axis=0),
    )
    small_ref[0:rows, :] += nn(dlog, n2)
    dg2 = dn2 * z
    small_ref[rows : rows + 1, :] += jnp.sum(dg2, axis=0, keepdims=True)
    a = dn2 * g2_ref[...]
    dh = dout + r2 * (a - z * jnp.mean(a * z, axis=-1, keepdims=True))
    da = dh.astype(BF)
    dob[...] = nt(da, wo_ref[...]).astype(BF)
    dobt[...] = nt(wo_ref[...], da).astype(BF)
    gall_ref[3 * width :, :] += nn(ob_ref[...], da)
    prod = dobt[...].astype(F32) * ob_ref[...].astype(F32)
    for hd in range(heads):
        delta[hd : hd + 1, :] = jnp.sum(
            prod[hd * HEAD_DIM : (hd + 1) * HEAD_DIM], axis=0, keepdims=True
        )
    masks = head_masks()

    def attend(i):
        low, count = key_range(packed, i)
        fill_bias(bias, start_ref, packed, i)
        keys = slice(low, low + count)

        def pair(hp, carry):
            lanes = pl.ds(pl.multiple_of(hp * 2 * HEAD_DIM, 2 * HEAD_DIM), 2 * HEAD_DIM)
            q_pair, dob_pair = q_ref[:, lanes], dob[:, lanes]
            k_pair, v_pair = k_ref[keys, lanes], v_ref[keys, lanes]
            dk_sum = dv_sum = None
            for h in range(2):
                qm, dm = q_pair * masks[h], dob_pair * masks[h]
                scores = add_bias(nt(k_pair, qm), bias, packed, count)
                p = jnp.exp(scores * SCALE - lse_ref[pl.ds(hp * 2 + h, 1), :])
                dp = nt(v_pair, dm)
                ds = (p * (dp - delta[pl.ds(hp * 2 + h, 1), :])).astype(BF)
                rows_h = pl.ds(pl.multiple_of(hp * 2 * HEAD_DIM + h * HEAD_DIM, HEAD_DIM), HEAD_DIM)
                dqt[rows_h, :] = (nn(kt_ref[rows_h, keys], ds) * SCALE).astype(BF)
                dk_part, dv_part = nn(ds, qm), nn(p.astype(BF), dm)
                dk_sum = dk_part if dk_sum is None else dk_sum + dk_part
                dv_sum = dv_part if dv_sum is None else dv_sum + dv_part
            dk_acc[keys, lanes] += dk_sum
            dv_acc[keys, lanes] += dv_sum
            return carry

        lax.fori_loop(0, pairs, pair, 0)

    for i in range(blocks):
        pl.when(step == blocks - 1 - i)(functools.partial(attend, i))

    at = pl.ds(pl.multiple_of(block * BLOCK, BLOCK), BLOCK)
    dk = (dk_acc[at, :] * SCALE).astype(BF)
    dv = dv_acc[at, :].astype(BF)
    x = x_ref[...].astype(F32)
    r1 = rms(x)
    z1 = x * r1
    n1 = (z1 * g1_ref[...]).astype(BF)
    dq_t = dqt[...]
    dn1 = tn(dq_t, wqt_ref[...]) + nt(dk, wk_ref[...]) + nt(dv, wv_ref[...])
    small_ref[rows + 8 : rows + 9, :] += jnp.sum(dn1 * z1, axis=0, keepdims=True)
    b = dn1 * g1_ref[...]
    gi = dh + r1 * (b - z1 * jnp.mean(b * z1, axis=-1, keepdims=True))
    gi_buf[block] = gi.astype(BF)
    gi_out.start(block)
    gall_ref[:width, :] += nn(dq_t, n1)
    gkv = tn(n1, jnp.concatenate([dk, dv], axis=1))
    gall_ref[width : 2 * width, :] += gkv[:, :width]
    gall_ref[2 * width : 3 * width, :] += gkv[:, width:]

    @pl.when(step == blocks - 1)
    def _():
        act_out.wait()
        gi_out.wait()
        if first:
            for d in range(1, planes):
                plane_copy(d).wait()
            parts = [ours[plane].astype(F32)] + [theirs[d].astype(F32) for d in range(planes - 1)]
            piece_ref[...] = pair_sum(parts).astype(BF)


def tail_kernel(nb, planes, gall, small, piece, flat, small_out, gin, gback, s1, r1, s2, r2, s3, r3,
                fl, acc, rs, small_acc, own, send_sem, recv_sem):
    sems = (send_sem, recv_sem)
    blk, dp = lax.axis_index("blk"), lax.axis_index("dp")
    kind, part, plane = blk % 2, my_part(), dp // 2
    width = gall.shape[1]
    total = gall.shape[0]
    steps = plane_steps(nb)
    members = len(steps) + 1
    core = peer("blk", blk, 1)
    half, quarter = total // 2, total // 2 // members
    share = quarter // planes
    cut = gin.shape[2] // members
    rows = piece.shape[1]
    counter = iter(range(10000))
    waits = []

    def send(src, dst, where):
        c = remote(src, dst, sems, next(counter), where)
        c.start()
        return c

    def done(copies):
        for c in copies:
            c.wait_recv()
        waits.extend(copies)

    def part_of(far, d):
        return ((blk ^ d) // 2) + (nb // 2) * ((dp % 2) ^ far)

    arrive([core] + [same_plane(*s) for s in steps] + [other_plane(d) for d in range(1, planes)])

    def rows_of(n, size):
        return pl.ds(pl.multiple_of(n * size, size), size)

    s1[...] = gall[rows_of(1 - kind, half), :].astype(BF)
    c1 = [send(s1, r1, core), send(small, rs.at[0], core)]
    windows = lambda e, p, z: (
        (e, rows_of(z, rows), pl.ds(pl.multiple_of(p * cut, cut), cut)),
        (e, pl.ds(pl.multiple_of(p * cut + z * rows, rows), rows), slice(None)),
    )
    w_in, w_back = windows(kind, part, plane)
    locals_ = [
        pltpu.make_async_copy(piece.at[0], gin.at[w_in], own.at[0]),
        pltpu.make_async_copy(piece.at[1], gback.at[w_back], own.at[1]),
    ]
    for c in locals_:
        c.start()
    cz = []
    for d in range(1, planes):
        cz.append(send(piece.at[0], gin.at[w_in], other_plane(d)))
        cz.append(send(piece.at[1], gback.at[w_back], other_plane(d)))

    done(c1)
    acc[...] = gall[rows_of(kind, half), :] + r1[...].astype(F32)
    small_acc[0] = small[...] + rs[0]
    c2 = []
    for n, (far, d) in enumerate(steps):
        p = part_of(far, d)
        s2[n] = acc[rows_of(p, quarter), :].astype(BF)
        c2.append(send(s2.at[n], r2.at[n], same_plane(far, d)))
        c2.append(send(small_acc.at[0], rs.at[1 + n], same_plane(far, d)))
    done(cz)
    for c in locals_:
        c.wait()
    columns = pl.ds(pl.multiple_of(part * cut, cut), cut)
    w_in, w_back = (kind, slice(None), columns), (kind, columns, slice(None))
    cp = []
    done(c2)
    mine = pair_sum([acc[rows_of(part, quarter), :]] + [r2[n].astype(F32) for n in range(members - 1)])
    small_acc[1] = pair_sum([small_acc[0]] + [rs[1 + n] for n in range(members - 1)])
    c3 = []
    acc[0:quarter, :] = mine
    s3[...] = mine.astype(BF)
    for d in range(1, planes):
        c3.append(send(s3.at[rows_of(plane ^ d, share), :], r3.at[d - 1], other_plane(d)))
        c3.append(send(small_acc.at[1], rs.at[members + d - 1], other_plane(d)))
    for far, d in steps:
        cp.append(send(gin.at[w_in], gin.at[w_in], same_plane(far, d)))
        cp.append(send(gback.at[w_back], gback.at[w_back], same_plane(far, d)))
    done(c3)
    mine = pair_sum([acc[rows_of(plane, share), :]] + [r3[d].astype(F32) for d in range(planes - 1)])
    small_out[...] = pair_sum([small_acc[1]] + [rs[members + d] for d in range(planes - 1)])
    at = pl.multiple_of(kind * half + part * quarter + plane * share, share)
    fl[pl.ds(at, share), :] = mine.astype(BF)
    w = fl.at[pl.ds(at, share), :]
    c4 = [send(w, w, other_plane(d)) for d in range(1, planes)]
    done(c4)
    at = pl.multiple_of(kind * half + part * quarter, quarter)
    w = fl.at[pl.ds(at, quarter), :]
    c5 = [send(w, w, same_plane(far, d)) for far, d in steps]
    done(c5)
    w = fl.at[rows_of(kind, half), :]
    c6 = [send(w, w, core)]
    done(cp)
    c7 = [send(gin.at[kind], gin.at[kind], core), send(gback.at[kind], gback.at[kind], core)]
    done(c6)
    flat[...] = fl[...]
    done(c7)
    for c in waits:
        c.wait_send()


def whole(shape):
    return pl.BlockSpec(shape, lambda *_: (0,) * len(shape))


def held(shape):
    return pl.BlockSpec(shape, lambda *_: (0,) * len(shape), pipeline_mode=pl.Buffered(1))


ANY = pl.BlockSpec(memory_space=pl.ANY)
DMA = pltpu.SemaphoreType.DMA


def shaped(shape, dtype):
    return jax.ShapeDtypeStruct(shape, dtype)


def params(number):
    return pltpu.CompilerParams(
        vmem_limit_bytes=VMEM_LIMIT, collective_id=number, has_side_effects=True
    )


def forward_call(packed, x, start, g1, wqkv, wkvt, wo, g2, wc, srcs):
    nb = lax.axis_size("blk")
    width = wo.shape[0]
    length = nb * BLOCK
    blocks = length // BLOCK
    rows = wc.shape[0]
    per = BLOCK // GROUP
    experts = rows // per
    phase = lambda i: jnp.maximum(i - blocks, 0)
    col_block = lambda n: pl.BlockSpec((n, BLOCK), lambda i: (0, phase(i)))
    moves = len(srcs)
    copies = moves + (not packed)
    return pl.pallas_call(
        functools.partial(forward_kernel, packed, blocks, nb, moves),
        grid=(2 * blocks,),
        in_specs=[
            held(x.shape) if packed else ANY, col_block(1), held(g1.shape), held(wqkv.shape),
            held(wkvt.shape), held(wo.shape), held(g2.shape), held(wc.shape),
        ] + [ANY] * moves,
        out_specs=[
            whole((length, width)), whole((length, width)), whole((length, width)),
            whole((width, length)), col_block(width), col_block(width // HEAD_DIM),
            pl.BlockSpec((BLOCK, width), lambda i: (phase(i), 0)),
            col_block(rows),
            pl.BlockSpec((experts, per, width), lambda i: (0, phase(i), 0)),
        ] + [ANY] * copies,
        out_shape=[
            shaped((length, width), BF), shaped((length, width), BF), shaped((length, width), BF),
            shaped((width, length), BF), shaped((width, length), BF),
            shaped((width // HEAD_DIM, length), F32),
            shaped((length, width), F32),
            shaped((rows, length), F32),
            shaped((experts, length // GROUP, width), F32),
        ] + [shaped(a.shape, a.dtype) for a in srcs]
        + ([] if packed else [shaped((nb, BLOCK, width), BF)]),
        scratch_shapes=[
            pltpu.VMEM((width, length), BF), pltpu.VMEM((length, BLOCK), F32),
            DMA((copies + 1,)), DMA((copies * (nb - 1),)), DMA((copies * (nb - 1),)),
        ] + ([] if packed else [pltpu.VMEM((nb, BLOCK, width), BF)]),
        compiler_params=params(2 if packed else 1),
        name="attention_forward",
    )(x, start, g1, wqkv, wkvt, wo, g2, wc, *srcs)


def experts_call(mgs, gates, cot, w_in, w_back):
    micros, length, width = cot.shape
    experts, _, ff = w_in.shape
    nb = lax.axis_size("blk")
    blocks = length // BLOCK
    groups = micros * length // GROUP
    chunk = min(CHUNK, ff)
    by_expert = lambda n: pl.BlockSpec((1, n, width), lambda e, c: (e, 0, 0))
    members = len(plane_steps(nb))
    return pl.pallas_call(
        functools.partial(experts_kernel, micros, blocks, nb),
        grid=(experts, ff // chunk),
        in_specs=[held(a.shape) for a in mgs] + [held(a.shape) for a in gates]
        + [
            held(cot.shape),
            pl.BlockSpec((1, width, chunk), lambda e, c: (e, 0, c)),
            pl.BlockSpec((1, chunk, width), lambda e, c: (e, c, 0)),
        ],
        out_specs=[by_expert(groups)] * 2 + [whole((2, 2 * (members + 1) * groups, width))],
        out_shape=[shaped((experts, groups, width), F32)] * 2
        + [shaped((2, 2 * (members + 1) * groups, width), BF)],
        scratch_shapes=[
            pltpu.VMEM((experts, 2, groups, width), BF), pltpu.VMEM((2, 2, groups, width), BF),
            pltpu.VMEM((members, 2, 2, groups, width), BF), DMA((members + 1,)), DMA((members + 1,)),
        ],
        compiler_params=params(3),
        name="experts",
    )(*mgs, *gates, cot, w_in, w_back)


def backward_call(packed, micro, x, cot, h, gate, eo, dmg, ob, lse, q, k, v, kt, start, g1, g2, wc,
                  wqt, wk, wv, wo, extra, first):
    nb = lax.axis_size("blk")
    planes = lax.axis_size("dp") // 2
    length, width = x.shape
    blocks = length // BLOCK
    rows = wc.shape[0]
    per = BLOCK // GROUP
    experts = rows // per
    heads = width // HEAD_DIM
    back = lambda i: blocks - 1 - i
    row_block = pl.BlockSpec((BLOCK, width), lambda i: (back(i), 0))
    col_block = lambda n: pl.BlockSpec((n, BLOCK), lambda i: (0, back(i)))
    group_block = pl.BlockSpec((experts, per, width), lambda i: (0, micro * blocks + back(i), 0))
    sums = [(4 * width, width), (rows + 16, width)]
    blocked = shaped((nb, BLOCK, width), BF)
    scratch = [
        pltpu.VMEM((length, width), F32), pltpu.VMEM((length, width), F32),
        pltpu.VMEM((width, BLOCK), BF), pltpu.VMEM((BLOCK, width), BF),
        pltpu.VMEM((width, BLOCK), BF), pltpu.VMEM((heads, BLOCK), F32),
        pltpu.VMEM((length, BLOCK), F32),
        pltpu.VMEM((nb, BLOCK, width), BF), pltpu.VMEM((nb, BLOCK, width), BF),
        DMA((2,)), DMA((2 * (nb - 1),)), DMA((2 * (nb - 1),)),
    ]
    out_specs = [ANY, ANY] + [whole(s) for s in sums]
    out_shape = [blocked, blocked] + [shaped(s, F32) for s in sums]
    if first:
        factors, w_in, w_back = extra
        cut = w_in.shape[2] // nb
        assert cut == width
        piece = (2, width // planes, cut)
        extra_specs = [held(factors.shape), ANY, ANY]
        out_specs.append(whole(piece))
        out_shape.append(shaped(piece, BF))
        scratch += [
            pltpu.VMEM((width, cut), BF), pltpu.VMEM((cut, width), BF),
            pltpu.VMEM((planes,) + piece, BF), pltpu.VMEM((planes - 1,) + piece, BF),
            DMA((2,)), DMA((planes - 1,)), DMA((planes - 1,)),
        ]
    else:
        extra_specs = [held(s) for s in sums]
    return pl.pallas_call(
        functools.partial(backward_kernel, packed, blocks, nb, planes, first),
        grid=(blocks,),
        in_specs=[
            row_block, row_block, row_block, col_block(rows), group_block, group_block,
            col_block(width), col_block(heads), row_block, held(k.shape), held(v.shape),
            held(kt.shape), col_block(1), held(g1.shape), held(g2.shape), held(wc.shape),
            held(wqt.shape), held(wk.shape), held(wv.shape), held(wo.shape),
        ] + extra_specs,
        out_specs=out_specs,
        out_shape=out_shape,
        scratch_shapes=scratch,
        compiler_params=params(4 if first else 5),
        name="attention_backward",
    )(x, cot, h, gate, eo, dmg, ob, lse, q, k, v, kt, start, g1, g2, wc, wqt, wk, wv, wo, *extra)


def tail_call(gall, small, piece, ff):
    nb = lax.axis_size("blk")
    planes = lax.axis_size("dp") // 2
    total, width = gall.shape
    members = len(plane_steps(nb)) + 1
    half, quarter = total // 2, total // 2 // members
    share = quarter // planes
    copies = 5 + 5 * (planes - 1) + 5 * (members - 1)
    vm = pl.BlockSpec(memory_space=pltpu.VMEM)
    return pl.pallas_call(
        functools.partial(tail_kernel, nb, planes),
        in_specs=[vm, vm, vm],
        out_specs=[vm, vm, ANY, ANY],
        out_shape=[
            shaped((total, width), BF), shaped(small.shape, F32),
            shaped((2, width, ff), BF), shaped((2, ff, width), BF),
        ],
        scratch_shapes=[
            pltpu.VMEM((half, width), BF), pltpu.VMEM((half, width), BF),
            pltpu.VMEM((members - 1, quarter, width), BF),
            pltpu.VMEM((members - 1, quarter, width), BF), pltpu.VMEM((quarter, width), BF),
            pltpu.VMEM((planes - 1, share, width), BF), pltpu.VMEM((total, width), BF),
            pltpu.VMEM((half, width), F32),
            pltpu.VMEM((members + planes - 1,) + small.shape, F32),
            pltpu.VMEM((2,) + small.shape, F32),
            DMA((2,)), DMA((copies,)), DMA((copies,)),
        ],
        compiler_params=params(6),
        name="gradient_sums",
    )(gall, small, piece)


def local(block_input, segment_ids, gain_one, w_query, w_key, w_value, w_out, gain_two, w_ctrl,
          w_in, w_back, cotangent):
    micros, seqs, rows, width = block_input.shape
    experts, _, ff = w_in.shape
    nb = lax.axis_size("blk")
    length = nb * rows
    per = BLOCK // GROUP

    g1, g2 = gain_one.reshape(1, width), gain_two.reshape(1, width)
    wqkv = jnp.concatenate([w_query, w_key, w_value], axis=1)
    wkvt = jnp.concatenate([w_key, w_value], axis=1).T
    wqt = w_query.T
    wc = jnp.repeat(w_ctrl.T, per, axis=0)
    no_start = jnp.zeros((1, length), jnp.int32)

    seg_src = segment_ids.reshape(nb, 2, rows // 2)
    *fwd0, x1, seg, x0 = forward_call(
        False, block_input[0], no_start, g1, wqkv, wkvt, w_out, g2, wc, (block_input[1], seg_src)
    )
    seg = seg.reshape(1, length)
    start = jnp.sum((seg.reshape(length, 1) < seg).astype(jnp.int32), axis=0, keepdims=True)
    x1 = x1.reshape(length, width)
    *fwd1, cot0, cot1 = forward_call(
        True, x1, start, g1, wqkv, wkvt, w_out, g2, wc, (cotangent[0], cotangent[1])
    )
    xs = [x0.reshape(length, width), x1]
    cots = [cot0.reshape(length, width), cot1.reshape(length, width)]
    fwd = [fwd0, fwd1]
    starts = [no_start, start]
    eo, dmg, factors = experts_call(
        [f[8] for f in fwd], [f[7] for f in fwd], jnp.stack(cots), w_in, w_back
    )
    acts, gis = [], []
    extra = (factors, w_in, w_back)
    for m in range(micros):
        q, k, v, kt, ob, lse, h, gate, _ = fwd[m]
        act, gi, *sums = backward_call(
            m > 0, m, xs[m], cots[m], h, gate, eo, dmg, ob, lse, q, k, v, kt, starts[m], g1, g2, wc,
            wqt, w_key, w_value, w_out, extra, m == 0,
        )
        acts.append(act)
        gis.append(gi)
        if m == 0:
            *sums, piece = sums
        extra = sums
    flat, small, grad_in, grad_back = tail_call(*sums, piece, ff)
    flat = flat.astype(F32).reshape(4, width, width)
    ctrl = jnp.sum(small[: experts * per].reshape(experts, per, width), axis=1).T
    return (
        jnp.stack(acts), jnp.stack(gis), small[experts * per + 8], flat[0].T, flat[1], flat[2],
        flat[3], small[experts * per], ctrl, grad_in.astype(F32), grad_back.astype(F32),
    )


def solution(mesh):
    data = P(None, "dp", "blk", None)
    in_specs = (data, P("dp", "blk")) + (P(),) * 9 + (data,)
    out_specs = (data, data) + (P(),) * 9
    return jax.shard_map(local, mesh=mesh, in_specs=in_specs, out_specs=out_specs, check_vma=False)
```

```python
import functools

import jax
import jax.numpy as jnp
from jax import lax
from jax.experimental import pallas as pl
from jax.experimental.pallas import tpu as pltpu
from jax.sharding import PartitionSpec as P

HEAD_DIM = 64
GROUP = 32
EPSILON = 1e-05
BLOCK = 256
CHUNK = 512
SCALE = 0.125
MASKED = -1e30
VMEM_LIMIT = 60 * 1024 * 1024
BF = jnp.bfloat16
F32 = jnp.float32
MESH = pl.DeviceIdType.MESH


def dot(a, b, ca, cb):
    return lax.dot_general(a, b, (((ca,), (cb,)), ((), ())), preferred_element_type=F32)


def nn(a, b):
    return dot(a, b, 1, 0)


def nt(a, b):
    return dot(a, b, 1, 1)


def tn(a, b):
    return dot(a, b, 0, 0)


def key_range(packed, i):
    low = max(0, i * BLOCK - BLOCK - BLOCK // 2) if packed else 0
    return low, (i + 1) * BLOCK - low


def head_masks():
    lane = lax.broadcasted_iota(jnp.int32, (1, 2 * HEAD_DIM), 1)
    first = (lane < HEAD_DIM).astype(F32).astype(BF)
    return first, (lane >= HEAD_DIM).astype(F32).astype(BF)


def group_match(rows, tokens):
    row = lax.broadcasted_iota(jnp.int32, (rows, tokens), 0)
    col = lax.broadcasted_iota(jnp.int32, (rows, tokens), 1)
    return (row % (tokens // GROUP)) == (col // GROUP)


def fill_bias(bias_ref, start_ref, packed, i):
    low, count = key_range(packed, i)
    q_pos = i * BLOCK + lax.broadcasted_iota(jnp.int32, (1, BLOCK), 1)
    if packed:
        k_pos = low + lax.broadcasted_iota(jnp.int32, (count, BLOCK), 0)
        allowed = (k_pos <= q_pos) & (k_pos >= start_ref[...])
        bias_ref[0:count, :] = jnp.where(allowed, 0.0, MASKED)
    else:
        k_pos = i * BLOCK + lax.broadcasted_iota(jnp.int32, (BLOCK, BLOCK), 0)
        bias_ref[0:BLOCK, :] = jnp.where(k_pos <= q_pos, 0.0, MASKED)


def add_bias(scores, bias_ref, packed, count):
    if packed:
        return scores + bias_ref[0:count, :]
    last = scores[count - BLOCK :, :] + bias_ref[0:BLOCK, :]
    if count == BLOCK:
        return last
    return jnp.concatenate([scores[: count - BLOCK, :], last], axis=0)


def rms(values):
    return lax.rsqrt(jnp.mean(values * values, axis=-1, keepdims=True) + EPSILON)


def peer(axis, me, d):
    return {axis: me ^ d}


def arrive(partners):
    barrier = pltpu.get_barrier_semaphore()
    for p in partners:
        pl.semaphore_signal(barrier, inc=1, device_id=p, device_id_type=MESH)
    pl.semaphore_wait(barrier, len(partners))


def remote(src, dst, sems, k, where):
    return pltpu.make_async_remote_copy(
        src_ref=src, dst_ref=dst, send_sem=sems[0].at[k], recv_sem=sems[1].at[k],
        device_id=where, device_id_type=MESH,
    )


class Exchange:
    def __init__(self, nb, src, dst, own, sems, base):
        self.nb, self.src, self.dst, self.own, self.sems, self.base = nb, src, dst, own, sems, base
        self.me = lax.axis_index("blk")

    def local(self):
        return pltpu.make_async_copy(
            self.src.at[self.me], self.dst.at[self.me], self.own.at[self.base]
        )

    def copy(self, d):
        return remote(
            self.src.at[self.me ^ d], self.dst.at[self.me], self.sems,
            self.base * (self.nb - 1) + d - 1, peer("blk", self.me, d),
        )

    def start(self):
        self.local().start()
        for d in range(1, self.nb):
            self.copy(d).start()

    def wait(self):
        self.local().wait()
        for d in range(1, self.nb):
            self.copy(d).wait()


def unit(n):
    row = lax.broadcasted_iota(jnp.int32, (n, n), 0)
    col = lax.broadcasted_iota(jnp.int32, (n, n), 1)
    return (row == col).astype(F32).astype(BF)


def split_three(a):
    high = a.astype(BF)
    rest = a - high.astype(F32)
    mid = rest.astype(BF)
    return [high, mid, (rest - mid.astype(F32)).astype(BF)]


def head_rows(heads, width):
    row = lax.broadcasted_iota(jnp.int32, (heads, width), 0)
    col = lax.broadcasted_iota(jnp.int32, (heads, width), 1)
    return (row == col // HEAD_DIM).astype(F32).astype(BF)


def forward_kernel(micros, blocks, nb, x_src, seg_src, cot_src, g1_ref, wq_ref, wk_ref, wv_ref, wo_ref,
                   g2_ref, wc_ref, q_ref, k_ref, v_ref, kt_ref, ob_ref, lse_ref, h_ref, gate_ref,
                   mg_ref, start_ref, x_out, cot_out, x_all, seg_all, bias, o_acc, sums, eye, own,
                   send_sem, recv_sem):
    sems = (send_sem, recv_sem)
    now = pl.program_id(0)
    span = 2 * blocks
    micro, step = now // span, now % span
    width = wo_ref.shape[0]
    pairs = width // (2 * HEAD_DIM)
    me = lax.axis_index("blk")
    xs = [Exchange(nb, x_src.at[m], x_all.at[m], own, sems, m) for m in range(micros)]
    segs = Exchange(nb, seg_src, seg_all, own, sems, micros)
    cots = [
        Exchange(nb, cot_src.at[m], cot_out.at[m], own, sems, micros + 1 + m) for m in range(micros)
    ]
    keep = pltpu.make_async_copy(x_all, x_out, own.at[2 * micros + 1])

    @pl.when(now == 0)
    def _():
        xs[0].local().start()
        eye[...] = unit(width)
        arrive([peer("blk", me, d) for d in range(1, nb)])
        for d in range(1, nb):
            xs[0].copy(d).start()

    @pl.when(step < blocks)
    def _():
        block = me ^ step
        for m in range(micros):
            pl.when((micro == m) & (step == 0))(xs[m].local().wait)
            for d in range(1, nb):
                pl.when((micro == m) & (step == d))(xs[m].copy(d).wait_recv)
        x = x_all[micro, block].astype(F32)
        n1 = (x * rms(x) * g1_ref[...]).astype(BF)
        at = pl.ds(pl.multiple_of(block * BLOCK, BLOCK), BLOCK)
        q_ref[0, at, :] = nn(n1, wq_ref[...]).astype(BF)
        k = nn(n1, wk_ref[...]).astype(BF)
        k_ref[0, at, :] = k
        v_ref[0, at, :] = nn(n1, wv_ref[...]).astype(BF)
        kt_ref[0, :, at] = nt(eye[...], k).astype(BF)

    @pl.when(now == nb - 1)
    def _():
        segs.start()
        for m in range(1, micros):
            xs[m].start()

    @pl.when(now == blocks)
    def _():
        for c in cots:
            c.start()

    @pl.when(now == span)
    def _():
        segs.wait()
        counts = [
            jnp.sum(jnp.sum((seg_all[...] < d).astype(F32), axis=0), keepdims=True)
            for d in range(1, nb * seg_all.shape[1] * seg_all.shape[2] // BLOCK)
        ]
        for b in range(blocks):
            seg = jnp.concatenate([seg_all[b, n : n + 1, :] for n in range(seg_all.shape[1])], axis=1)
            start = jnp.zeros(seg.shape, F32)
            for d, count in enumerate(counts):
                start = jnp.where(seg == d + 1, count, start)
            start_ref[b] = start.astype(jnp.int32)

    masks = head_masks()

    def attend(packed, i):
        low, count = key_range(packed, i)
        fill_bias(bias, start_ref[i], packed, i)
        for hp in range(pairs):
            lanes = slice(hp * 2 * HEAD_DIM, (hp + 1) * 2 * HEAD_DIM)
            q_pair = q_ref[0, i * BLOCK : (i + 1) * BLOCK, lanes]
            k_pair = k_ref[0, low : low + count, lanes]
            v_pair = v_ref[0, low : low + count, lanes]
            o_pair = None
            for h in range(2):
                scores = add_bias(nt(k_pair, q_pair * masks[h]), bias, packed, count)
                top = jnp.max(scores, axis=0, keepdims=True)
                p = jnp.exp((scores - top) * SCALE)
                total = jnp.sum(p, axis=0, keepdims=True)
                o = tn(p.astype(BF), v_pair * masks[h])
                o_pair = o if o_pair is None else o_pair + o
                sums[hp * 2 + h : hp * 2 + h + 1, :] = 1.0 / total
                lse_ref[0, hp * 2 + h : hp * 2 + h + 1, :] = top * SCALE + jnp.log(total)
            o_acc[:, lanes] = o_pair

    for m in range(micros):
        for i in range(blocks):
            pl.when(now == m * span + blocks + i)(functools.partial(attend, m > 0, i))

    @pl.when(step >= blocks)
    def _():
        heads = head_rows(sums.shape[0], width)
        scale = tn(
            jnp.concatenate(split_three(sums[...]), axis=0), jnp.concatenate([heads] * 3, axis=0)
        )
        ob = (o_acc[...] * scale).astype(BF)
        ob_ref[0] = ob
        h = x_all[micro, step - blocks].astype(F32) + nn(ob, wo_ref[...])
        h_ref[0] = h
        n2 = (h * rms(h) * g2_ref[...]).astype(BF)
        logits = nt(wc_ref[...], n2)
        rows = logits.shape[0]
        match = group_match(rows, BLOCK)
        logits = jnp.where(match, logits, MASKED)
        e = jnp.where(match, jnp.exp(logits - jnp.max(logits, axis=1, keepdims=True)), 0.0)
        gate = e / jnp.sum(e, axis=1, keepdims=True)
        gate_ref[...] = gate
        mg = nn(gate.astype(BF), n2).astype(BF).astype(F32)
        half = rows // mg_ref.shape[0]
        for j in range(mg_ref.shape[0]):
            mg_ref[j] = mg[j * half : (j + 1) * half]

    @pl.when(now == span + nb)
    def _():
        keep.start()

    @pl.when(now == micros * span - 1)
    def _():
        keep.wait()
        for x in xs:
            for d in range(1, nb):
                x.copy(d).wait_send()
        for c in cots:
            c.wait()


def gelu_both(u):
    c = 0.7978845608028654
    t = jnp.tanh(c * (u + 0.044715 * (u * u * u)))
    act = 0.5 * u * (1.0 + t)
    slope = 0.5 * (1.0 + t) + 0.5 * u * (1.0 - t * t) * (c * (1.0 + 3 * 0.044715 * (u * u)))
    return act, slope


def same_plane(far, d):
    return {"dp": lax.axis_index("dp") ^ far, "blk": lax.axis_index("blk") ^ d}


def plane_steps(nb):
    return [(far, d) for far in (0, 1) for d in range(0, nb, 2) if far or d]


def experts_kernel(micros, blocks, nb, *refs):
    mg_ref, gate_ref, cot_ref, win_ref, wback_ref = refs[:5]
    eo_ref, dmg_ref, all_ref, factors, mine, gathered, send_sem, recv_sem = refs[5:]
    sems = (send_sem, recv_sem)
    e, c = pl.program_id(0), pl.program_id(1)
    at = e * pl.num_programs(1) + c
    last = pl.num_programs(0) * pl.num_programs(1) - 1
    per = BLOCK // GROUP
    n_exp = factors.shape[0]
    groups = micros * blocks * per
    blk = lax.axis_index("blk")
    kind = blk % n_exp
    steps = plane_steps(nb)

    def core_copy():
        return remote(factors.at[1 - kind], mine.at[1], sems, 0, peer("blk", blk, 1))

    def plane_copy(n):
        return remote(mine, gathered.at[n], sems, 1 + n, same_plane(*steps[n]))

    @pl.when(at == 0)
    def _():
        deo = []
        for m in range(micros):
            for i in range(blocks):
                at_rows = (m * blocks + i) * BLOCK
                deo.append(nn(gate_ref[:, at_rows : at_rows + BLOCK].astype(BF), cot_ref[m, i]))
        for j in range(n_exp):
            factors[j, 0] = mg_ref[j].astype(BF)
            factors[j, 1] = jnp.concatenate(
                [d[j * per : (j + 1) * per] for d in deo], axis=0
            ).astype(BF)
        arrive([peer("blk", blk, 1)] + [same_plane(*s) for s in steps])
        core_copy().start()
        mine[0] = factors[kind]

    mg, deo = factors[e, 0], factors[e, 1]
    act, slope = gelu_both(nn(mg, win_ref[0]))
    eo_part = nn(act.astype(BF), wback_ref[0])
    du = (slope * nt(deo, wback_ref[0])).astype(BF)
    dmg_part = nt(du, win_ref[0])

    @pl.when(c == 0)
    def _():
        eo_ref[0] = eo_part
        dmg_ref[0] = dmg_part

    @pl.when(c > 0)
    def _():
        eo_ref[0] += eo_part
        dmg_ref[0] += dmg_part

    @pl.when(at == 2)
    def _():
        core_copy().wait()
        for n in range(len(steps)):
            plane_copy(n).start()

    @pl.when(at == last)
    def _():
        for n in range(len(steps)):
            plane_copy(n).wait()
        for n in range(len(steps) + 1):
            piece = mine[...] if n == 0 else gathered[n - 1]
            for f in range(2):
                for j in range(2):
                    rows = slice((2 * n + j) * groups, (2 * n + j + 1) * groups)
                    all_ref[f, rows, :] = piece[j, f]


class Return:
    def __init__(self, nb, buf, out, own, sems, base):
        self.nb, self.buf, self.out, self.own, self.sems, self.base = nb, buf, out, own, sems, base
        self.me = lax.axis_index("blk")

    def local(self):
        return pltpu.make_async_copy(
            self.buf.at[self.me], self.out.at[self.me], self.own.at[self.base]
        )

    def copy(self, d):
        return remote(
            self.buf.at[self.me ^ d], self.out.at[self.me], self.sems,
            self.base * (self.nb - 1) + d - 1, peer("blk", self.me, d),
        )

    def start(self, i):
        pl.when(i == self.me)(lambda: self.local().start())
        for d in range(1, self.nb):
            pl.when(i == (self.me ^ d))(lambda d=d: self.copy(d).start())

    def wait(self):
        self.local().wait()
        for d in range(1, self.nb):
            self.copy(d).wait()


class Plan:
    def __init__(self, sems):
        self.sems, self.count, self.sets = sems, 0, {}

    def add(self, name, makers):
        self.sets[name] = list(enumerate(makers, self.count))
        self.count += len(makers)

    def each(self, name):
        for k, maker in self.sets[name]:
            src, dst, where = maker()
            yield remote(src, dst, self.sems, k, where)

    def start(self, name):
        for c in self.each(name):
            c.start()

    def arrived(self, name):
        for c in self.each(name):
            c.wait_recv()

    def sent(self, name):
        for c in self.each(name):
            c.wait_send()


def other_plane(d):
    return {"dp": lax.axis_index("dp") ^ (2 * d)}


def pair_sum(parts):
    while len(parts) > 1:
        parts = [parts[n] + parts[n + 1] for n in range(0, len(parts), 2)]
    return parts[0]


def rows_of(n, size):
    return pl.ds(pl.multiple_of(n * size, size), size)


def backward_kernel(micros, blocks, nb, planes, x_ref, cot_ref, h_ref, gate_ref, eo_ref, dmg_ref, ob_ref,
                    lse_ref, q_ref, k_ref, v_ref, kt_ref, start_ref, g1_ref, g2_ref, wc_ref, wq_ref,
                    wk_ref, wv_ref, wo_ref, factors, win_hbm, wback_hbm, act_ref, gi_ref, flat_ref,
                    small_ref, gin, gback, dh_all, n1_all, dob, delta, dq_all, dk_all, dv_all, dk_acc,
                    dv_acc, gacc, go_acc, bias, act_buf, gi_buf, win, wback, ours, theirs, piece, s1,
                    r1, s2, r2, s3, r3, fl, small, rs, own, load_sem, ret_send, ret_recv, send_sem,
                    recv_sem):
    now = pl.program_id(0)
    width = wo_ref.shape[0]
    pairs = width // (2 * HEAD_DIM)
    pair_lanes = 2 * HEAD_DIM
    span = 2 * blocks + pairs
    micro, step = now // span, now % span
    last = (micros - 1) * span
    blk, dp = lax.axis_index("blk"), lax.axis_index("dp")
    kind, plane = blk % 2, dp // 2
    steps = plane_steps(nb)
    members = len(steps) + 1
    core = lambda: peer("blk", lax.axis_index("blk"), 1)

    def part_of(far, d):
        return ((blk ^ d) // 2) + (nb // 2) * ((dp % 2) ^ far)

    part = part_of(0, 0)
    cut = win.shape[1]
    rets = (ret_send, ret_recv)
    acts = [Return(nb, act_buf.at[m], act_ref.at[m], own, rets, 2 * m) for m in range(micros)]
    gis = [Return(nb, gi_buf.at[m], gi_ref.at[m], own, rets, 2 * m + 1) for m in range(micros)]
    columns = rows_of(part, cut)
    loads = [
        lambda: pltpu.make_async_copy(win_hbm.at[kind, :, columns], win, load_sem.at[0]),
        lambda: pltpu.make_async_copy(wback_hbm.at[kind, columns, :], wback, load_sem.at[1]),
    ]
    rows = width // planes

    def window(which, p, z):
        if which == 0:
            return gin.at[kind, rows_of(z, rows), rows_of(p, cut)]
        at = pl.multiple_of(p * cut + z * rows, rows)
        return gback.at[kind, pl.ds(at, rows), :]

    def slab(which, p):
        if which == 0:
            return gin.at[kind, :, rows_of(p, cut)]
        return gback.at[kind, rows_of(p, cut), :]

    mine = [
        lambda: pltpu.make_async_copy(piece.at[0], window(0, part, plane), load_sem.at[2]),
        lambda: pltpu.make_async_copy(piece.at[1], window(1, part, plane), load_sem.at[3]),
    ]
    y_peer, x_peer = steps[0], steps[1]
    others = range(1, planes)
    both = range(2)
    half = fl.shape[1] // 2
    quarter = half // members
    plan = Plan((send_sem, recv_sem))
    plan.add("rs", [lambda d=d: (ours.at[plane ^ d], theirs.at[d - 1], other_plane(d)) for d in others])
    plan.add("z", [
        lambda d=d, w=w: (piece.at[w], window(w, part, plane), other_plane(d)) for d in others for w in both
    ])
    for name, to in (("y0", y_peer), ("x0", x_peer)):
        plan.add(name, [
            lambda w=w, to=to: (piece.at[w], window(w, part, plane), same_plane(*to)) for w in both
        ])

    def onward(p, z, w, to):
        return window(w, p, z), window(w, p, z), same_plane(*to)

    part_y = part_of(*y_peer)
    plan.add("yx0", [lambda w=w: onward(part_y, plane, w, x_peer) for w in both])
    for name, p, to in (("y1", part, y_peer), ("x1", part, x_peer), ("yx1", part_y, x_peer)):
        plan.add(name, [
            lambda d=d, w=w, p=p, to=to: onward(p, plane ^ d, w, to) for d in others for w in both
        ])
    for name, p in zip(("c_own", "c_y", "c_x", "c_d"), [part] + [part_of(*t) for t in steps]):
        plan.add(name, [lambda w=w, p=p: (slab(w, p), slab(w, p), core()) for w in both])
    for c in range(pairs):
        plan.add(f"a{c}", [lambda c=c: (s1.at[c], r1.at[c], core())])
        plan.add(f"b{c}", [
            lambda c=c, n=n: (s2.at[c, n], r2.at[c, n], same_plane(*steps[n])) for n in range(members - 1)
        ])
        plan.add(f"z{c}", [lambda c=c, d=d: (s3.at[c], r3.at[c, d - 1], other_plane(d)) for d in others])

        def share(c, n):
            at = pl.multiple_of(kind * half + part * quarter, quarter)
            ref = fl.at[c, pl.ds(at, quarter), :]
            return ref, ref, same_plane(*steps[n])

        def side(c):
            ref = fl.at[c, rows_of(kind, half), :]
            return ref, ref, core()

        plan.add(f"g{c}", [lambda c=c, n=n: share(c, n) for n in range(members - 1)])
        plan.add(f"h{c}", [lambda c=c: side(c)])
    plan.add("sa", [lambda: (small.at[0], rs.at[0], core())])
    plan.add("sb", [lambda n=n: (small.at[1], rs.at[1 + n], same_plane(*steps[n])) for n in range(members - 1)])
    plan.add("sz", [lambda d=d: (small.at[2], rs.at[members + d - 1], other_plane(d)) for d in others])
    assert plan.count <= send_sem.shape[0]

    def chunk_start(c):
        s1[c] = gacc[c, rows_of(1 - kind, half), :].astype(BF)
        plan.start(f"a{c}")

    def chunk_b(c):
        plan.arrived(f"a{c}")
        at = rows_of(kind, half)
        gacc[c, at, :] = gacc[c, at, :] + r1[c].astype(F32)
        for n, to in enumerate(steps):
            s2[c, n] = gacc[c, pl.ds(pl.multiple_of(kind * half + part_of(*to) * quarter, quarter), quarter), :].astype(BF)
        plan.start(f"b{c}")

    def chunk_z(c):
        plan.arrived(f"b{c}")
        at = pl.ds(pl.multiple_of(kind * half + part * quarter, quarter), quarter)
        total = pair_sum([gacc[c, at, :]] + [r2[c, n].astype(F32) for n in range(members - 1)])
        s3[c] = total.astype(BF)
        plan.start(f"z{c}")

    def chunk_g(c):
        plan.arrived(f"z{c}")
        total = pair_sum([s3[c].astype(F32)] + [r3[c, d - 1].astype(F32) for d in others])
        at = pl.ds(pl.multiple_of(kind * half + part * quarter, quarter), quarter)
        fl[c, at, :] = total.astype(BF)
        plan.start(f"g{c}")

    def chunk_h(c):
        plan.arrived(f"g{c}")
        plan.start(f"h{c}")

    def out_copy(c):
        return pltpu.make_async_copy(fl.at[c], flat_ref.at[c], load_sem.at[4 + c])

    def chunk_done(c):
        plan.arrived(f"h{c}")
        out_copy(c).start()

    stages = [chunk_start, chunk_b, chunk_z, chunk_g, chunk_h, chunk_done]

    @pl.when(now == 0)
    def _():
        for c in loads:
            c().start()
        partners = [peer("blk", blk, d) for d in range(1, nb)]
        partners += [same_plane(*s) for s in steps if s[0]] + [other_plane(d) for d in others]
        arrive(partners)
        small[0] = jnp.zeros(small.shape[1:], F32)
        go_acc[...] = jnp.zeros_like(go_acc)
        fill_bias(bias.at[0], None, False, 0)
        for c in loads:
            c().wait()
        mg, deo = factors[0], factors[1]
        act, slope = gelu_both(nn(mg, win[...]))
        du = (slope * nt(deo, wback[...])).astype(BF)
        g_in = tn(mg, du).astype(BF)
        g_back = tn(act.astype(BF), deo).astype(BF)
        for n in range(planes):
            ours[n, 0] = g_in[n * rows : (n + 1) * rows]
            ours[n, 1] = g_back[n * rows : (n + 1) * rows]
        plan.start("rs")

    gate_rows = gate_ref.shape[0]

    @pl.when(step < blocks)
    def _():
        at = rows_of(step, BLOCK)
        h = h_ref[0]
        cot_b = cot_ref[0, 0]
        dout = cot_b.astype(F32)
        r2_ = rms(h)
        z = h * r2_
        n2 = (z * g2_ref[...]).astype(BF)
        gate = gate_ref[...]
        gate_b = gate.astype(BF)
        gate_low = (gate - gate_b.astype(F32)).astype(BF)
        eo = jnp.concatenate([eo_ref[j] for j in range(eo_ref.shape[0])], axis=0)
        dmg = jnp.concatenate([dmg_ref[j] for j in range(dmg_ref.shape[0])], axis=0).astype(BF)
        eo_b = eo.astype(BF)
        eo_low = (eo - eo_b.astype(F32)).astype(BF)
        mixed = tn(
            jnp.concatenate([gate_b, gate_low, gate_b], axis=0),
            jnp.concatenate([eo_b, eo_b, eo_low], axis=0),
        )
        act_buf[micro, step] = (h + mixed).astype(BF)
        for m in range(micros):
            pl.when(micro == m)(functools.partial(acts[m].start, step))
        dw2 = nt(jnp.concatenate([eo_b, eo_low], axis=0), cot_b)
        dw = dw2[:gate_rows] + dw2[gate_rows:] + nt(dmg, n2)
        wdw = gate * dw
        dlog = (wdw - gate * jnp.sum(wdw, axis=1, keepdims=True)).astype(BF)
        dn2 = tn(
            jnp.concatenate([gate_b, dlog], axis=0),
            jnp.concatenate([dmg, wc_ref[...]], axis=0),
        )
        small[0, 0:gate_rows, :] += nn(dlog, n2)
        small[0, gate_rows : gate_rows + 1, :] += jnp.sum(dn2 * z, axis=0, keepdims=True)
        a = dn2 * g2_ref[...]
        dh = dout + r2_ * (a - z * jnp.mean(a * z, axis=-1, keepdims=True))
        dh_all[at, :] = dh
        da = dh.astype(BF)
        dob_b = nt(da, wo_ref[...]).astype(BF)
        dob[at, :] = dob_b
        ob = ob_ref[0]
        go_acc[...] += tn(ob, da)
        prod = dob_b.astype(F32) * ob.astype(F32)
        high = prod.astype(BF)
        low = (prod - high.astype(F32)).astype(BF)
        heads = head_rows(delta.shape[0], width)
        delta[:, at] = nt(heads, high) + nt(heads, low)
        x = x_ref[0, 0].astype(F32)
        n1_all[at, :] = (x * rms(x) * g1_ref[...]).astype(BF)

    for m in range(1, micros):
        for i in range(blocks):
            pl.when(now == m * span + i)(
                functools.partial(fill_bias, bias.at[i], start_ref[i], True, i)
            )

    masks = head_masks()

    def attend(packed):
        hp = step - blocks
        lanes = rows_of(hp, pair_lanes)
        for i in range(blocks):
            low, count = key_range(packed, i)
            at = slice(i * BLOCK, (i + 1) * BLOCK)
            q_pair, dob_pair = q_ref[0, at, :], dob[at, lanes]
            k_pair, v_pair = k_ref[0, low : low + count, :], v_ref[0, low : low + count, :]
            dk_sum = dv_sum = None
            dqs = []
            for h in range(2):
                qm, dm = q_pair * masks[h], dob_pair * masks[h]
                scores = add_bias(nt(k_pair, qm), bias.at[i if packed else 0], packed, count)
                p = jnp.exp(scores * SCALE - lse_ref[0, pl.ds(hp * 2 + h, 1), at])
                dp_ = nt(v_pair, dm)
                ds = (p * (dp_ - delta[pl.ds(hp * 2 + h, 1), at])).astype(BF)
                kt = kt_ref[0, h * HEAD_DIM : (h + 1) * HEAD_DIM, low : low + count]
                dqs.append(nn(kt, ds) * SCALE)
                dk_part, dv_part = nn(ds, qm), nn(p.astype(BF), dm)
                dk_sum = dk_part if dk_sum is None else dk_sum + dk_part
                dv_sum = dv_part if dv_sum is None else dv_sum + dv_part
            old = i * BLOCK - low
            dk_acc[at, :] = dk_sum[old:]
            dv_acc[at, :] = dv_sum[old:]
            if old:
                dk_acc[low : i * BLOCK, :] += dk_sum[:old]
                dv_acc[low : i * BLOCK, :] += dv_sum[:old]
            dq_all[at, lanes] = jnp.concatenate(dqs, axis=0).T.astype(BF)
        dk = (dk_acc[...] * SCALE).astype(BF)
        dv = dv_acc[...].astype(BF)
        dk_all[:, lanes] = dk
        dv_all[:, lanes] = dv
        g = tn(jnp.concatenate([dq_all[:, lanes], dk, dv], axis=1), n1_all[...])
        top = 3 * pair_lanes
        if packed:
            gacc[hp, 0:top, :] += g
            gacc[hp, top:, :] = go_acc[rows_of(hp, pair_lanes), :]
        else:
            gacc[hp, 0:top, :] = g

    for m in range(micros):
        in_phase = (micro == m) & (step >= blocks) & (step < blocks + pairs)
        pl.when(in_phase)(functools.partial(attend, m > 0))

    @pl.when(step >= blocks + pairs)
    def _():
        i = step - blocks - pairs
        at = rows_of(i, BLOCK)
        x = x_ref[0, 0].astype(F32)
        r1_ = rms(x)
        z1 = x * r1_
        dn1 = (
            nt(dq_all[at, :], wq_ref[...]) + nt(dk_all[at, :], wk_ref[...]) + nt(dv_all[at, :], wv_ref[...])
        )
        small[0, gate_rows + 8 : gate_rows + 9, :] += jnp.sum(dn1 * z1, axis=0, keepdims=True)
        b = dn1 * g1_ref[...]
        gi = dh_all[at, :] + r1_ * (b - z1 * jnp.mean(b * z1, axis=-1, keepdims=True))
        gi_buf[micro, i] = gi.astype(BF)
        for m in range(micros):
            pl.when(micro == m)(functools.partial(gis[m].start, i))

    @pl.when(now == blocks + pairs)
    def _():
        plan.arrived("rs")
        total = pair_sum([ours[plane].astype(F32)] + [theirs[d - 1].astype(F32) for d in others])
        piece[...] = total.astype(BF)
        for c in mine:
            c().start()
        for name in ("z", "y0", "x0"):
            plan.start(name)

    @pl.when(now == last + blocks - 1)
    def _():
        plan.arrived("y0")
        plan.start("yx0")

    @pl.when(now == last + blocks + 1)
    def _():
        for c in mine:
            c().wait()
        plan.arrived("z")
        for name in ("y1", "x1", "c_own"):
            plan.start(name)

    final = micros * span - 1
    late = []
    for at in range(len(stages) + pairs - 1):
        todo = [(at - n, n) for n in reversed(range(len(stages))) if 0 <= at - n < pairs]
        if last + blocks + at > final:
            late += todo
            continue

        @pl.when(now == last + blocks + at)
        def _(todo=todo):
            for c, n in todo:
                stages[n](c)

    @pl.when(now == final)
    def _():
        plan.start("sa")
        plan.arrived("y1")
        for name in ("yx1", "c_y"):
            plan.start(name)
        plan.arrived("sa")
        small[1] = small[0] + rs[0]
        plan.start("sb")
        for c, n in late:
            stages[n](c)
        plan.arrived("sb")
        small[2] = pair_sum([small[1]] + [rs[1 + n] for n in range(members - 1)])
        plan.start("sz")
        for name in ("x0", "x1"):
            plan.arrived(name)
        plan.start("c_x")
        plan.arrived("sz")
        small_ref[...] = pair_sum([small[2]] + [rs[members + d - 1] for d in others])
        for name in ("yx0", "yx1"):
            plan.arrived(name)
        plan.start("c_d")
        for name in ("c_own", "c_y", "c_x", "c_d"):
            plan.arrived(name)
        for c in range(pairs):
            out_copy(c).wait()
        for name in plan.sets:
            plan.sent(name)
        for r in acts + gis:
            r.wait()


def whole(shape):
    return pl.BlockSpec(shape, lambda *_: (0,) * len(shape))


def held(shape):
    return pl.BlockSpec(shape, lambda *_: (0,) * len(shape), pipeline_mode=pl.Buffered(1))


ANY = pl.BlockSpec(memory_space=pl.ANY)
DMA = pltpu.SemaphoreType.DMA


def shaped(shape, dtype):
    return jax.ShapeDtypeStruct(shape, dtype)


def params(number):
    return pltpu.CompilerParams(
        vmem_limit_bytes=VMEM_LIMIT, collective_id=number, has_side_effects=True
    )


def forward_call(x, seg, cot, g1, wq, wk, wv, wo, g2, wc):
    nb = lax.axis_size("blk")
    micros, _, rows_in, width = x.shape
    length = nb * rows_in
    blocks = length // BLOCK
    assert x.shape[1] == nb and rows_in == BLOCK
    rows = wc.shape[0]
    heads = width // HEAD_DIM
    per = BLOCK // GROUP
    experts = rows // per
    span = 2 * blocks
    phase = lambda s: jnp.maximum(s % span - blocks, 0)
    whole_micro = lambda a, b: pl.BlockSpec((1, a, b), lambda s: (s // span, 0, 0))
    flat = lambda s: (s // span) * blocks + phase(s)
    moves = 2 * micros + 1
    return pl.pallas_call(
        functools.partial(forward_kernel, micros, blocks, nb),
        grid=(micros * span,),
        in_specs=[ANY, ANY, ANY] + [held(a.shape) for a in (g1, wq, wk, wv, wo, g2, wc)],
        out_specs=[
            whole_micro(length, width), whole_micro(length, width), whole_micro(length, width),
            whole_micro(width, length),
            pl.BlockSpec((1, BLOCK, width), lambda s: (s // span, phase(s), 0)),
            pl.BlockSpec((1, heads, BLOCK), lambda s: (s // span, 0, phase(s))),
            pl.BlockSpec((1, BLOCK, width), lambda s: (s // span, phase(s), 0)),
            pl.BlockSpec((rows, BLOCK), lambda s: (0, flat(s))),
            pl.BlockSpec((experts, per, width), lambda s: (0, flat(s), 0)),
            whole((blocks, 1, BLOCK)), ANY, ANY,
        ],
        out_shape=[
            shaped((micros, length, width), BF), shaped((micros, length, width), BF),
            shaped((micros, length, width), BF), shaped((micros, width, length), BF),
            shaped((micros, length, width), BF), shaped((micros, heads, length), F32),
            shaped((micros, length, width), F32), shaped((rows, micros * length), F32),
            shaped((experts, micros * length // GROUP, width), F32),
            shaped((blocks, 1, BLOCK), jnp.int32), shaped(x.shape, BF), shaped(x.shape, BF),
        ],
        scratch_shapes=[
            pltpu.VMEM(x.shape, BF), pltpu.VMEM(seg.shape, seg.dtype),
            pltpu.VMEM((length, BLOCK), F32), pltpu.VMEM((BLOCK, width), F32),
            pltpu.VMEM((heads, BLOCK), F32), pltpu.VMEM((width, width), BF),
            DMA((moves + 1,)), DMA((moves * (nb - 1),)), DMA((moves * (nb - 1),)),
        ],
        compiler_params=params(1),
        name="attention_forward",
    )(x, seg, cot, g1, wq, wk, wv, wo, g2, wc)


def experts_call(mg, gate, cot, w_in, w_back):
    micros, nb, _, width = cot.shape
    experts, groups, _ = mg.shape
    ff = w_in.shape[2]
    blocks = gate.shape[1] // BLOCK // micros
    chunk = min(CHUNK, ff)
    by_expert = lambda n: pl.BlockSpec((1, n, width), lambda e, c: (e, 0, 0))
    members = len(plane_steps(nb))
    return pl.pallas_call(
        functools.partial(experts_kernel, micros, blocks, nb),
        grid=(experts, ff // chunk),
        in_specs=[
            held(mg.shape), held(gate.shape), held(cot.shape),
            pl.BlockSpec((1, width, chunk), lambda e, c: (e, 0, c)),
            pl.BlockSpec((1, chunk, width), lambda e, c: (e, c, 0)),
        ],
        out_specs=[by_expert(groups)] * 2 + [whole((2, 2 * (members + 1) * groups, width))],
        out_shape=[shaped((experts, groups, width), F32)] * 2
        + [shaped((2, 2 * (members + 1) * groups, width), BF)],
        scratch_shapes=[
            pltpu.VMEM((experts, 2, groups, width), BF), pltpu.VMEM((2, 2, groups, width), BF),
            pltpu.VMEM((members, 2, 2, groups, width), BF), DMA((members + 1,)), DMA((members + 1,)),
        ],
        compiler_params=params(2),
        name="experts",
    )(mg, gate, cot, w_in, w_back)


def backward_call(x, cot, h, gate, eo, dmg, ob, lse, q, k, v, kt, start, g1, g2, wc, wq, wk, wv, wo,
                  factors, w_in, w_back):
    micros, nb, _, width = x.shape
    planes = lax.axis_size("dp") // 2
    length = q.shape[1]
    blocks = length // BLOCK
    rows = wc.shape[0]
    per = BLOCK // GROUP
    experts = rows // per
    heads = width // HEAD_DIM
    pairs = heads // 2
    ff = w_in.shape[2]
    cut = ff // nb
    assert cut == width
    members = len(plane_steps(nb)) + 1
    span = 2 * blocks + pairs
    m_of = lambda s: s // span
    early = lambda s: jnp.minimum(s % span, blocks - 1)
    pair_of = lambda s: jnp.clip(s % span - blocks, 0, pairs - 1)

    def early_or_late(s):
        t = s % span
        return jnp.where(t < blocks + pairs, jnp.minimum(t, blocks - 1), t - blocks - pairs)

    flat = lambda s: m_of(s) * blocks + early(s)
    row_block = pl.BlockSpec((1, BLOCK, width), lambda s: (m_of(s), early(s), 0))
    group_block = pl.BlockSpec((experts, per, width), lambda s: (0, flat(s), 0))
    pair_block = pl.BlockSpec((1, length, 2 * HEAD_DIM), lambda s: (m_of(s), 0, pair_of(s)))
    piece = (2, width // planes, cut)
    chunk = 4 * 2 * HEAD_DIM
    half = chunk // 2
    quarter = half // members
    reach = max(key_range(True, i)[1] for i in range(blocks))
    small = (rows + 16, width)
    vm = pltpu.VMEM
    copies = 64 + 16 * pairs + 24 * planes
    return pl.pallas_call(
        functools.partial(backward_kernel, micros, blocks, nb, planes),
        grid=(micros * span,),
        in_specs=[
            pl.BlockSpec((1, 1, BLOCK, width), lambda s: (m_of(s), early_or_late(s), 0, 0)),
            pl.BlockSpec((1, 1, BLOCK, width), lambda s: (m_of(s), early(s), 0, 0)),
            row_block,
            pl.BlockSpec((rows, BLOCK), lambda s: (0, flat(s))),
            group_block, group_block, row_block,
            pl.BlockSpec((1, heads, length), lambda s: (m_of(s), 0, 0)),
            pair_block, pair_block, pair_block,
            pl.BlockSpec((1, 2 * HEAD_DIM, length), lambda s: (m_of(s), pair_of(s), 0)),
        ] + [held(a.shape) for a in (start, g1, g2, wc, wq, wk, wv, wo, factors)] + [ANY, ANY],
        out_specs=[ANY, ANY, ANY, whole(small), ANY, ANY],
        out_shape=[
            shaped(x.shape, BF), shaped(x.shape, BF), shaped((pairs, chunk, width), BF),
            shaped(small, F32), shaped(w_in.shape, BF), shaped(w_back.shape, BF),
        ],
        scratch_shapes=[
            vm((length, width), F32), vm((length, width), BF), vm((length, width), BF),
            vm((heads, length), F32), vm((length, width), BF), vm((length, width), BF),
            vm((length, width), BF), vm((length, 2 * HEAD_DIM), F32), vm((length, 2 * HEAD_DIM), F32),
            vm((pairs, chunk, width), F32), vm((width, width), F32), vm((blocks, reach, BLOCK), F32),
            vm(x.shape, BF), vm(x.shape, BF), vm((width, cut), BF), vm((cut, width), BF),
            vm((planes,) + piece, BF), vm((planes - 1,) + piece, BF), vm(piece, BF),
            vm((pairs, half, width), BF), vm((pairs, half, width), BF),
            vm((pairs, members - 1, quarter, width), BF), vm((pairs, members - 1, quarter, width), BF),
            vm((pairs, quarter, width), BF), vm((pairs, planes - 1, quarter, width), BF),
            vm((pairs, chunk, width), BF), vm((3,) + small, F32),
            vm((members + planes - 1,) + small, F32),
            DMA((2 * micros,)), DMA((4 + pairs,)), DMA((2 * micros * (nb - 1),)),
            DMA((2 * micros * (nb - 1),)), DMA((copies,)), DMA((copies,)),
        ],
        compiler_params=params(3),
        name="attention_backward",
    )(x, cot, h, gate, eo, dmg, ob, lse, q, k, v, kt, start, g1, g2, wc, wq, wk, wv, wo, factors, w_in,
      w_back)


def local(block_input, segment_ids, gain_one, w_query, w_key, w_value, w_out, gain_two, w_ctrl,
          w_in, w_back, cotangent):
    micros, seqs, rows, width = block_input.shape
    experts, _, ff = w_in.shape
    nb = lax.axis_size("blk")
    per = BLOCK // GROUP
    g1, g2 = gain_one.reshape(1, width), gain_two.reshape(1, width)
    wc = jnp.repeat(w_ctrl.T, per, axis=0)
    seg = segment_ids.reshape(nb, 2, rows // 2)
    q, k, v, kt, ob, lse, h, gate, mg, start, x, cot = forward_call(
        block_input, seg, cotangent, g1, w_query, w_key, w_value, w_out, g2, wc
    )
    eo, dmg, factors = experts_call(mg, gate, cot, w_in, w_back)
    acts, gis, flat, small, grad_in, grad_back = backward_call(
        x, cot, h, gate, eo, dmg, ob, lse, q, k, v, kt, start, g1, g2, wc, w_query, w_key, w_value,
        w_out, factors, w_in, w_back,
    )
    flat = flat.reshape(width // (2 * HEAD_DIM), 4, 2 * HEAD_DIM, width)
    one = lambda n: flat[:, n].reshape(width, width).astype(F32)
    ctrl = jnp.sum(small[: experts * per].reshape(experts, per, width), axis=1).T
    return (
        acts, gis, small[experts * per + 8], one(0).T, one(1).T, one(2).T, one(3),
        small[experts * per], ctrl, grad_in.astype(F32), grad_back.astype(F32),
    )


def solution(mesh):
    data = P(None, "dp", "blk", None)
    in_specs = (data, P("dp", "blk")) + (P(),) * 9 + (data,)
    out_specs = (data, data) + (P(),) * 9
    return jax.shard_map(local, mesh=mesh, in_specs=in_specs, out_specs=out_specs, check_vma=False)
```

```python
import functools

import jax
import jax.numpy as jnp
from jax import lax
from jax.experimental import pallas as pl
from jax.experimental.pallas import tpu as pltpu
from jax.sharding import PartitionSpec as P

HEAD_DIM = 64
GROUP = 32
EPSILON = 1e-05
BLOCK = 256
CHUNK = 512
SCALE = 0.125
MASKED = -1e30
VMEM_LIMIT = 60 * 1024 * 1024
BF = jnp.bfloat16
F32 = jnp.float32
MESH = pl.DeviceIdType.MESH


def dot(a, b, ca, cb):
    return lax.dot_general(a, b, (((ca,), (cb,)), ((), ())), preferred_element_type=F32)


def nn(a, b):
    return dot(a, b, 1, 0)


def nt(a, b):
    return dot(a, b, 1, 1)


def tn(a, b):
    return dot(a, b, 0, 0)


def key_range(packed, i):
    low = max(0, i * BLOCK - BLOCK - BLOCK // 2) if packed else 0
    return low, (i + 1) * BLOCK - low


def head_masks():
    lane = lax.broadcasted_iota(jnp.int32, (1, 2 * HEAD_DIM), 1)
    first = (lane < HEAD_DIM).astype(F32).astype(BF)
    return first, (lane >= HEAD_DIM).astype(F32).astype(BF)


def group_match(rows, tokens):
    row = lax.broadcasted_iota(jnp.int32, (rows, tokens), 0)
    col = lax.broadcasted_iota(jnp.int32, (rows, tokens), 1)
    return (row % (tokens // GROUP)) == (col // GROUP)


def fill_bias(bias_ref, start_ref, packed, i):
    low, count = key_range(packed, i)
    q_pos = i * BLOCK + lax.broadcasted_iota(jnp.int32, (1, BLOCK), 1)
    if packed:
        k_pos = low + lax.broadcasted_iota(jnp.int32, (count, BLOCK), 0)
        allowed = (k_pos <= q_pos) & (k_pos >= start_ref[...])
        bias_ref[0:count, :] = jnp.where(allowed, 0.0, MASKED)
    else:
        k_pos = i * BLOCK + lax.broadcasted_iota(jnp.int32, (BLOCK, BLOCK), 0)
        bias_ref[0:BLOCK, :] = jnp.where(k_pos <= q_pos, 0.0, MASKED)


def add_bias(scores, bias_ref, packed, count):
    if packed:
        return scores + bias_ref[0:count, :]
    last = scores[count - BLOCK :, :] + bias_ref[0:BLOCK, :]
    if count == BLOCK:
        return last
    return jnp.concatenate([scores[: count - BLOCK, :], last], axis=0)


def rms(values):
    return lax.rsqrt(jnp.mean(values * values, axis=-1, keepdims=True) + EPSILON)


def peer(axis, me, d):
    return {axis: me ^ d}


def arrive(partners):
    barrier = pltpu.get_barrier_semaphore()
    for p in partners:
        pl.semaphore_signal(barrier, inc=1, device_id=p, device_id_type=MESH)
    pl.semaphore_wait(barrier, len(partners))


def remote(src, dst, sems, k, where):
    return pltpu.make_async_remote_copy(
        src_ref=src, dst_ref=dst, send_sem=sems[0].at[k], recv_sem=sems[1].at[k],
        device_id=where, device_id_type=MESH,
    )


class Exchange:
    def __init__(self, nb, src, dst, own, sems, base):
        self.nb, self.src, self.dst, self.own, self.sems, self.base = nb, src, dst, own, sems, base
        self.me = lax.axis_index("blk")

    def local(self):
        return pltpu.make_async_copy(
            self.src.at[self.me], self.dst.at[self.me], self.own.at[self.base]
        )

    def copy(self, d):
        return remote(
            self.src.at[self.me ^ d], self.dst.at[self.me], self.sems,
            self.base * (self.nb - 1) + d - 1, peer("blk", self.me, d),
        )

    def start(self):
        self.local().start()
        for d in range(1, self.nb):
            self.copy(d).start()

    def wait(self):
        self.local().wait()
        for d in range(1, self.nb):
            self.copy(d).wait()


def unit(n):
    row = lax.broadcasted_iota(jnp.int32, (n, n), 0)
    col = lax.broadcasted_iota(jnp.int32, (n, n), 1)
    return (row == col).astype(F32).astype(BF)


def split_three(a):
    high = a.astype(BF)
    rest = a - high.astype(F32)
    mid = rest.astype(BF)
    return [high, mid, (rest - mid.astype(F32)).astype(BF)]


def head_rows(heads, width):
    row = lax.broadcasted_iota(jnp.int32, (heads, width), 0)
    col = lax.broadcasted_iota(jnp.int32, (heads, width), 1)
    return (row == col // HEAD_DIM).astype(F32).astype(BF)


def forward_kernel(micros, blocks, nb, x_src, seg_src, cot_src, g1_ref, wq_ref, wk_ref, wv_ref, wo_ref,
                   g2_ref, wc_ref, q_ref, k_ref, v_ref, kt_ref, ob_ref, lse_ref, h_ref, gate_ref,
                   mg_ref, start_ref, x_out, cot_out, x_all, seg_all, bias, o_acc, sums, eye, own,
                   send_sem, recv_sem):
    sems = (send_sem, recv_sem)
    now = pl.program_id(0)
    span = 2 * blocks
    micro, step = now // span, now % span
    width = wo_ref.shape[0]
    pairs = width // (2 * HEAD_DIM)
    me = lax.axis_index("blk")
    xs = [Exchange(nb, x_src.at[m], x_all.at[m], own, sems, m) for m in range(micros)]
    segs = Exchange(nb, seg_src, seg_all, own, sems, micros)
    cots = [
        Exchange(nb, cot_src.at[m], cot_out.at[m], own, sems, micros + 1 + m) for m in range(micros)
    ]
    keep = pltpu.make_async_copy(x_all, x_out, own.at[2 * micros + 1])

    @pl.when(now == 0)
    def _():
        xs[0].local().start()
        eye[...] = unit(width)
        arrive([peer("blk", me, d) for d in range(1, nb)])
        for d in range(1, nb):
            xs[0].copy(d).start()

    @pl.when(step < blocks)
    def _():
        block = me ^ step
        for m in range(micros):
            pl.when((micro == m) & (step == 0))(xs[m].local().wait)
            for d in range(1, nb):
                pl.when((micro == m) & (step == d))(xs[m].copy(d).wait_recv)
        x = x_all[micro, block].astype(F32)
        n1 = (x * rms(x) * g1_ref[...]).astype(BF)
        at = pl.ds(pl.multiple_of(block * BLOCK, BLOCK), BLOCK)
        q_ref[0, at, :] = nn(n1, wq_ref[...]).astype(BF)
        k = nn(n1, wk_ref[...]).astype(BF)
        k_ref[0, at, :] = k
        v_ref[0, at, :] = nn(n1, wv_ref[...]).astype(BF)
        kt_ref[0, :, at] = nt(eye[...], k).astype(BF)

    @pl.when(now == nb - 1)
    def _():
        segs.start()
        for m in range(1, micros):
            xs[m].start()

    @pl.when(now == blocks)
    def _():
        for c in cots:
            c.start()

    @pl.when(now == span)
    def _():
        segs.wait()
        counts = [
            jnp.sum(jnp.sum((seg_all[...] < d).astype(F32), axis=0), keepdims=True)
            for d in range(1, nb * seg_all.shape[1] * seg_all.shape[2] // BLOCK)
        ]
        for b in range(blocks):
            seg = jnp.concatenate([seg_all[b, n : n + 1, :] for n in range(seg_all.shape[1])], axis=1)
            start = jnp.zeros(seg.shape, F32)
            for d, count in enumerate(counts):
                start = jnp.where(seg == d + 1, count, start)
            start_ref[b] = start.astype(jnp.int32)

    masks = head_masks()

    def attend(packed, i):
        low, count = key_range(packed, i)
        fill_bias(bias, start_ref[i], packed, i)
        for hp in range(pairs):
            lanes = slice(hp * 2 * HEAD_DIM, (hp + 1) * 2 * HEAD_DIM)
            q_pair = q_ref[0, i * BLOCK : (i + 1) * BLOCK, lanes]
            k_pair = k_ref[0, low : low + count, lanes]
            v_pair = v_ref[0, low : low + count, lanes]
            o_pair = None
            for h in range(2):
                scores = add_bias(nt(k_pair, q_pair * masks[h]), bias, packed, count)
                top = jnp.max(scores, axis=0, keepdims=True)
                p = jnp.exp((scores - top) * SCALE)
                total = jnp.sum(p, axis=0, keepdims=True)
                o = tn(p.astype(BF), v_pair * masks[h])
                o_pair = o if o_pair is None else o_pair + o
                sums[hp * 2 + h : hp * 2 + h + 1, :] = 1.0 / total
                lse_ref[0, hp * 2 + h : hp * 2 + h + 1, :] = top * SCALE + jnp.log(total)
            o_acc[:, lanes] = o_pair

    for m in range(micros):
        for i in range(blocks):
            pl.when(now == m * span + blocks + i)(functools.partial(attend, m > 0, i))

    @pl.when(step >= blocks)
    def _():
        heads = head_rows(sums.shape[0], width)
        scale = tn(
            jnp.concatenate(split_three(sums[...]), axis=0), jnp.concatenate([heads] * 3, axis=0)
        )
        ob = (o_acc[...] * scale).astype(BF)
        ob_ref[0] = ob
        h = x_all[micro, step - blocks].astype(F32) + nn(ob, wo_ref[...])
        h_ref[0] = h
        n2 = (h * rms(h) * g2_ref[...]).astype(BF)
        logits = nt(wc_ref[...], n2)
        rows = logits.shape[0]
        match = group_match(rows, BLOCK)
        logits = jnp.where(match, logits, MASKED)
        e = jnp.where(match, jnp.exp(logits - jnp.max(logits, axis=1, keepdims=True)), 0.0)
        gate = e / jnp.sum(e, axis=1, keepdims=True)
        gate_ref[...] = gate
        mg = nn(gate.astype(BF), n2).astype(BF).astype(F32)
        half = rows // mg_ref.shape[0]
        for j in range(mg_ref.shape[0]):
            mg_ref[j] = mg[j * half : (j + 1) * half]

    @pl.when(now == span + nb)
    def _():
        keep.start()

    @pl.when(now == micros * span - 1)
    def _():
        keep.wait()
        for x in xs:
            for d in range(1, nb):
                x.copy(d).wait_send()
        for c in cots:
            c.wait()


def gelu_both(u):
    c = 0.7978845608028654
    t = jnp.tanh(c * (u + 0.044715 * (u * u * u)))
    act = 0.5 * u * (1.0 + t)
    slope = 0.5 * (1.0 + t) + 0.5 * u * (1.0 - t * t) * (c * (1.0 + 3 * 0.044715 * (u * u)))
    return act, slope


def same_plane(far, d):
    return {"dp": lax.axis_index("dp") ^ far, "blk": lax.axis_index("blk") ^ d}


def plane_steps(nb):
    return [(far, d) for far in (0, 1) for d in range(0, nb, 2) if far or d]


def experts_kernel(micros, blocks, nb, *refs):
    mg_ref, gate_ref, cot_ref, win_ref, wback_ref = refs[:5]
    eo_ref, dmg_ref, all_ref, factors, gathered, send_sem, recv_sem = refs[5:]
    sems = (send_sem, recv_sem)
    e, c = pl.program_id(0), pl.program_id(1)
    at = e * pl.num_programs(1) + c
    last = pl.num_programs(0) * pl.num_programs(1) - 1
    per = BLOCK // GROUP
    n_exp = factors.shape[0]
    groups = micros * blocks * per
    blk = lax.axis_index("blk")
    kind = blk % n_exp
    steps = [(far, d) for far in (0, 1) for d in range(nb) if far or d]

    def plane_copy(n):
        far, d = steps[n]
        return remote(factors.at[kind ^ (d & 1)], gathered.at[n], sems, n, same_plane(far, d))

    @pl.when(at == 0)
    def _():
        deo = []
        for m in range(micros):
            for i in range(blocks):
                at_rows = (m * blocks + i) * BLOCK
                deo.append(nn(gate_ref[:, at_rows : at_rows + BLOCK].astype(BF), cot_ref[m, i]))
        for j in range(n_exp):
            factors[j, 0] = mg_ref[j].astype(BF)
            factors[j, 1] = jnp.concatenate(
                [d[j * per : (j + 1) * per] for d in deo], axis=0
            ).astype(BF)
        arrive([same_plane(*s) for s in steps])
        for n in range(len(steps)):
            plane_copy(n).start()

    mg, deo = factors[e, 0], factors[e, 1]
    act, slope = gelu_both(nn(mg, win_ref[0]))
    eo_part = nn(act.astype(BF), wback_ref[0])
    du = (slope * nt(deo, wback_ref[0])).astype(BF)
    dmg_part = nt(du, win_ref[0])

    @pl.when(c == 0)
    def _():
        eo_ref[0] = eo_part
        dmg_ref[0] = dmg_part

    @pl.when(c > 0)
    def _():
        eo_ref[0] += eo_part
        dmg_ref[0] += dmg_part

    @pl.when(at == last)
    def _():
        for n in range(len(steps)):
            plane_copy(n).wait()
        for n in range(len(steps) + 1):
            piece = factors[kind] if n == 0 else gathered[n - 1]
            for f in range(2):
                all_ref[f, n * groups : (n + 1) * groups, :] = piece[f]


class Return:
    def __init__(self, nb, buf, out, own, sems, base):
        self.nb, self.buf, self.out, self.own, self.sems, self.base = nb, buf, out, own, sems, base
        self.me = lax.axis_index("blk")

    def local(self):
        return pltpu.make_async_copy(
            self.buf.at[self.me], self.out.at[self.me], self.own.at[self.base]
        )

    def copy(self, d):
        return remote(
            self.buf.at[self.me ^ d], self.out.at[self.me], self.sems,
            self.base * (self.nb - 1) + d - 1, peer("blk", self.me, d),
        )

    def start(self, i):
        pl.when(i == self.me)(lambda: self.local().start())
        for d in range(1, self.nb):
            pl.when(i == (self.me ^ d))(lambda d=d: self.copy(d).start())

    def wait(self):
        self.local().wait()
        for d in range(1, self.nb):
            self.copy(d).wait()


class Plan:
    def __init__(self, sems):
        self.sems, self.count, self.sets = sems, 0, {}

    def add(self, name, makers):
        self.sets[name] = list(enumerate(makers, self.count))
        self.count += len(makers)

    def each(self, name):
        for k, maker in self.sets[name]:
            src, dst, where = maker()
            yield remote(src, dst, self.sems, k, where)

    def start(self, name):
        for c in self.each(name):
            c.start()

    def arrived(self, name):
        for c in self.each(name):
            c.wait_recv()

    def sent(self, name):
        for c in self.each(name):
            c.wait_send()


def other_plane(d):
    return {"dp": lax.axis_index("dp") ^ (2 * d)}


def pair_sum(parts):
    while len(parts) > 1:
        parts = [parts[n] + parts[n + 1] for n in range(0, len(parts), 2)]
    return parts[0]


def rows_of(n, size):
    return pl.ds(pl.multiple_of(n * size, size), size)


def backward_kernel(micros, blocks, nb, planes, x_ref, cot_ref, h_ref, gate_ref, eo_ref, dmg_ref, ob_ref,
                    lse_ref, q_ref, k_ref, v_ref, kt_ref, start_ref, g1_ref, g2_ref, wc_ref, wq_ref,
                    wk_ref, wv_ref, wo_ref, factors, win_hbm, wback_hbm, act_ref, gi_ref, flat_ref,
                    small_ref, gin, gback, dh_all, n1_all, dob, delta, dq_all, dk_all, dv_all, dk_acc,
                    dv_acc, gacc, go_acc, bias, act_buf, gi_buf, win, wback, ours, theirs, piece, s1,
                    r1, s2, r2, s3, r3, fl, small, few, rs, own, load_sem, ret_send, ret_recv, send_sem,
                    recv_sem):
    now = pl.program_id(0)
    width = wo_ref.shape[0]
    pairs = width // (2 * HEAD_DIM)
    pair_lanes = 2 * HEAD_DIM
    span = 2 * blocks + pairs
    micro, step = now // span, now % span
    last = (micros - 1) * span
    blk, dp = lax.axis_index("blk"), lax.axis_index("dp")
    kind, plane = blk % 2, dp // 2
    steps = plane_steps(nb)
    members = len(steps) + 1
    core = lambda: peer("blk", lax.axis_index("blk"), 1)

    def part_of(far, d):
        return ((blk ^ d) // 2) + (nb // 2) * ((dp % 2) ^ far)

    part = part_of(0, 0)
    cut = win.shape[1]
    rets = (ret_send, ret_recv)
    acts = [Return(nb, act_buf.at[m], act_ref.at[m], own, rets, 2 * m) for m in range(micros)]
    gis = [Return(nb, gi_buf.at[m], gi_ref.at[m], own, rets, 2 * m + 1) for m in range(micros)]
    columns = rows_of(part, cut)
    loads = [
        lambda: pltpu.make_async_copy(win_hbm.at[kind, :, columns], win, load_sem.at[0]),
        lambda: pltpu.make_async_copy(wback_hbm.at[kind, columns, :], wback, load_sem.at[1]),
    ]
    rows = width // planes

    def window(which, p, z):
        if which == 0:
            return gin.at[kind, rows_of(z, rows), rows_of(p, cut)]
        at = pl.multiple_of(p * cut + z * rows, rows)
        return gback.at[kind, pl.ds(at, rows), :]

    def slab(which, p):
        if which == 0:
            return gin.at[kind, :, rows_of(p, cut)]
        return gback.at[kind, rows_of(p, cut), :]

    mine = [
        lambda w=w: pltpu.make_async_copy(piece.at[w], window(w, part, plane), load_sem.at[2 + w])
        for w in range(2)
    ]
    y_peer, x_peer = steps[0], steps[1]
    others = range(1, planes)
    both = range(2)
    plan = Plan((send_sem, recv_sem))
    for w in both:
        plan.add(f"rs{w}", [
            lambda d=d, w=w: (ours.at[w, plane ^ d], theirs.at[w, d - 1], other_plane(d)) for d in others
        ])
        plan.add(f"z{w}", [
            lambda d=d, w=w: (piece.at[w], window(w, part, plane), other_plane(d)) for d in others
        ])
        for name, to in ((f"y0{w}", y_peer), (f"x0{w}", x_peer)):
            plan.add(name, [
                lambda w=w, to=to: (piece.at[w], window(w, part, plane), same_plane(*to))
            ])

    def onward(p, z, w, to):
        return window(w, p, z), window(w, p, z), same_plane(*to)

    part_y = part_of(*y_peer)
    for w in both:
        plan.add(f"yx0{w}", [lambda w=w: onward(part_y, plane, w, x_peer)])
        for name, p, to in ((f"y1{w}", part, y_peer), (f"x1{w}", part, x_peer), (f"yx1{w}", part_y, x_peer)):
            plan.add(name, [
                lambda d=d, w=w, p=p, to=to: onward(p, plane ^ d, w, to) for d in others
            ])
        for name, p in zip("oyxd", [part] + [part_of(*t) for t in steps]):
            plan.add(f"c{name}{w}", [lambda w=w, p=p: (slab(w, p), slab(w, p), core())])

    sizes = [width] + [3 * pair_lanes] * pairs
    halves = [n // 2 for n in sizes]
    quarters = [n // 2 // members for n in sizes]

    def held_sum(c):
        return go_acc if c == 0 else gacc.at[c - 1]

    def quarter_at(c, p):
        at = pl.multiple_of(kind * halves[c] + p * quarters[c], quarters[c])
        return pl.ds(at, quarters[c])

    for c in range(pairs + 1):
        n_half, n_quarter = halves[c], quarters[c]
        plan.add(f"ha{c}", [lambda c=c, r=n_half: (s1.at[c, 0:r], r1.at[c, 0:r], core())])
        plan.add(f"hb{c}", [
            lambda c=c, n=n, r=n_quarter: (s2.at[c, n, 0:r], r2.at[c, n, 0:r], same_plane(*steps[n]))
            for n in range(members - 1)
        ])
        plan.add(f"hz{c}", [
            lambda c=c, d=d, r=n_quarter: (s3.at[c, 0:r], r3.at[c, d - 1, 0:r], other_plane(d))
            for d in others
        ])

        def share(c, n):
            ref = fl.at[c, quarter_at(c, part), :]
            return ref, ref, same_plane(*steps[n])

        def side(c):
            ref = fl.at[c, rows_of(kind, halves[c]), :]
            return ref, ref, core()

        plan.add(f"hg{c}", [lambda c=c, n=n: share(c, n) for n in range(members - 1)])
        plan.add(f"hh{c}", [lambda c=c: side(c)])
    near = [(far, d) for far in (0, 1) for d in range(nb) if far or d]
    plan.add("sb", [lambda n=n: (few.at[0], rs.at[n], same_plane(*near[n])) for n in range(len(near))])
    plan.add("sz", [lambda d=d: (few.at[1], rs.at[len(near) + d - 1], other_plane(d)) for d in others])
    assert plan.count <= send_sem.shape[0]

    def chunk_start(c):
        s1[c, 0 : halves[c]] = held_sum(c)[rows_of(1 - kind, halves[c]), :].astype(BF)
        plan.start(f"ha{c}")

    def chunk_b(c):
        plan.arrived(f"ha{c}")
        at = rows_of(kind, halves[c])
        ref = held_sum(c)
        ref[at, :] = ref[at, :] + r1[c, 0 : halves[c]].astype(F32)
        for n, to in enumerate(steps):
            s2[c, n, 0 : quarters[c]] = ref[quarter_at(c, part_of(*to)), :].astype(BF)
        plan.start(f"hb{c}")

    def chunk_z(c):
        plan.arrived(f"hb{c}")
        r = quarters[c]
        total = pair_sum(
            [held_sum(c)[quarter_at(c, part), :]] + [r2[c, n, 0:r].astype(F32) for n in range(members - 1)]
        )
        s3[c, 0:r] = total.astype(BF)
        plan.start(f"hz{c}")

    def chunk_g(c):
        plan.arrived(f"hz{c}")
        r = quarters[c]
        total = pair_sum([s3[c, 0:r].astype(F32)] + [r3[c, d - 1, 0:r].astype(F32) for d in others])
        fl[c, quarter_at(c, part), :] = total.astype(BF)
        plan.start(f"hg{c}")

    def chunk_h(c):
        plan.arrived(f"hg{c}")
        plan.start(f"hh{c}")

    def out_copy(c):
        return pltpu.make_async_copy(fl.at[c], flat_ref.at[c], load_sem.at[4 + c])

    def chunk_done(c):
        plan.arrived(f"hh{c}")
        out_copy(c).start()

    def reduced(w):
        plan.arrived(f"rs{w}")
        total = pair_sum([ours[w, plane].astype(F32)] + [theirs[w, d - 1].astype(F32) for d in others])
        piece[w] = total.astype(BF)
        mine[w]().start()
        for name in ("z", "y0", "x0"):
            plan.start(f"{name}{w}")

    def own_y(w):
        plan.arrived(f"y0{w}")
        plan.start(f"yx0{w}")

    def whole_slice(w):
        mine[w]().wait()
        plan.arrived(f"z{w}")
        for name in ("y1", "x1", "co"):
            plan.start(f"{name}{w}")

    def slice_y(w):
        plan.arrived(f"y1{w}")
        for name in ("yx1", "cy"):
            plan.start(f"{name}{w}")

    def slice_x(w):
        plan.arrived(f"x0{w}")
        plan.arrived(f"x1{w}")
        plan.start(f"cx{w}")

    def slice_d(w):
        plan.arrived(f"yx0{w}")
        plan.arrived(f"yx1{w}")
        plan.start(f"cd{w}")

    stages = [chunk_start, chunk_b, chunk_z, chunk_g, chunk_h, chunk_done]

    @pl.when(now == 0)
    def _():
        for c in loads:
            c().start()
        partners = [peer("blk", blk, d) for d in range(1, nb)]
        partners += [same_plane(1, d) for d in range(nb)] + [other_plane(d) for d in others]
        arrive(partners)
        small[...] = jnp.zeros_like(small)
        go_acc[...] = jnp.zeros_like(go_acc)
        fill_bias(bias.at[0], None, False, 0)
        for c in loads:
            c().wait()
        mg, deo = factors[0], factors[1]
        act, slope = gelu_both(nn(mg, win[...]))
        du = (slope * nt(deo, wback[...])).astype(BF)
        g_in = tn(mg, du).astype(BF)
        for n in range(planes):
            ours[0, n] = g_in[n * rows : (n + 1) * rows]
        plan.start("rs0")
        g_back = tn(act.astype(BF), deo).astype(BF)
        for n in range(planes):
            ours[1, n] = g_back[n * rows : (n + 1) * rows]

    gate_rows = gate_ref.shape[0]

    @pl.when(step < blocks)
    def _():
        at = rows_of(step, BLOCK)
        h = h_ref[0]
        cot_b = cot_ref[0, 0]
        dout = cot_b.astype(F32)
        r2_ = rms(h)
        z = h * r2_
        n2 = (z * g2_ref[...]).astype(BF)
        gate = gate_ref[...]
        gate_b = gate.astype(BF)
        gate_low = (gate - gate_b.astype(F32)).astype(BF)
        eo = jnp.concatenate([eo_ref[j] for j in range(eo_ref.shape[0])], axis=0)
        dmg = jnp.concatenate([dmg_ref[j] for j in range(dmg_ref.shape[0])], axis=0).astype(BF)
        eo_b = eo.astype(BF)
        eo_low = (eo - eo_b.astype(F32)).astype(BF)
        mixed = tn(
            jnp.concatenate([gate_b, gate_low, gate_b], axis=0),
            jnp.concatenate([eo_b, eo_b, eo_low], axis=0),
        )
        act_buf[micro, step] = (h + mixed).astype(BF)
        for m in range(micros):
            pl.when(micro == m)(functools.partial(acts[m].start, step))
        dw2 = nt(jnp.concatenate([eo_b, eo_low], axis=0), cot_b)
        dw = dw2[:gate_rows] + dw2[gate_rows:] + nt(dmg, n2)
        wdw = gate * dw
        dlog = (wdw - gate * jnp.sum(wdw, axis=1, keepdims=True)).astype(BF)
        dn2 = tn(
            jnp.concatenate([gate_b, dlog], axis=0),
            jnp.concatenate([dmg, wc_ref[...]], axis=0),
        )
        small[0:gate_rows, :] += nn(dlog, n2)
        small[gate_rows : gate_rows + 1, :] += jnp.sum(dn2 * z, axis=0, keepdims=True)
        a = dn2 * g2_ref[...]
        dh = dout + r2_ * (a - z * jnp.mean(a * z, axis=-1, keepdims=True))
        dh_all[at, :] = dh
        da = dh.astype(BF)
        dob_b = nt(da, wo_ref[...]).astype(BF)
        dob[at, :] = dob_b
        ob = ob_ref[0]
        go_acc[...] += tn(ob, da)
        prod = dob_b.astype(F32) * ob.astype(F32)
        high = prod.astype(BF)
        low = (prod - high.astype(F32)).astype(BF)
        heads = head_rows(delta.shape[0], width)
        delta[:, at] = nt(heads, high) + nt(heads, low)
        x = x_ref[0, step].astype(F32)
        n1_all[at, :] = (x * rms(x) * g1_ref[...]).astype(BF)

    for m in range(1, micros):
        for i in range(blocks):
            pl.when(now == m * span + i)(
                functools.partial(fill_bias, bias.at[i], start_ref[i], True, i)
            )

    masks = head_masks()

    def attend(packed):
        hp = step - blocks
        lanes = rows_of(hp, pair_lanes)
        for i in range(blocks):
            low, count = key_range(packed, i)
            at = slice(i * BLOCK, (i + 1) * BLOCK)
            q_pair, dob_pair = q_ref[0, at, :], dob[at, lanes]
            k_pair, v_pair = k_ref[0, low : low + count, :], v_ref[0, low : low + count, :]
            dk_sum = dv_sum = None
            dqs = []
            for h in range(2):
                qm, dm = q_pair * masks[h], dob_pair * masks[h]
                scores = add_bias(nt(k_pair, qm), bias.at[i if packed else 0], packed, count)
                p = jnp.exp(scores * SCALE - lse_ref[0, pl.ds(hp * 2 + h, 1), at])
                dp_ = nt(v_pair, dm)
                ds = (p * (dp_ - delta[pl.ds(hp * 2 + h, 1), at])).astype(BF)
                kt = kt_ref[0, h * HEAD_DIM : (h + 1) * HEAD_DIM, low : low + count]
                dqs.append(nn(kt, ds) * SCALE)
                dk_part, dv_part = nn(ds, qm), nn(p.astype(BF), dm)
                dk_sum = dk_part if dk_sum is None else dk_sum + dk_part
                dv_sum = dv_part if dv_sum is None else dv_sum + dv_part
            old = i * BLOCK - low
            dk_acc[at, :] = dk_sum[old:]
            dv_acc[at, :] = dv_sum[old:]
            if old:
                dk_acc[low : i * BLOCK, :] += dk_sum[:old]
                dv_acc[low : i * BLOCK, :] += dv_sum[:old]
            dq_all[at, lanes] = jnp.concatenate(dqs, axis=0).T.astype(BF)
        dk = (dk_acc[...] * SCALE).astype(BF)
        dv = dv_acc[...].astype(BF)
        dk_all[:, lanes] = dk
        dv_all[:, lanes] = dv
        g = tn(jnp.concatenate([dq_all[:, lanes], dk, dv], axis=1), n1_all[...])
        if packed:
            gacc[hp] += g
        else:
            gacc[hp] = g

    for m in range(micros):
        in_phase = (micro == m) & (step >= blocks) & (step < blocks + pairs)
        pl.when(in_phase)(functools.partial(attend, m > 0))

    @pl.when(step >= blocks + pairs)
    def _():
        i = blk ^ (nb - 1 - (step - blocks - pairs))
        at = rows_of(i, BLOCK)
        x = x_ref[0, i].astype(F32)
        r1_ = rms(x)
        z1 = x * r1_
        dn1 = (
            nt(dq_all[at, :], wq_ref[...]) + nt(dk_all[at, :], wk_ref[...]) + nt(dv_all[at, :], wv_ref[...])
        )
        small[gate_rows + 8 : gate_rows + 9, :] += jnp.sum(dn1 * z1, axis=0, keepdims=True)
        b = dn1 * g1_ref[...]
        gi = dh_all[at, :] + r1_ * (b - z1 * jnp.mean(b * z1, axis=-1, keepdims=True))
        gi_buf[micro, i] = gi.astype(BF)
        for m in range(micros):
            pl.when(micro == m)(functools.partial(gis[m].start, i))

    final = micros * span - 1
    sums_from = last + blocks - 1
    tasks = {}

    def after(at, task, *args):
        tasks.setdefault(min(at, final), []).append(functools.partial(task, *args))

    def start_second():
        plan.start("rs1")

    after(blocks - 1, start_second)
    after(blocks, reduced, 0)
    after(blocks + pairs - 1, reduced, 1)
    after(blocks + pairs - 1, own_y, 0)
    after(last, whole_slice, 0)
    after(last, own_y, 1)
    after(last + blocks - 1, whole_slice, 1)
    after(last + blocks, slice_y, 0)
    after(last + blocks + 1, slice_x, 0)
    after(last + blocks + 2, slice_y, 1)
    after(last + blocks + 2, slice_x, 1)
    after(last + blocks + 3, slice_d, 0)
    for c in range(pairs):
        for n, stage in enumerate(stages):
            after(sums_from + c + n, stage, c)
    c = pairs
    after(sums_from + c, chunk_start, c)
    after(sums_from + c + 1, chunk_b, c)
    after(sums_from + c + 3, chunk_z, c)
    for at, todo in tasks.items():
        if at < final:

            @pl.when(now == at)
            def _(todo=todo):
                for task in todo:
                    task()

    @pl.when(now == final)
    def _():
        per = gate_rows // 2
        few[0] = jnp.concatenate(
            [jnp.sum(small[n * per : (n + 1) * per, :], axis=0, keepdims=True) for n in range(2)]
            + [small[gate_rows : gate_rows + 1, :], small[gate_rows + 8 : gate_rows + 9, :]]
            + [jnp.zeros((4, width), F32)],
            axis=0,
        )
        plan.start("sb")
        for task in tasks[final]:
            task()
        chunk_g(c)
        plan.arrived("sb")
        few[1] = pair_sum([few[0]] + [rs[n] for n in range(len(near))])
        plan.start("sz")
        chunk_h(c)
        slice_d(1)
        chunk_done(c)
        plan.arrived("sz")
        small_ref[...] = pair_sum([few[1]] + [rs[len(near) + d - 1] for d in others])
        for w in both:
            for name in "oyxd":
                plan.arrived(f"c{name}{w}")
        for n in range(pairs + 1):
            out_copy(n).wait()
        for name in plan.sets:
            plan.sent(name)
        for r in acts + gis:
            r.wait()


def whole(shape):
    return pl.BlockSpec(shape, lambda *_: (0,) * len(shape))


def held(shape):
    return pl.BlockSpec(shape, lambda *_: (0,) * len(shape), pipeline_mode=pl.Buffered(1))


ANY = pl.BlockSpec(memory_space=pl.ANY)
DMA = pltpu.SemaphoreType.DMA


def shaped(shape, dtype):
    return jax.ShapeDtypeStruct(shape, dtype)


def params(number):
    return pltpu.CompilerParams(
        vmem_limit_bytes=VMEM_LIMIT, collective_id=number, has_side_effects=True
    )


def forward_call(x, seg, cot, g1, wq, wk, wv, wo, g2, wc):
    nb = lax.axis_size("blk")
    micros, _, rows_in, width = x.shape
    length = nb * rows_in
    blocks = length // BLOCK
    assert x.shape[1] == nb and rows_in == BLOCK
    rows = wc.shape[0]
    heads = width // HEAD_DIM
    per = BLOCK // GROUP
    experts = rows // per
    span = 2 * blocks
    phase = lambda s: jnp.maximum(s % span - blocks, 0)
    whole_micro = lambda a, b: pl.BlockSpec((1, a, b), lambda s: (s // span, 0, 0))
    flat = lambda s: (s // span) * blocks + phase(s)
    moves = 2 * micros + 1
    return pl.pallas_call(
        functools.partial(forward_kernel, micros, blocks, nb),
        grid=(micros * span,),
        in_specs=[ANY, ANY, ANY] + [held(a.shape) for a in (g1, wq, wk, wv, wo, g2, wc)],
        out_specs=[
            whole_micro(length, width), whole_micro(length, width), whole_micro(length, width),
            whole_micro(width, length),
            pl.BlockSpec((1, BLOCK, width), lambda s: (s // span, phase(s), 0)),
            pl.BlockSpec((1, heads, BLOCK), lambda s: (s // span, 0, phase(s))),
            pl.BlockSpec((1, BLOCK, width), lambda s: (s // span, phase(s), 0)),
            pl.BlockSpec((rows, BLOCK), lambda s: (0, flat(s))),
            pl.BlockSpec((experts, per, width), lambda s: (0, flat(s), 0)),
            whole((blocks, 1, BLOCK)), ANY, ANY,
        ],
        out_shape=[
            shaped((micros, length, width), BF), shaped((micros, length, width), BF),
            shaped((micros, length, width), BF), shaped((micros, width, length), BF),
            shaped((micros, length, width), BF), shaped((micros, heads, length), F32),
            shaped((micros, length, width), F32), shaped((rows, micros * length), F32),
            shaped((experts, micros * length // GROUP, width), F32),
            shaped((blocks, 1, BLOCK), jnp.int32), shaped(x.shape, BF), shaped(x.shape, BF),
        ],
        scratch_shapes=[
            pltpu.VMEM(x.shape, BF), pltpu.VMEM(seg.shape, seg.dtype),
            pltpu.VMEM((length, BLOCK), F32), pltpu.VMEM((BLOCK, width), F32),
            pltpu.VMEM((heads, BLOCK), F32), pltpu.VMEM((width, width), BF),
            DMA((moves + 1,)), DMA((moves * (nb - 1),)), DMA((moves * (nb - 1),)),
        ],
        compiler_params=params(1),
        name="attention_forward",
    )(x, seg, cot, g1, wq, wk, wv, wo, g2, wc)


def experts_call(mg, gate, cot, w_in, w_back):
    micros, nb, _, width = cot.shape
    experts, groups, _ = mg.shape
    ff = w_in.shape[2]
    blocks = gate.shape[1] // BLOCK // micros
    chunk = min(CHUNK, ff)
    by_expert = lambda n: pl.BlockSpec((1, n, width), lambda e, c: (e, 0, 0))
    members = 2 * nb
    return pl.pallas_call(
        functools.partial(experts_kernel, micros, blocks, nb),
        grid=(experts, ff // chunk),
        in_specs=[
            held(mg.shape), held(gate.shape), held(cot.shape),
            pl.BlockSpec((1, width, chunk), lambda e, c: (e, 0, c)),
            pl.BlockSpec((1, chunk, width), lambda e, c: (e, c, 0)),
        ],
        out_specs=[by_expert(groups)] * 2 + [whole((2, members * groups, width))],
        out_shape=[shaped((experts, groups, width), F32)] * 2
        + [shaped((2, members * groups, width), BF)],
        scratch_shapes=[
            pltpu.VMEM((experts, 2, groups, width), BF),
            pltpu.VMEM((members - 1, 2, groups, width), BF), DMA((members - 1,)), DMA((members - 1,)),
        ],
        compiler_params=params(2),
        name="experts",
    )(mg, gate, cot, w_in, w_back)


def backward_call(x, cot, h, gate, eo, dmg, ob, lse, q, k, v, kt, start, g1, g2, wc, wq, wk, wv, wo,
                  factors, w_in, w_back):
    micros, nb, _, width = x.shape
    planes = lax.axis_size("dp") // 2
    length = q.shape[1]
    blocks = length // BLOCK
    rows = wc.shape[0]
    per = BLOCK // GROUP
    experts = rows // per
    heads = width // HEAD_DIM
    pairs = heads // 2
    ff = w_in.shape[2]
    cut = ff // nb
    assert cut == width
    members = len(plane_steps(nb)) + 1
    span = 2 * blocks + pairs
    m_of = lambda s: s // span
    early = lambda s: jnp.minimum(s % span, blocks - 1)
    pair_of = lambda s: jnp.clip(s % span - blocks, 0, pairs - 1)

    flat = lambda s: m_of(s) * blocks + early(s)
    row_block = pl.BlockSpec((1, BLOCK, width), lambda s: (m_of(s), early(s), 0))
    group_block = pl.BlockSpec((experts, per, width), lambda s: (0, flat(s), 0))
    pair_block = pl.BlockSpec((1, length, 2 * HEAD_DIM), lambda s: (m_of(s), 0, pair_of(s)))
    piece = (2, width // planes, cut)
    chunk = width
    chunks = pairs + 1
    half = chunk // 2
    quarter = half // members
    reach = max(key_range(True, i)[1] for i in range(blocks))
    small = (rows + 16, width)
    few = (8, width)
    vm = pltpu.VMEM
    copies = 96 + 16 * chunks + 32 * planes
    return pl.pallas_call(
        functools.partial(backward_kernel, micros, blocks, nb, planes),
        grid=(micros * span,),
        in_specs=[
            pl.BlockSpec((1, nb, BLOCK, width), lambda s: (m_of(s), 0, 0, 0)),
            pl.BlockSpec((1, 1, BLOCK, width), lambda s: (m_of(s), early(s), 0, 0)),
            row_block,
            pl.BlockSpec((rows, BLOCK), lambda s: (0, flat(s))),
            group_block, group_block, row_block,
            pl.BlockSpec((1, heads, length), lambda s: (m_of(s), 0, 0)),
            pair_block, pair_block, pair_block,
            pl.BlockSpec((1, 2 * HEAD_DIM, length), lambda s: (m_of(s), pair_of(s), 0)),
        ] + [held(a.shape) for a in (start, g1, g2, wc, wq, wk, wv, wo, factors)] + [ANY, ANY],
        out_specs=[ANY, ANY, ANY, whole(few), ANY, ANY],
        out_shape=[
            shaped(x.shape, BF), shaped(x.shape, BF), shaped((chunks, chunk, width), BF),
            shaped(few, F32), shaped(w_in.shape, BF), shaped(w_back.shape, BF),
        ],
        scratch_shapes=[
            vm((length, width), F32), vm((length, width), BF), vm((length, width), BF),
            vm((heads, length), F32), vm((length, width), BF), vm((length, width), BF),
            vm((length, width), BF), vm((length, 2 * HEAD_DIM), F32), vm((length, 2 * HEAD_DIM), F32),
            vm((pairs, 6 * HEAD_DIM, width), F32), vm((width, width), F32), vm((blocks, reach, BLOCK), F32),
            vm(x.shape, BF), vm(x.shape, BF), vm((width, cut), BF), vm((cut, width), BF),
            vm((2, planes) + piece[1:], BF), vm((2, planes - 1) + piece[1:], BF), vm(piece, BF),
            vm((chunks, half, width), BF), vm((chunks, half, width), BF),
            vm((chunks, members - 1, quarter, width), BF), vm((chunks, members - 1, quarter, width), BF),
            vm((chunks, quarter, width), BF), vm((chunks, planes - 1, quarter, width), BF),
            vm((chunks, chunk, width), BF), vm(small, F32), vm((2,) + few, F32),
            vm((2 * nb + planes - 2,) + few, F32),
            DMA((2 * micros,)), DMA((5 + pairs,)), DMA((2 * micros * (nb - 1),)),
            DMA((2 * micros * (nb - 1),)), DMA((copies,)), DMA((copies,)),
        ],
        compiler_params=params(3),
        name="attention_backward",
    )(x, cot, h, gate, eo, dmg, ob, lse, q, k, v, kt, start, g1, g2, wc, wq, wk, wv, wo, factors, w_in,
      w_back)


def local(block_input, segment_ids, gain_one, w_query, w_key, w_value, w_out, gain_two, w_ctrl,
          w_in, w_back, cotangent):
    micros, seqs, rows, width = block_input.shape
    experts, _, ff = w_in.shape
    nb = lax.axis_size("blk")
    per = BLOCK // GROUP
    g1, g2 = gain_one.reshape(1, width), gain_two.reshape(1, width)
    wc = jnp.repeat(w_ctrl.T, per, axis=0)
    seg = segment_ids.reshape(nb, 2, rows // 2)
    q, k, v, kt, ob, lse, h, gate, mg, start, x, cot = forward_call(
        block_input, seg, cotangent, g1, w_query, w_key, w_value, w_out, g2, wc
    )
    eo, dmg, factors = experts_call(mg, gate, cot, w_in, w_back)
    acts, gis, flat, small, grad_in, grad_back = backward_call(
        x, cot, h, gate, eo, dmg, ob, lse, q, k, v, kt, start, g1, g2, wc, w_query, w_key, w_value,
        w_out, factors, w_in, w_back,
    )
    lanes = 2 * HEAD_DIM
    one = lambda n: flat[1:, n * lanes : (n + 1) * lanes].reshape(width, width).astype(F32).T
    return (
        acts, gis, small[3], one(0), one(1), one(2), flat[0].astype(F32), small[2], small[:experts].T,
        grad_in.astype(F32), grad_back.astype(F32),
    )


def solution(mesh):
    data = P(None, "dp", "blk", None)
    in_specs = (data, P("dp", "blk")) + (P(),) * 9 + (data,)
    out_specs = (data, data) + (P(),) * 9
    return jax.shard_map(local, mesh=mesh, in_specs=in_specs, out_specs=out_specs, check_vma=False)
```

```python
import functools

import jax
import jax.numpy as jnp
from jax import lax
from jax.experimental import pallas as pl
from jax.experimental.pallas import tpu as pltpu
from jax.sharding import PartitionSpec as P

HEAD_DIM = 64
GROUP = 32
EPSILON = 1e-05
BLOCK = 256
CHUNK = 512
SCALE = 0.125
MASKED = -1e30
VMEM_LIMIT = 60 * 1024 * 1024
BF = jnp.bfloat16
F32 = jnp.float32
MESH = pl.DeviceIdType.MESH


def dot(a, b, ca, cb):
    return lax.dot_general(a, b, (((ca,), (cb,)), ((), ())), preferred_element_type=F32)


def nn(a, b):
    return dot(a, b, 1, 0)


def nt(a, b):
    return dot(a, b, 1, 1)


def tn(a, b):
    return dot(a, b, 0, 0)


def key_range(packed, i):
    low = max(0, i * BLOCK - BLOCK - BLOCK // 2) if packed else 0
    return low, (i + 1) * BLOCK - low


def head_masks():
    lane = lax.broadcasted_iota(jnp.int32, (1, 2 * HEAD_DIM), 1)
    first = (lane < HEAD_DIM).astype(F32).astype(BF)
    return first, (lane >= HEAD_DIM).astype(F32).astype(BF)


def group_match(rows, tokens):
    row = lax.broadcasted_iota(jnp.int32, (rows, tokens), 0)
    col = lax.broadcasted_iota(jnp.int32, (rows, tokens), 1)
    return (row % (tokens // GROUP)) == (col // GROUP)


def fill_bias(bias_ref, start_ref, packed, i):
    low, count = key_range(packed, i)
    q_pos = i * BLOCK + lax.broadcasted_iota(jnp.int32, (1, BLOCK), 1)
    if packed:
        k_pos = low + lax.broadcasted_iota(jnp.int32, (count, BLOCK), 0)
        allowed = (k_pos <= q_pos) & (k_pos >= start_ref[...])
        bias_ref[0:count, :] = jnp.where(allowed, 0.0, MASKED)
    else:
        k_pos = i * BLOCK + lax.broadcasted_iota(jnp.int32, (BLOCK, BLOCK), 0)
        bias_ref[0:BLOCK, :] = jnp.where(k_pos <= q_pos, 0.0, MASKED)


def add_bias(scores, bias_ref, packed, count):
    if packed:
        return scores + bias_ref[0:count, :]
    last = scores[count - BLOCK :, :] + bias_ref[0:BLOCK, :]
    if count == BLOCK:
        return last
    return jnp.concatenate([scores[: count - BLOCK, :], last], axis=0)


def rms(values):
    return lax.rsqrt(jnp.mean(values * values, axis=-1, keepdims=True) + EPSILON)


def peer(axis, me, d):
    return {axis: me ^ d}


def arrive(partners):
    barrier = pltpu.get_barrier_semaphore()
    for p in partners:
        pl.semaphore_signal(barrier, inc=1, device_id=p, device_id_type=MESH)
    pl.semaphore_wait(barrier, len(partners))


def remote(src, dst, sems, k, where):
    return pltpu.make_async_remote_copy(
        src_ref=src, dst_ref=dst, send_sem=sems[0].at[k], recv_sem=sems[1].at[k],
        device_id=where, device_id_type=MESH,
    )


class Exchange:
    def __init__(self, nb, src, dst, own, sems, base):
        self.nb, self.src, self.dst, self.own, self.sems, self.base = nb, src, dst, own, sems, base
        self.me = lax.axis_index("blk")

    def local(self):
        return pltpu.make_async_copy(
            self.src.at[self.me], self.dst.at[self.me], self.own.at[self.base]
        )

    def copy(self, d):
        return remote(
            self.src.at[self.me ^ d], self.dst.at[self.me], self.sems,
            self.base * (self.nb - 1) + d - 1, peer("blk", self.me, d),
        )

    def start(self):
        self.local().start()
        for d in range(1, self.nb):
            self.copy(d).start()

    def wait(self):
        self.local().wait()
        for d in range(1, self.nb):
            self.copy(d).wait()


def unit(n):
    row = lax.broadcasted_iota(jnp.int32, (n, n), 0)
    col = lax.broadcasted_iota(jnp.int32, (n, n), 1)
    return (row == col).astype(F32).astype(BF)


def split_three(a):
    high = a.astype(BF)
    rest = a - high.astype(F32)
    mid = rest.astype(BF)
    return [high, mid, (rest - mid.astype(F32)).astype(BF)]


def head_rows(heads, width):
    row = lax.broadcasted_iota(jnp.int32, (heads, width), 0)
    col = lax.broadcasted_iota(jnp.int32, (heads, width), 1)
    return (row == col // HEAD_DIM).astype(F32).astype(BF)


def forward_kernel(micros, blocks, nb, x_src, seg_src, cot_src, g1_ref, wq_ref, wk_ref, wv_ref, wo_ref,
                   g2_ref, wc_ref, q_ref, k_ref, v_ref, kt_ref, ob_ref, lse_ref, h_ref, gate_ref,
                   mg_ref, start_ref, x_out, cot_out, x_all, seg_all, bias, o_acc, sums, eye, own,
                   send_sem, recv_sem):
    sems = (send_sem, recv_sem)
    now = pl.program_id(0)
    span = 2 * blocks
    micro, step = now // span, now % span
    width = wo_ref.shape[0]
    pairs = width // (2 * HEAD_DIM)
    me = lax.axis_index("blk")
    xs = [Exchange(nb, x_src.at[m], x_all.at[m], own, sems, m) for m in range(micros)]
    segs = Exchange(nb, seg_src, seg_all, own, sems, micros)
    cots = [
        Exchange(nb, cot_src.at[m], cot_out.at[m], own, sems, micros + 1 + m) for m in range(micros)
    ]
    keep = pltpu.make_async_copy(x_all, x_out, own.at[2 * micros + 1])

    @pl.when(now == 0)
    def _():
        xs[0].local().start()
        eye[...] = unit(width)
        arrive([peer("blk", me, d) for d in range(1, nb)])
        for d in range(1, nb):
            xs[0].copy(d).start()

    @pl.when(step < blocks)
    def _():
        block = me ^ step
        for m in range(micros):
            pl.when((micro == m) & (step == 0))(xs[m].local().wait)
            for d in range(1, nb):
                pl.when((micro == m) & (step == d))(xs[m].copy(d).wait_recv)
        x = x_all[micro, block].astype(F32)
        n1 = (x * rms(x) * g1_ref[...]).astype(BF)
        at = pl.ds(pl.multiple_of(block * BLOCK, BLOCK), BLOCK)
        q_ref[0, at, :] = nn(n1, wq_ref[...]).astype(BF)
        k = nn(n1, wk_ref[...]).astype(BF)
        k_ref[0, at, :] = k
        v_ref[0, at, :] = nn(n1, wv_ref[...]).astype(BF)
        kt_ref[0, :, at] = nt(eye[...], k).astype(BF)

    @pl.when(now == nb - 1)
    def _():
        segs.start()
        for m in range(1, micros):
            xs[m].start()

    @pl.when(now == blocks)
    def _():
        for c in cots:
            c.start()

    @pl.when(now == span)
    def _():
        segs.wait()
        counts = [
            jnp.sum(jnp.sum((seg_all[...] < d).astype(F32), axis=0), keepdims=True)
            for d in range(1, nb * seg_all.shape[1] * seg_all.shape[2] // BLOCK)
        ]
        for b in range(blocks):
            seg = jnp.concatenate([seg_all[b, n : n + 1, :] for n in range(seg_all.shape[1])], axis=1)
            start = jnp.zeros(seg.shape, F32)
            for d, count in enumerate(counts):
                start = jnp.where(seg == d + 1, count, start)
            start_ref[b] = start.astype(jnp.int32)

    masks = head_masks()

    def attend(packed, i):
        low, count = key_range(packed, i)
        fill_bias(bias, start_ref[i], packed, i)
        for hp in range(pairs):
            lanes = slice(hp * 2 * HEAD_DIM, (hp + 1) * 2 * HEAD_DIM)
            q_pair = q_ref[0, i * BLOCK : (i + 1) * BLOCK, lanes]
            k_pair = k_ref[0, low : low + count, lanes]
            v_pair = v_ref[0, low : low + count, lanes]
            o_pair = None
            for h in range(2):
                scores = add_bias(nt(k_pair, q_pair * masks[h]), bias, packed, count)
                top = jnp.max(scores, axis=0, keepdims=True)
                p = jnp.exp((scores - top) * SCALE)
                total = jnp.sum(p, axis=0, keepdims=True)
                o = tn(p.astype(BF), v_pair * masks[h])
                o_pair = o if o_pair is None else o_pair + o
                sums[hp * 2 + h : hp * 2 + h + 1, :] = 1.0 / total
                lse_ref[0, hp * 2 + h : hp * 2 + h + 1, :] = top * SCALE + jnp.log(total)
            o_acc[:, lanes] = o_pair

    for m in range(micros):
        for i in range(blocks):
            pl.when(now == m * span + blocks + i)(functools.partial(attend, m > 0, i))

    @pl.when(step >= blocks)
    def _():
        heads = head_rows(sums.shape[0], width)
        scale = tn(
            jnp.concatenate(split_three(sums[...]), axis=0), jnp.concatenate([heads] * 3, axis=0)
        )
        ob = (o_acc[...] * scale).astype(BF)
        ob_ref[0] = ob
        h = x_all[micro, step - blocks].astype(F32) + nn(ob, wo_ref[...])
        h_ref[0] = h
        n2 = (h * rms(h) * g2_ref[...]).astype(BF)
        logits = nt(wc_ref[...], n2)
        rows = logits.shape[0]
        match = group_match(rows, BLOCK)
        logits = jnp.where(match, logits, MASKED)
        e = jnp.where(match, jnp.exp(logits - jnp.max(logits, axis=1, keepdims=True)), 0.0)
        gate = e / jnp.sum(e, axis=1, keepdims=True)
        gate_ref[...] = gate
        mg = nn(gate.astype(BF), n2).astype(BF).astype(F32)
        half = rows // mg_ref.shape[0]
        for j in range(mg_ref.shape[0]):
            mg_ref[j] = mg[j * half : (j + 1) * half]

    @pl.when(now == span + nb)
    def _():
        keep.start()

    @pl.when(now == micros * span - 1)
    def _():
        keep.wait()
        for x in xs:
            for d in range(1, nb):
                x.copy(d).wait_send()
        for c in cots:
            c.wait()


def gelu_both(u):
    c = 0.7978845608028654
    t = jnp.tanh(c * (u + 0.044715 * (u * u * u)))
    act = 0.5 * u * (1.0 + t)
    slope = 0.5 * (1.0 + t) + 0.5 * u * (1.0 - t * t) * (c * (1.0 + 3 * 0.044715 * (u * u)))
    return act, slope


def same_plane(far, d):
    return {"dp": lax.axis_index("dp") ^ far, "blk": lax.axis_index("blk") ^ d}


def plane_steps(nb):
    return [(far, d) for far in (0, 1) for d in range(0, nb, 2) if far or d]


def experts_kernel(micros, blocks, nb, *refs):
    mg_ref, gate_ref, cot_ref, win_ref, wback_ref = refs[:5]
    eo_ref, dmg_ref, all_ref, factors, gathered, send_sem, recv_sem = refs[5:]
    sems = (send_sem, recv_sem)
    e, c = pl.program_id(0), pl.program_id(1)
    at = e * pl.num_programs(1) + c
    last = pl.num_programs(0) * pl.num_programs(1) - 1
    per = BLOCK // GROUP
    n_exp = factors.shape[0]
    groups = micros * blocks * per
    blk = lax.axis_index("blk")
    kind = blk % n_exp
    steps = [(far, d) for far in (0, 1) for d in range(nb) if far or d]

    def plane_copy(n):
        far, d = steps[n]
        return remote(factors.at[kind ^ (d & 1)], gathered.at[n], sems, n, same_plane(far, d))

    @pl.when(at == 0)
    def _():
        deo = []
        for m in range(micros):
            for i in range(blocks):
                at_rows = (m * blocks + i) * BLOCK
                deo.append(nn(gate_ref[:, at_rows : at_rows + BLOCK].astype(BF), cot_ref[m, i]))
        for j in range(n_exp):
            factors[j, 0] = mg_ref[j].astype(BF)
            factors[j, 1] = jnp.concatenate(
                [d[j * per : (j + 1) * per] for d in deo], axis=0
            ).astype(BF)
        arrive([same_plane(*s) for s in steps])
        for n in range(len(steps)):
            plane_copy(n).start()

    mg, deo = factors[e, 0], factors[e, 1]
    act, slope = gelu_both(nn(mg, win_ref[0]))
    eo_part = nn(act.astype(BF), wback_ref[0])
    du = (slope * nt(deo, wback_ref[0])).astype(BF)
    dmg_part = nt(du, win_ref[0])

    @pl.when(c == 0)
    def _():
        eo_ref[0] = eo_part
        dmg_ref[0] = dmg_part

    @pl.when(c > 0)
    def _():
        eo_ref[0] += eo_part
        dmg_ref[0] += dmg_part

    @pl.when(at == last)
    def _():
        for n in range(len(steps)):
            plane_copy(n).wait()
        for n in range(len(steps) + 1):
            piece = factors[kind] if n == 0 else gathered[n - 1]
            for f in range(2):
                all_ref[f, n * groups : (n + 1) * groups, :] = piece[f]


class Return:
    def __init__(self, nb, buf, out, own, sems, base):
        self.nb, self.buf, self.out, self.own, self.sems, self.base = nb, buf, out, own, sems, base
        self.me = lax.axis_index("blk")

    def local(self):
        return pltpu.make_async_copy(
            self.buf.at[self.me], self.out.at[self.me], self.own.at[self.base]
        )

    def copy(self, d):
        return remote(
            self.buf.at[self.me ^ d], self.out.at[self.me], self.sems,
            self.base * (self.nb - 1) + d - 1, peer("blk", self.me, d),
        )

    def start(self, i):
        pl.when(i == self.me)(lambda: self.local().start())
        for d in range(1, self.nb):
            pl.when(i == (self.me ^ d))(lambda d=d: self.copy(d).start())

    def wait(self):
        self.local().wait()
        for d in range(1, self.nb):
            self.copy(d).wait()


class Plan:
    def __init__(self, sems):
        self.sems, self.count, self.sets = sems, 0, {}

    def add(self, name, makers):
        self.sets[name] = list(enumerate(makers, self.count))
        self.count += len(makers)

    def each(self, name):
        for k, maker in self.sets[name]:
            src, dst, where = maker()
            yield remote(src, dst, self.sems, k, where)

    def start(self, name):
        for c in self.each(name):
            c.start()

    def arrived(self, name):
        for c in self.each(name):
            c.wait_recv()

    def sent(self, name):
        for c in self.each(name):
            c.wait_send()


def other_plane(d):
    return {"dp": lax.axis_index("dp") ^ (2 * d)}


def pair_sum(parts):
    while len(parts) > 1:
        parts = [parts[n] + parts[n + 1] for n in range(0, len(parts), 2)]
    return parts[0]


def rows_of(n, size):
    return pl.ds(pl.multiple_of(n * size, size), size)


def backward_kernel(micros, blocks, nb, planes, x_ref, cot_ref, h_ref, gate_ref, eo_ref, dmg_ref, ob_ref,
                    lse_ref, q_ref, k_ref, v_ref, kt_ref, start_ref, g1_ref, g2_ref, wc_ref, wq_ref,
                    wk_ref, wv_ref, wo_ref, factors, win_hbm, wback_hbm, act_ref, gi_ref, flat_ref,
                    small_ref, gin, gback, dh_all, n1_all, dob, delta, dq_all, dk_all, dv_all, dk_acc,
                    dv_acc, gacc, go_acc, bias_own, bias, act_buf, gi_buf, win, wback, ours, theirs, piece, s1,
                    r1, s2, r2, s3, r3, fl, small, few, rs, own, load_sem, ret_send, ret_recv, send_sem,
                    recv_sem):
    now = pl.program_id(0)
    width = wo_ref.shape[0]
    pairs = width // (2 * HEAD_DIM)
    pair_lanes = 2 * HEAD_DIM
    lead, span = micros * blocks, blocks + pairs
    micro = jnp.where(now < lead, now // blocks, (now - lead) // span)
    step = jnp.where(now < lead, now % blocks, (now - lead) % span)
    last = lead + (micros - 1) * span
    blk, dp = lax.axis_index("blk"), lax.axis_index("dp")
    kind, plane = blk % 2, dp // 2
    steps = plane_steps(nb)
    members = len(steps) + 1
    core = lambda: peer("blk", lax.axis_index("blk"), 1)

    def part_of(far, d):
        return ((blk ^ d) // 2) + (nb // 2) * ((dp % 2) ^ far)

    part = part_of(0, 0)
    cut = win.shape[1]
    rets = (ret_send, ret_recv)
    acts = [Return(nb, act_buf.at[m], act_ref.at[m], own, rets, 2 * m) for m in range(micros)]
    gis = [Return(nb, gi_buf.at[m], gi_ref.at[m], own, rets, 2 * m + 1) for m in range(micros)]
    columns = rows_of(part, cut)
    loads = [
        lambda: pltpu.make_async_copy(win_hbm.at[kind, :, columns], win, load_sem.at[0]),
        lambda: pltpu.make_async_copy(wback_hbm.at[kind, columns, :], wback, load_sem.at[1]),
    ]
    rows = width // planes

    def window(which, p, z):
        if which == 0:
            return gin.at[kind, rows_of(z, rows), rows_of(p, cut)]
        at = pl.multiple_of(p * cut + z * rows, rows)
        return gback.at[kind, pl.ds(at, rows), :]

    def slab(which, p):
        if which == 0:
            return gin.at[kind, :, rows_of(p, cut)]
        return gback.at[kind, rows_of(p, cut), :]

    mine = [
        lambda w=w: pltpu.make_async_copy(piece.at[w], window(w, part, plane), load_sem.at[2 + w])
        for w in range(2)
    ]
    y_peer, x_peer = steps[0], steps[1]
    others = range(1, planes)
    both = range(2)
    plan = Plan((send_sem, recv_sem))
    for w in both:
        plan.add(f"rs{w}", [
            lambda d=d, w=w: (ours.at[w, plane ^ d], theirs.at[w, d - 1], other_plane(d)) for d in others
        ])
        plan.add(f"z{w}", [
            lambda d=d, w=w: (piece.at[w], window(w, part, plane), other_plane(d)) for d in others
        ])
        for name, to in ((f"y0{w}", y_peer), (f"x0{w}", x_peer)):
            plan.add(name, [
                lambda w=w, to=to: (piece.at[w], window(w, part, plane), same_plane(*to))
            ])

    def onward(p, z, w, to):
        return window(w, p, z), window(w, p, z), same_plane(*to)

    part_y = part_of(*y_peer)
    for w in both:
        plan.add(f"yx0{w}", [lambda w=w: onward(part_y, plane, w, x_peer)])
        for name, p, to in ((f"y1{w}", part, y_peer), (f"x1{w}", part, x_peer), (f"yx1{w}", part_y, x_peer)):
            plan.add(name, [
                lambda d=d, w=w, p=p, to=to: onward(p, plane ^ d, w, to) for d in others
            ])
        for name, p in zip("oyxd", [part] + [part_of(*t) for t in steps]):
            plan.add(f"c{name}{w}", [lambda w=w, p=p: (slab(w, p), slab(w, p), core())])

    sizes = [width] + [3 * pair_lanes] * pairs
    halves = [n // 2 for n in sizes]
    quarters = [n // 2 // members for n in sizes]

    def held_sum(c):
        return go_acc if c == 0 else gacc.at[c - 1]

    def quarter_at(c, p):
        at = pl.multiple_of(kind * halves[c] + p * quarters[c], quarters[c])
        return pl.ds(at, quarters[c])

    for c in range(pairs + 1):
        n_half, n_quarter = halves[c], quarters[c]
        plan.add(f"ha{c}", [lambda c=c, r=n_half: (s1.at[c, 0:r], r1.at[c, 0:r], core())])
        plan.add(f"hb{c}", [
            lambda c=c, n=n, r=n_quarter: (s2.at[c, n, 0:r], r2.at[c, n, 0:r], same_plane(*steps[n]))
            for n in range(members - 1)
        ])
        plan.add(f"hz{c}", [
            lambda c=c, d=d, r=n_quarter: (s3.at[c, 0:r], r3.at[c, d - 1, 0:r], other_plane(d))
            for d in others
        ])

        def share(c, n):
            ref = fl.at[c, quarter_at(c, part), :]
            return ref, ref, same_plane(*steps[n])

        def side(c):
            ref = fl.at[c, rows_of(kind, halves[c]), :]
            return ref, ref, core()

        plan.add(f"hg{c}", [lambda c=c, n=n: share(c, n) for n in range(members - 1)])
        plan.add(f"hh{c}", [lambda c=c: side(c)])
    near = [(far, d) for far in (0, 1) for d in range(nb) if far or d]
    plan.add("sb", [lambda n=n: (few.at[0], rs.at[n], same_plane(*near[n])) for n in range(len(near))])
    plan.add("sz", [lambda d=d: (few.at[1], rs.at[len(near) + d - 1], other_plane(d)) for d in others])
    assert plan.count <= send_sem.shape[0]

    def chunk_start(c):
        s1[c, 0 : halves[c]] = held_sum(c)[rows_of(1 - kind, halves[c]), :].astype(BF)
        plan.start(f"ha{c}")

    def chunk_b(c):
        plan.arrived(f"ha{c}")
        at = rows_of(kind, halves[c])
        ref = held_sum(c)
        ref[at, :] = ref[at, :] + r1[c, 0 : halves[c]].astype(F32)
        for n, to in enumerate(steps):
            s2[c, n, 0 : quarters[c]] = ref[quarter_at(c, part_of(*to)), :].astype(BF)
        plan.start(f"hb{c}")

    def chunk_z(c):
        plan.arrived(f"hb{c}")
        r = quarters[c]
        total = pair_sum(
            [held_sum(c)[quarter_at(c, part), :]] + [r2[c, n, 0:r].astype(F32) for n in range(members - 1)]
        )
        s3[c, 0:r] = total.astype(BF)
        plan.start(f"hz{c}")

    def chunk_g(c):
        plan.arrived(f"hz{c}")
        r = quarters[c]
        total = pair_sum([s3[c, 0:r].astype(F32)] + [r3[c, d - 1, 0:r].astype(F32) for d in others])
        fl[c, quarter_at(c, part), :] = total.astype(BF)
        plan.start(f"hg{c}")

    def chunk_h(c):
        plan.arrived(f"hg{c}")
        plan.start(f"hh{c}")

    def out_copy(c):
        return pltpu.make_async_copy(fl.at[c], flat_ref.at[c], load_sem.at[4 + c])

    def chunk_done(c):
        plan.arrived(f"hh{c}")
        out_copy(c).start()

    def reduced(w):
        plan.arrived(f"rs{w}")
        total = pair_sum([ours[w, plane].astype(F32)] + [theirs[w, d - 1].astype(F32) for d in others])
        piece[w] = total.astype(BF)
        mine[w]().start()
        for name in ("z", "y0", "x0"):
            plan.start(f"{name}{w}")

    def own_y(w):
        plan.arrived(f"y0{w}")
        plan.start(f"yx0{w}")

    def whole_slice(w):
        mine[w]().wait()
        plan.arrived(f"z{w}")
        for name in ("y1", "x1", "co"):
            plan.start(f"{name}{w}")

    def slice_y(w):
        plan.arrived(f"y1{w}")
        for name in ("yx1", "cy"):
            plan.start(f"{name}{w}")

    def slice_x(w):
        plan.arrived(f"x0{w}")
        plan.arrived(f"x1{w}")
        plan.start(f"cx{w}")

    def slice_d(w):
        plan.arrived(f"yx0{w}")
        plan.arrived(f"yx1{w}")
        plan.start(f"cd{w}")

    stages = [chunk_start, chunk_b, chunk_z, chunk_g, chunk_h, chunk_done]

    @pl.when(now == 0)
    def _():
        for c in loads:
            c().start()
        partners = [peer("blk", blk, d) for d in range(1, nb)]
        partners += [same_plane(1, d) for d in range(nb)] + [other_plane(d) for d in others]
        arrive(partners)
        small[...] = jnp.zeros_like(small)
        go_acc[...] = jnp.zeros_like(go_acc)
        fill_bias(bias_own, None, False, 0)
        for c in loads:
            c().wait()
        mg, deo = factors[0], factors[1]
        act, slope = gelu_both(nn(mg, win[...]))
        du = (slope * nt(deo, wback[...])).astype(BF)
        g_in = tn(mg, du).astype(BF)
        for n in range(planes):
            ours[0, n] = g_in[n * rows : (n + 1) * rows]
        plan.start("rs0")
        g_back = tn(act.astype(BF), deo).astype(BF)
        for n in range(planes):
            ours[1, n] = g_back[n * rows : (n + 1) * rows]

    gate_rows = gate_ref.shape[0]

    @pl.when(now < lead)
    def _():
        at = rows_of(step, BLOCK)
        h = h_ref[0]
        cot_b = cot_ref[0, 0]
        dout = cot_b.astype(F32)
        r2_ = rms(h)
        z = h * r2_
        n2 = (z * g2_ref[...]).astype(BF)
        gate = gate_ref[...]
        gate_b = gate.astype(BF)
        gate_low = (gate - gate_b.astype(F32)).astype(BF)
        eo = jnp.concatenate([eo_ref[j] for j in range(eo_ref.shape[0])], axis=0)
        dmg = jnp.concatenate([dmg_ref[j] for j in range(dmg_ref.shape[0])], axis=0).astype(BF)
        eo_b = eo.astype(BF)
        eo_low = (eo - eo_b.astype(F32)).astype(BF)
        mixed = tn(
            jnp.concatenate([gate_b, gate_low, gate_b], axis=0),
            jnp.concatenate([eo_b, eo_b, eo_low], axis=0),
        )
        act_buf[micro, step] = (h + mixed).astype(BF)
        for m in range(micros):
            pl.when(micro == m)(functools.partial(acts[m].start, step))
        dw2 = nt(jnp.concatenate([eo_b, eo_low], axis=0), cot_b)
        dw = dw2[:gate_rows] + dw2[gate_rows:] + nt(dmg, n2)
        wdw = gate * dw
        dlog = (wdw - gate * jnp.sum(wdw, axis=1, keepdims=True)).astype(BF)
        dn2 = tn(
            jnp.concatenate([gate_b, dlog], axis=0),
            jnp.concatenate([dmg, wc_ref[...]], axis=0),
        )
        small[0:gate_rows, :] += nn(dlog, n2)
        small[gate_rows : gate_rows + 1, :] += jnp.sum(dn2 * z, axis=0, keepdims=True)
        a = dn2 * g2_ref[...]
        dh = dout + r2_ * (a - z * jnp.mean(a * z, axis=-1, keepdims=True))
        dh_all[micro, at, :] = dh
        da = dh.astype(BF)
        dob_b = nt(da, wo_ref[...]).astype(BF)
        dob[micro, at, :] = dob_b
        ob = ob_ref[0]
        go_acc[...] += tn(ob, da)
        prod = dob_b.astype(F32) * ob.astype(F32)
        high = prod.astype(BF)
        low = (prod - high.astype(F32)).astype(BF)
        heads = head_rows(delta.shape[1], width)
        delta[micro, :, at] = nt(heads, high) + nt(heads, low)
        x = x_ref[0, step].astype(F32)
        n1_all[micro, at, :] = (x * rms(x) * g1_ref[...]).astype(BF)

    for m in range(1, micros):
        for i in range(blocks):
            pl.when(now == m * blocks + i)(
                functools.partial(fill_bias, bias.at[i], start_ref[i], True, i)
            )

    masks = head_masks()

    def attend(m):
        hp = step
        packed = m > 0
        lanes = rows_of(hp, pair_lanes)
        for i in range(blocks):
            low, count = key_range(packed, i)
            at = slice(i * BLOCK, (i + 1) * BLOCK)
            q_pair, dob_pair = q_ref[0, at, :], dob[m, at, lanes]
            k_pair, v_pair = k_ref[0, low : low + count, :], v_ref[0, low : low + count, :]
            dk_sum = dv_sum = None
            dqs = []
            for h in range(2):
                qm, dm = q_pair * masks[h], dob_pair * masks[h]
                scores = add_bias(nt(k_pair, qm), bias.at[i] if packed else bias_own, packed, count)
                p = jnp.exp(scores * SCALE - lse_ref[0, pl.ds(hp * 2 + h, 1), at])
                dp_ = nt(v_pair, dm)
                ds = (p * (dp_ - delta[m, pl.ds(hp * 2 + h, 1), at])).astype(BF)
                kt = kt_ref[0, h * HEAD_DIM : (h + 1) * HEAD_DIM, low : low + count]
                dqs.append(nn(kt, ds) * SCALE)
                dk_part, dv_part = nn(ds, qm), nn(p.astype(BF), dm)
                dk_sum = dk_part if dk_sum is None else dk_sum + dk_part
                dv_sum = dv_part if dv_sum is None else dv_sum + dv_part
            old = i * BLOCK - low
            dk_acc[at, :] = dk_sum[old:]
            dv_acc[at, :] = dv_sum[old:]
            if old:
                dk_acc[low : i * BLOCK, :] += dk_sum[:old]
                dv_acc[low : i * BLOCK, :] += dv_sum[:old]
            dq_all[at, lanes] = jnp.concatenate(dqs, axis=0).T.astype(BF)
        dk = (dk_acc[...] * SCALE).astype(BF)
        dv = dv_acc[...].astype(BF)
        dk_all[:, lanes] = dk
        dv_all[:, lanes] = dv
        g = tn(jnp.concatenate([dq_all[:, lanes], dk, dv], axis=1), n1_all[m])
        if packed:
            gacc[hp] += g
        else:
            gacc[hp] = g

    for m in range(micros):
        in_phase = (now >= lead) & (micro == m) & (step < pairs)
        pl.when(in_phase)(functools.partial(attend, m))

    in_third = (now >= lead) & (step >= pairs)
    i = blk ^ (nb - 1 - (step - pairs))

    @pl.when(in_third)
    def _():
        at = rows_of(i, BLOCK)
        x = x_ref[0, i].astype(F32)
        r1_ = rms(x)
        z1 = x * r1_
        dn1 = (
            nt(dq_all[at, :], wq_ref[...]) + nt(dk_all[at, :], wk_ref[...]) + nt(dv_all[at, :], wv_ref[...])
        )
        small[gate_rows + 8 : gate_rows + 9, :] += jnp.sum(dn1 * z1, axis=0, keepdims=True)
        b = dn1 * g1_ref[...]
        gi = dh_all[micro, at, :] + r1_ * (b - z1 * jnp.mean(b * z1, axis=-1, keepdims=True))
        gi_buf[micro, i] = gi.astype(BF)

    final = lead + micros * span - 1
    tasks = {}

    def after(at, task, *args):
        tasks.setdefault(min(at, final), []).append(functools.partial(task, *args))

    def start_second():
        plan.start("rs1")

    first = last - span
    after(blocks - 1, start_second)
    after(blocks, reduced, 0)
    after(first, reduced, 1)
    after(first, own_y, 0)
    after(first + 2, whole_slice, 0)
    after(first + 2, own_y, 1)
    after(last - 1, whole_slice, 1)
    after(last - 1, slice_y, 0)
    after(last - 1, slice_x, 0)
    after(last + pairs - 2, slice_y, 1)
    after(last + pairs - 2, slice_x, 1)
    after(last + pairs - 1, slice_d, 0)
    for n, stage in enumerate(stages):
        after(lead - 1 + n, stage, 0)
    for c in range(1, pairs):
        for n, stage in enumerate(stages):
            after(last + c - 1 + n, stage, c)
    c = pairs
    after(last + c - 1, chunk_start, c)
    after(last + c, chunk_b, c)
    after(last + c + 2, chunk_z, c)
    for at, todo in tasks.items():
        if at < final:

            @pl.when(now == at)
            def _(todo=todo):
                for task in todo:
                    task()

    @pl.when(in_third)
    def _():
        for m in range(micros):
            pl.when(micro == m)(functools.partial(gis[m].start, i))

    @pl.when(now == final)
    def _():
        per = gate_rows // 2
        few[0] = jnp.concatenate(
            [jnp.sum(small[n * per : (n + 1) * per, :], axis=0, keepdims=True) for n in range(2)]
            + [small[gate_rows : gate_rows + 1, :], small[gate_rows + 8 : gate_rows + 9, :]]
            + [jnp.zeros((4, width), F32)],
            axis=0,
        )
        plan.start("sb")
        for task in tasks[final]:
            task()
        chunk_g(c)
        plan.arrived("sb")
        few[1] = pair_sum([few[0]] + [rs[n] for n in range(len(near))])
        plan.start("sz")
        chunk_h(c)
        slice_d(1)
        chunk_done(c)
        plan.arrived("sz")
        small_ref[...] = pair_sum([few[1]] + [rs[len(near) + d - 1] for d in others])
        for w in both:
            for name in "oyxd":
                plan.arrived(f"c{name}{w}")
        for n in range(pairs + 1):
            out_copy(n).wait()
        for name in plan.sets:
            plan.sent(name)
        for r in acts + gis:
            r.wait()


def whole(shape):
    return pl.BlockSpec(shape, lambda *_: (0,) * len(shape))


def held(shape):
    return pl.BlockSpec(shape, lambda *_: (0,) * len(shape), pipeline_mode=pl.Buffered(1))


ANY = pl.BlockSpec(memory_space=pl.ANY)
DMA = pltpu.SemaphoreType.DMA


def shaped(shape, dtype):
    return jax.ShapeDtypeStruct(shape, dtype)


def params(number):
    return pltpu.CompilerParams(
        vmem_limit_bytes=VMEM_LIMIT, collective_id=number, has_side_effects=True
    )


def forward_call(x, seg, cot, g1, wq, wk, wv, wo, g2, wc):
    nb = lax.axis_size("blk")
    micros, _, rows_in, width = x.shape
    length = nb * rows_in
    blocks = length // BLOCK
    assert x.shape[1] == nb and rows_in == BLOCK
    rows = wc.shape[0]
    heads = width // HEAD_DIM
    per = BLOCK // GROUP
    experts = rows // per
    span = 2 * blocks
    phase = lambda s: jnp.maximum(s % span - blocks, 0)
    whole_micro = lambda a, b: pl.BlockSpec((1, a, b), lambda s: (s // span, 0, 0))
    flat = lambda s: (s // span) * blocks + phase(s)
    moves = 2 * micros + 1
    return pl.pallas_call(
        functools.partial(forward_kernel, micros, blocks, nb),
        grid=(micros * span,),
        in_specs=[ANY, ANY, ANY] + [held(a.shape) for a in (g1, wq, wk, wv, wo, g2, wc)],
        out_specs=[
            whole_micro(length, width), whole_micro(length, width), whole_micro(length, width),
            whole_micro(width, length),
            pl.BlockSpec((1, BLOCK, width), lambda s: (s // span, phase(s), 0)),
            pl.BlockSpec((1, heads, BLOCK), lambda s: (s // span, 0, phase(s))),
            pl.BlockSpec((1, BLOCK, width), lambda s: (s // span, phase(s), 0)),
            pl.BlockSpec((rows, BLOCK), lambda s: (0, flat(s))),
            pl.BlockSpec((experts, per, width), lambda s: (0, flat(s), 0)),
            whole((blocks, 1, BLOCK)), ANY, ANY,
        ],
        out_shape=[
            shaped((micros, length, width), BF), shaped((micros, length, width), BF),
            shaped((micros, length, width), BF), shaped((micros, width, length), BF),
            shaped((micros, length, width), BF), shaped((micros, heads, length), F32),
            shaped((micros, length, width), F32), shaped((rows, micros * length), F32),
            shaped((experts, micros * length // GROUP, width), F32),
            shaped((blocks, 1, BLOCK), jnp.int32), shaped(x.shape, BF), shaped(x.shape, BF),
        ],
        scratch_shapes=[
            pltpu.VMEM(x.shape, BF), pltpu.VMEM(seg.shape, seg.dtype),
            pltpu.VMEM((length, BLOCK), F32), pltpu.VMEM((BLOCK, width), F32),
            pltpu.VMEM((heads, BLOCK), F32), pltpu.VMEM((width, width), BF),
            DMA((moves + 1,)), DMA((moves * (nb - 1),)), DMA((moves * (nb - 1),)),
        ],
        compiler_params=params(1),
        name="attention_forward",
    )(x, seg, cot, g1, wq, wk, wv, wo, g2, wc)


def experts_call(mg, gate, cot, w_in, w_back):
    micros, nb, _, width = cot.shape
    experts, groups, _ = mg.shape
    ff = w_in.shape[2]
    blocks = gate.shape[1] // BLOCK // micros
    chunk = min(CHUNK, ff)
    by_expert = lambda n: pl.BlockSpec((1, n, width), lambda e, c: (e, 0, 0))
    members = 2 * nb
    return pl.pallas_call(
        functools.partial(experts_kernel, micros, blocks, nb),
        grid=(experts, ff // chunk),
        in_specs=[
            held(mg.shape), held(gate.shape), held(cot.shape),
            pl.BlockSpec((1, width, chunk), lambda e, c: (e, 0, c)),
            pl.BlockSpec((1, chunk, width), lambda e, c: (e, c, 0)),
        ],
        out_specs=[by_expert(groups)] * 2 + [whole((2, members * groups, width))],
        out_shape=[shaped((experts, groups, width), F32)] * 2
        + [shaped((2, members * groups, width), BF)],
        scratch_shapes=[
            pltpu.VMEM((experts, 2, groups, width), BF),
            pltpu.VMEM((members - 1, 2, groups, width), BF), DMA((members - 1,)), DMA((members - 1,)),
        ],
        compiler_params=params(2),
        name="experts",
    )(mg, gate, cot, w_in, w_back)


def backward_call(x, cot, h, gate, eo, dmg, ob, lse, q, k, v, kt, start, g1, g2, wc, wq, wk, wv, wo,
                  factors, w_in, w_back):
    micros, nb, _, width = x.shape
    planes = lax.axis_size("dp") // 2
    length = q.shape[1]
    blocks = length // BLOCK
    rows = wc.shape[0]
    per = BLOCK // GROUP
    experts = rows // per
    heads = width // HEAD_DIM
    pairs = heads // 2
    ff = w_in.shape[2]
    cut = ff // nb
    assert cut == width
    members = len(plane_steps(nb)) + 1
    lead, span = micros * blocks, blocks + pairs
    flat = lambda s: jnp.minimum(s, lead - 1)
    m_late = lambda s: jnp.maximum(s - lead, 0) // span
    m_of = lambda s: jnp.where(s < lead, s // blocks, m_late(s))
    pair_of = lambda s: jnp.minimum(jnp.maximum(s - lead, 0) % span, pairs - 1)
    row_block = pl.BlockSpec((1, BLOCK, width), lambda s: (flat(s) // blocks, flat(s) % blocks, 0))
    group_block = pl.BlockSpec((experts, per, width), lambda s: (0, flat(s), 0))
    pair_block = pl.BlockSpec((1, length, 2 * HEAD_DIM), lambda s: (m_late(s), 0, pair_of(s)))
    piece = (2, width // planes, cut)
    chunk = width
    chunks = pairs + 1
    half = chunk // 2
    quarter = half // members
    reach = max(key_range(True, i)[1] for i in range(blocks))
    small = (rows + 16, width)
    few = (8, width)
    vm = pltpu.VMEM
    copies = 96 + 16 * chunks + 32 * planes
    return pl.pallas_call(
        functools.partial(backward_kernel, micros, blocks, nb, planes),
        grid=(lead + micros * span,),
        in_specs=[
            pl.BlockSpec((1, nb, BLOCK, width), lambda s: (m_of(s), 0, 0, 0)),
            pl.BlockSpec((1, 1, BLOCK, width), lambda s: (flat(s) // blocks, flat(s) % blocks, 0, 0)),
            row_block,
            pl.BlockSpec((rows, BLOCK), lambda s: (0, flat(s))),
            group_block, group_block, row_block,
            pl.BlockSpec((1, heads, length), lambda s: (m_late(s), 0, 0)),
            pair_block, pair_block, pair_block,
            pl.BlockSpec((1, 2 * HEAD_DIM, length), lambda s: (m_late(s), pair_of(s), 0)),
        ] + [held(a.shape) for a in (start, g1, g2, wc, wq, wk, wv, wo, factors)] + [ANY, ANY],
        out_specs=[ANY, ANY, ANY, whole(few), ANY, ANY],
        out_shape=[
            shaped(x.shape, BF), shaped(x.shape, BF), shaped((chunks, chunk, width), BF),
            shaped(few, F32), shaped(w_in.shape, BF), shaped(w_back.shape, BF),
        ],
        scratch_shapes=[
            vm((micros, length, width), F32), vm((micros, length, width), BF),
            vm((micros, length, width), BF), vm((micros, heads, length), F32), vm((length, width), BF), vm((length, width), BF),
            vm((length, width), BF), vm((length, 2 * HEAD_DIM), F32), vm((length, 2 * HEAD_DIM), F32),
            vm((pairs, 6 * HEAD_DIM, width), F32), vm((width, width), F32), vm((BLOCK, BLOCK), F32),
            vm((blocks, reach, BLOCK), F32),
            vm(x.shape, BF), vm(x.shape, BF), vm((width, cut), BF), vm((cut, width), BF),
            vm((2, planes) + piece[1:], BF), vm((2, planes - 1) + piece[1:], BF), vm(piece, BF),
            vm((chunks, half, width), BF), vm((chunks, half, width), BF),
            vm((chunks, members - 1, quarter, width), BF), vm((chunks, members - 1, quarter, width), BF),
            vm((chunks, quarter, width), BF), vm((chunks, planes - 1, quarter, width), BF),
            vm((chunks, chunk, width), BF), vm(small, F32), vm((2,) + few, F32),
            vm((2 * nb + planes - 2,) + few, F32),
            DMA((2 * micros,)), DMA((5 + pairs,)), DMA((2 * micros * (nb - 1),)),
            DMA((2 * micros * (nb - 1),)), DMA((copies,)), DMA((copies,)),
        ],
        compiler_params=params(3),
        name="attention_backward",
    )(x, cot, h, gate, eo, dmg, ob, lse, q, k, v, kt, start, g1, g2, wc, wq, wk, wv, wo, factors, w_in,
      w_back)


def widen_kernel(flat_ref, one_ref, gin_ref, gback_ref, q_ref, k_ref, v_ref, o_ref, gin_out, gback_out):
    gin_out[...] = gin_ref[...].astype(F32)
    gback_out[...] = gback_ref[...].astype(F32)
    lanes = q_ref.shape[1]
    for n, ref in enumerate((q_ref, k_ref, v_ref)):
        ref[...] = flat_ref[0, n * lanes : (n + 1) * lanes, :].astype(F32).T
    o_ref[...] = one_ref[0].astype(F32)


def widen_call(flat, gin, gback):
    experts, width, ff = gin.shape
    lanes = 2 * HEAD_DIM
    pairs = width // lanes
    cuts = ff // width
    pair = lambda s: jnp.minimum(s, pairs - 1)
    tall = pl.BlockSpec((width, lanes), lambda s: (0, pair(s)))
    in_block = pl.BlockSpec((1, width, width), lambda s: (s // cuts, 0, s % cuts))
    back_block = pl.BlockSpec((1, width, width), lambda s: (s // cuts, s % cuts, 0))
    square = shaped((width, width), F32)
    return pl.pallas_call(
        widen_kernel,
        grid=(experts * cuts,),
        in_specs=[
            pl.BlockSpec((1,) + flat.shape[1:], lambda s: (1 + pair(s), 0, 0)),
            pl.BlockSpec((1, lanes, width), lambda s: (0, pair(s), 0)), in_block, back_block,
        ],
        out_specs=[tall, tall, tall, pl.BlockSpec((lanes, width), lambda s: (pair(s), 0)), in_block, back_block],
        out_shape=[square] * 4 + [shaped(gin.shape, F32), shaped(gback.shape, F32)],
        compiler_params=pltpu.CompilerParams(vmem_limit_bytes=VMEM_LIMIT),
        name="gradients_out",
    )(flat, flat, gin, gback)


def local(block_input, segment_ids, gain_one, w_query, w_key, w_value, w_out, gain_two, w_ctrl,
          w_in, w_back, cotangent):
    micros, seqs, rows, width = block_input.shape
    experts, _, ff = w_in.shape
    nb = lax.axis_size("blk")
    per = BLOCK // GROUP
    g1, g2 = gain_one.reshape(1, width), gain_two.reshape(1, width)
    wc = jnp.repeat(w_ctrl.T, per, axis=0)
    seg = segment_ids.reshape(nb, 2, rows // 2)
    q, k, v, kt, ob, lse, h, gate, mg, start, x, cot = forward_call(
        block_input, seg, cotangent, g1, w_query, w_key, w_value, w_out, g2, wc
    )
    eo, dmg, factors = experts_call(mg, gate, cot, w_in, w_back)
    acts, gis, flat, small, grad_in, grad_back = backward_call(
        x, cot, h, gate, eo, dmg, ob, lse, q, k, v, kt, start, g1, g2, wc, w_query, w_key, w_value,
        w_out, factors, w_in, w_back,
    )
    gq, gk, gv, go, grad_in, grad_back = widen_call(flat, grad_in, grad_back)
    return acts, gis, small[3], gq, gk, gv, go, small[2], small[:experts].T, grad_in, grad_back


def solution(mesh):
    data = P(None, "dp", "blk", None)
    in_specs = (data, P("dp", "blk")) + (P(),) * 9 + (data,)
    out_specs = (data, data) + (P(),) * 9
    return jax.shard_map(local, mesh=mesh, in_specs=in_specs, out_specs=out_specs, check_vma=False)
```

```python
import functools

import jax
import jax.numpy as jnp
from jax import lax
from jax.experimental import pallas as pl
from jax.experimental.pallas import tpu as pltpu
from jax.sharding import PartitionSpec as P

HEAD_DIM = 64
GROUP = 32
EPSILON = 1e-05
BLOCK = 256
CHUNK = 512
SCALE = 0.125
MASKED = -1e30
VMEM_LIMIT = 60 * 1024 * 1024
BF = jnp.bfloat16
F32 = jnp.float32
MESH = pl.DeviceIdType.MESH


def dot(a, b, ca, cb):
    return lax.dot_general(a, b, (((ca,), (cb,)), ((), ())), preferred_element_type=F32)


def nn(a, b):
    return dot(a, b, 1, 0)


def nt(a, b):
    return dot(a, b, 1, 1)


def tn(a, b):
    return dot(a, b, 0, 0)


def key_range(packed, i):
    low = max(0, i * BLOCK - BLOCK - BLOCK // 2) if packed else 0
    return low, (i + 1) * BLOCK - low


def head_masks():
    lane = lax.broadcasted_iota(jnp.int32, (1, 2 * HEAD_DIM), 1)
    first = (lane < HEAD_DIM).astype(F32).astype(BF)
    return first, (lane >= HEAD_DIM).astype(F32).astype(BF)


def group_match(rows, tokens):
    row = lax.broadcasted_iota(jnp.int32, (rows, tokens), 0)
    col = lax.broadcasted_iota(jnp.int32, (rows, tokens), 1)
    return (row % (tokens // GROUP)) == (col // GROUP)


def fill_bias(bias_ref, start_ref, packed, i):
    low, count = key_range(packed, i)
    q_pos = i * BLOCK + lax.broadcasted_iota(jnp.int32, (1, BLOCK), 1)
    if packed:
        k_pos = low + lax.broadcasted_iota(jnp.int32, (count, BLOCK), 0)
        allowed = (k_pos <= q_pos) & (k_pos >= start_ref[...])
        bias_ref[0:count, :] = jnp.where(allowed, 0.0, MASKED)
    else:
        k_pos = i * BLOCK + lax.broadcasted_iota(jnp.int32, (BLOCK, BLOCK), 0)
        bias_ref[0:BLOCK, :] = jnp.where(k_pos <= q_pos, 0.0, MASKED)


def add_bias(scores, bias_ref, packed, count):
    if packed:
        return scores + bias_ref[0:count, :]
    last = scores[count - BLOCK :, :] + bias_ref[0:BLOCK, :]
    if count == BLOCK:
        return last
    return jnp.concatenate([scores[: count - BLOCK, :], last], axis=0)


def rms(values):
    return lax.rsqrt(jnp.mean(values * values, axis=-1, keepdims=True) + EPSILON)


def peer(axis, me, d):
    return {axis: me ^ d}


def arrive(partners):
    barrier = pltpu.get_barrier_semaphore()
    for p in partners:
        pl.semaphore_signal(barrier, inc=1, device_id=p, device_id_type=MESH)
    pl.semaphore_wait(barrier, len(partners))


def remote(src, dst, sems, k, where):
    return pltpu.make_async_remote_copy(
        src_ref=src, dst_ref=dst, send_sem=sems[0].at[k], recv_sem=sems[1].at[k],
        device_id=where, device_id_type=MESH,
    )


class Exchange:
    def __init__(self, nb, src, dst, own, sems, base):
        self.nb, self.src, self.dst, self.own, self.sems, self.base = nb, src, dst, own, sems, base
        self.me = lax.axis_index("blk")

    def local(self):
        return pltpu.make_async_copy(
            self.src.at[self.me], self.dst.at[self.me], self.own.at[self.base]
        )

    def copy(self, d):
        return remote(
            self.src.at[self.me ^ d], self.dst.at[self.me], self.sems,
            self.base * (self.nb - 1) + d - 1, peer("blk", self.me, d),
        )

    def start(self):
        self.local().start()
        for d in range(1, self.nb):
            self.copy(d).start()

    def wait(self):
        self.local().wait()
        for d in range(1, self.nb):
            self.copy(d).wait()


def unit(n):
    row = lax.broadcasted_iota(jnp.int32, (n, n), 0)
    col = lax.broadcasted_iota(jnp.int32, (n, n), 1)
    return (row == col).astype(F32).astype(BF)


def split_three(a):
    high = a.astype(BF)
    rest = a - high.astype(F32)
    mid = rest.astype(BF)
    return [high, mid, (rest - mid.astype(F32)).astype(BF)]


def head_rows(heads, width):
    row = lax.broadcasted_iota(jnp.int32, (heads, width), 0)
    col = lax.broadcasted_iota(jnp.int32, (heads, width), 1)
    return (row == col // HEAD_DIM).astype(F32).astype(BF)


def forward_kernel(micros, blocks, nb, x_src, seg_src, cot_src, g1_ref, wq_ref, wk_ref, wv_ref, wo_ref,
                   g2_ref, wc_ref, q_ref, k_ref, v_ref, kt_ref, ob_ref, lse_ref, h_ref, gate_ref,
                   mg_ref, start_ref, x_out, cot_out, x_all, seg_all, bias, o_acc, sums, eye, own,
                   send_sem, recv_sem):
    sems = (send_sem, recv_sem)
    now = pl.program_id(0)
    span = 2 * blocks
    micro, step = now // span, now % span
    width = wo_ref.shape[0]
    pairs = width // (2 * HEAD_DIM)
    me = lax.axis_index("blk")
    xs = [Exchange(nb, x_src.at[m], x_all.at[m], own, sems, m) for m in range(micros)]
    segs = Exchange(nb, seg_src, seg_all, own, sems, micros)
    cots = [
        Exchange(nb, cot_src.at[m], cot_out.at[m], own, sems, micros + 1 + m) for m in range(micros)
    ]
    keep = pltpu.make_async_copy(x_all, x_out, own.at[2 * micros + 1])

    @pl.when(now == 0)
    def _():
        xs[0].local().start()
        eye[...] = unit(width)
        arrive([peer("blk", me, d) for d in range(1, nb)])
        for d in range(1, nb):
            xs[0].copy(d).start()

    @pl.when(step < blocks)
    def _():
        block = me ^ step
        for m in range(micros):
            pl.when((micro == m) & (step == 0))(xs[m].local().wait)
            for d in range(1, nb):
                pl.when((micro == m) & (step == d))(xs[m].copy(d).wait_recv)
        x = x_all[micro, block].astype(F32)
        n1 = (x * rms(x) * g1_ref[...]).astype(BF)
        at = pl.ds(pl.multiple_of(block * BLOCK, BLOCK), BLOCK)
        q_ref[0, at, :] = nn(n1, wq_ref[...]).astype(BF)
        k = nn(n1, wk_ref[...]).astype(BF)
        k_ref[0, at, :] = k
        v_ref[0, at, :] = nn(n1, wv_ref[...]).astype(BF)
        kt_ref[0, :, at] = nt(eye[...], k).astype(BF)

    @pl.when(now == nb - 1)
    def _():
        segs.start()
        for m in range(1, micros):
            xs[m].start()

    @pl.when(now == blocks)
    def _():
        for c in cots:
            c.start()

    @pl.when(now == span)
    def _():
        segs.wait()
        counts = [
            jnp.sum(jnp.sum((seg_all[...] < d).astype(F32), axis=0), keepdims=True)
            for d in range(1, nb * seg_all.shape[1] * seg_all.shape[2] // BLOCK)
        ]
        for b in range(blocks):
            seg = jnp.concatenate([seg_all[b, n : n + 1, :] for n in range(seg_all.shape[1])], axis=1)
            start = jnp.zeros(seg.shape, F32)
            for d, count in enumerate(counts):
                start = jnp.where(seg == d + 1, count, start)
            start_ref[b] = start.astype(jnp.int32)

    masks = head_masks()

    def attend(packed, i):
        low, count = key_range(packed, i)
        fill_bias(bias, start_ref[i], packed, i)
        for hp in range(pairs):
            lanes = slice(hp * 2 * HEAD_DIM, (hp + 1) * 2 * HEAD_DIM)
            q_pair = q_ref[0, i * BLOCK : (i + 1) * BLOCK, lanes]
            k_pair = k_ref[0, low : low + count, lanes]
            v_pair = v_ref[0, low : low + count, lanes]
            o_pair = None
            for h in range(2):
                scores = add_bias(nt(k_pair, q_pair * masks[h]), bias, packed, count)
                top = jnp.max(scores, axis=0, keepdims=True)
                p = jnp.exp((scores - top) * SCALE)
                total = jnp.sum(p, axis=0, keepdims=True)
                o = tn(p.astype(BF), v_pair * masks[h])
                o_pair = o if o_pair is None else o_pair + o
                sums[hp * 2 + h : hp * 2 + h + 1, :] = 1.0 / total
                lse_ref[0, hp * 2 + h : hp * 2 + h + 1, :] = top * SCALE + jnp.log(total)
            o_acc[:, lanes] = o_pair

    for m in range(micros):
        for i in range(blocks):
            pl.when(now == m * span + blocks + i)(functools.partial(attend, m > 0, i))

    @pl.when(step >= blocks)
    def _():
        heads = head_rows(sums.shape[0], width)
        scale = tn(
            jnp.concatenate(split_three(sums[...]), axis=0), jnp.concatenate([heads] * 3, axis=0)
        )
        ob = (o_acc[...] * scale).astype(BF)
        ob_ref[0] = ob
        h = x_all[micro, step - blocks].astype(F32) + nn(ob, wo_ref[...])
        h_ref[0] = h
        n2 = (h * rms(h) * g2_ref[...]).astype(BF)
        logits = nt(wc_ref[...], n2)
        rows = logits.shape[0]
        match = group_match(rows, BLOCK)
        logits = jnp.where(match, logits, MASKED)
        e = jnp.where(match, jnp.exp(logits - jnp.max(logits, axis=1, keepdims=True)), 0.0)
        gate = e / jnp.sum(e, axis=1, keepdims=True)
        gate_ref[...] = gate
        mg = nn(gate.astype(BF), n2).astype(BF).astype(F32)
        half = rows // mg_ref.shape[0]
        for j in range(mg_ref.shape[0]):
            mg_ref[j] = mg[j * half : (j + 1) * half]

    @pl.when(now == span + nb)
    def _():
        keep.start()

    @pl.when(now == micros * span - 1)
    def _():
        keep.wait()
        for x in xs:
            for d in range(1, nb):
                x.copy(d).wait_send()
        for c in cots:
            c.wait()


def gelu_both(u):
    c = 0.7978845608028654
    t = jnp.tanh(c * (u + 0.044715 * (u * u * u)))
    act = 0.5 * u * (1.0 + t)
    slope = 0.5 * (1.0 + t) + 0.5 * u * (1.0 - t * t) * (c * (1.0 + 3 * 0.044715 * (u * u)))
    return act, slope


def same_plane(far, d):
    return {"dp": lax.axis_index("dp") ^ far, "blk": lax.axis_index("blk") ^ d}


def plane_steps(nb):
    return [(far, d) for far in (0, 1) for d in range(0, nb, 2) if far or d]


def experts_kernel(micros, blocks, nb, *refs):
    mg_ref, gate_ref, cot_ref, win_ref, wback_ref = refs[:5]
    eo_ref, dmg_ref, all_ref, factors, gathered, send_sem, recv_sem = refs[5:]
    sems = (send_sem, recv_sem)
    e, c = pl.program_id(0), pl.program_id(1)
    at = e * pl.num_programs(1) + c
    last = pl.num_programs(0) * pl.num_programs(1) - 1
    per = BLOCK // GROUP
    n_exp = factors.shape[0]
    groups = micros * blocks * per
    blk = lax.axis_index("blk")
    kind = blk % n_exp
    steps = [(far, d) for far in (0, 1) for d in range(nb) if far or d]

    def plane_copy(n):
        far, d = steps[n]
        return remote(factors.at[kind ^ (d & 1)], gathered.at[n], sems, n, same_plane(far, d))

    @pl.when(at == 0)
    def _():
        deo = []
        for m in range(micros):
            for i in range(blocks):
                at_rows = (m * blocks + i) * BLOCK
                deo.append(nn(gate_ref[:, at_rows : at_rows + BLOCK].astype(BF), cot_ref[m, i]))
        for j in range(n_exp):
            factors[j, 0] = mg_ref[j].astype(BF)
            factors[j, 1] = jnp.concatenate(
                [d[j * per : (j + 1) * per] for d in deo], axis=0
            ).astype(BF)
        arrive([same_plane(*s) for s in steps])
        for n in range(len(steps)):
            plane_copy(n).start()

    mg, deo = factors[e, 0], factors[e, 1]
    act, slope = gelu_both(nn(mg, win_ref[0]))
    eo_part = nn(act.astype(BF), wback_ref[0])
    du = (slope * nt(deo, wback_ref[0])).astype(BF)
    dmg_part = nt(du, win_ref[0])

    @pl.when(c == 0)
    def _():
        eo_ref[0] = eo_part
        dmg_ref[0] = dmg_part

    @pl.when(c > 0)
    def _():
        eo_ref[0] += eo_part
        dmg_ref[0] += dmg_part

    @pl.when(at == last)
    def _():
        for n in range(len(steps)):
            plane_copy(n).wait()
        for n in range(len(steps) + 1):
            piece = factors[kind] if n == 0 else gathered[n - 1]
            for f in range(2):
                all_ref[f, n * groups : (n + 1) * groups, :] = piece[f]


class Return:
    def __init__(self, nb, buf, out, own, sems, base):
        self.nb, self.buf, self.out, self.own, self.sems, self.base = nb, buf, out, own, sems, base
        self.me = lax.axis_index("blk")

    def local(self):
        return pltpu.make_async_copy(
            self.buf.at[self.me], self.out.at[self.me], self.own.at[self.base]
        )

    def copy(self, d):
        return remote(
            self.buf.at[self.me ^ d], self.out.at[self.me], self.sems,
            self.base * (self.nb - 1) + d - 1, peer("blk", self.me, d),
        )

    def start(self, i, reach=None):
        pl.when(i == self.me)(lambda: self.local().start())
        for d in range(1, reach or self.nb):
            pl.when(i == (self.me ^ d))(lambda d=d: self.copy(d).start())

    def wait(self):
        self.local().wait()
        for d in range(1, self.nb):
            self.copy(d).wait()


class Plan:
    def __init__(self, sems):
        self.sems, self.count, self.sets = sems, 0, {}

    def add(self, name, makers):
        self.sets[name] = list(enumerate(makers, self.count))
        self.count += len(makers)

    def each(self, name):
        for k, maker in self.sets[name]:
            src, dst, where = maker()
            yield remote(src, dst, self.sems, k, where)

    def start(self, name):
        for c in self.each(name):
            c.start()

    def arrived(self, name):
        for c in self.each(name):
            c.wait_recv()

    def sent(self, name):
        for c in self.each(name):
            c.wait_send()


def other_plane(d):
    return {"dp": lax.axis_index("dp") ^ (2 * d)}


def pair_sum(parts):
    while len(parts) > 1:
        parts = [parts[n] + parts[n + 1] for n in range(0, len(parts), 2)]
    return parts[0]


def rows_of(n, size):
    return pl.ds(pl.multiple_of(n * size, size), size)


def backward_kernel(micros, blocks, nb, planes, x_ref, cot_ref, h_ref, gate_ref, eo_ref, dmg_ref, ob_ref,
                    lse_ref, q_ref, k_ref, v_ref, kt_ref, start_ref, g1_ref, g2_ref, wc_ref, wq_ref,
                    wk_ref, wv_ref, wo_ref, factors, win_hbm, wback_hbm, act_ref, gi_ref, flat_ref,
                    small_ref, gin, gback, dh_all, n1_all, dob, delta, dq_all, dk_all, dv_all, dk_acc,
                    dv_acc, gacc, go_acc, bias_own, bias, act_buf, gi_buf, win, wback, ours, theirs, piece, s1,
                    r1, s2, r2, s3, r3, fl, small, few, rs, own, load_sem, ret_send, ret_recv, send_sem,
                    recv_sem):
    now = pl.program_id(0)
    width = wo_ref.shape[0]
    pairs = width // (2 * HEAD_DIM)
    pair_lanes = 2 * HEAD_DIM
    lead, span = micros * blocks, blocks + pairs
    micro = jnp.where(now < lead, now // blocks, (now - lead) // span)
    step = jnp.where(now < lead, now % blocks, (now - lead) % span)
    last = lead + (micros - 1) * span
    blk, dp = lax.axis_index("blk"), lax.axis_index("dp")
    kind, plane = blk % 2, dp // 2
    steps = plane_steps(nb)
    members = len(steps) + 1
    core = lambda: peer("blk", lax.axis_index("blk"), 1)

    def part_of(far, d):
        return ((blk ^ d) // 2) + (nb // 2) * ((dp % 2) ^ far)

    part = part_of(0, 0)
    cut = win.shape[1]
    rets = (ret_send, ret_recv)
    acts = [Return(nb, act_buf.at[m], act_ref.at[m], own, rets, 2 * m) for m in range(micros)]
    gis = [Return(nb, gi_buf.at[m], gi_ref.at[m], own, rets, 2 * m + 1) for m in range(micros)]
    columns = rows_of(part, cut)
    loads = [
        lambda: pltpu.make_async_copy(win_hbm.at[kind, :, columns], win, load_sem.at[0]),
        lambda: pltpu.make_async_copy(wback_hbm.at[kind, columns, :], wback, load_sem.at[1]),
    ]
    rows = width // planes

    def window(which, p, z):
        if which == 0:
            return gin.at[kind, rows_of(z, rows), rows_of(p, cut)]
        at = pl.multiple_of(p * cut + z * rows, rows)
        return gback.at[kind, pl.ds(at, rows), :]

    def slab(which, p):
        if which == 0:
            return gin.at[kind, :, rows_of(p, cut)]
        return gback.at[kind, rows_of(p, cut), :]

    mine = [
        lambda w=w: pltpu.make_async_copy(piece.at[w], window(w, part, plane), load_sem.at[2 + w])
        for w in range(2)
    ]
    y_peer, x_peer = steps[0], steps[1]
    others = range(1, planes)
    both = range(2)
    plan = Plan((send_sem, recv_sem))
    for w in both:
        plan.add(f"rs{w}", [
            lambda d=d, w=w: (ours.at[w, plane ^ d], theirs.at[w, d - 1], other_plane(d)) for d in others
        ])
        plan.add(f"z{w}", [
            lambda d=d, w=w: (piece.at[w], window(w, part, plane), other_plane(d)) for d in others
        ])
        for name, to in ((f"y0{w}", y_peer), (f"x0{w}", x_peer)):
            plan.add(name, [
                lambda w=w, to=to: (piece.at[w], window(w, part, plane), same_plane(*to))
            ])

    def onward(p, z, w, to):
        return window(w, p, z), window(w, p, z), same_plane(*to)

    part_y = part_of(*y_peer)
    for w in both:
        plan.add(f"yx0{w}", [lambda w=w: onward(part_y, plane, w, x_peer)])
        for name, p, to in ((f"y1{w}", part, y_peer), (f"x1{w}", part, x_peer), (f"yx1{w}", part_y, x_peer)):
            plan.add(name, [
                lambda d=d, w=w, p=p, to=to: onward(p, plane ^ d, w, to) for d in others
            ])
        for name, p in zip("oyxd", [part] + [part_of(*t) for t in steps]):
            plan.add(f"c{name}{w}", [lambda w=w, p=p: (slab(w, p), slab(w, p), core())])

    sizes = [width] + [3 * pair_lanes] * pairs
    halves = [n // 2 for n in sizes]
    quarters = [n // 2 // members for n in sizes]

    def held_sum(c):
        return go_acc if c == 0 else gacc.at[c - 1]

    def quarter_at(c, p):
        at = pl.multiple_of(kind * halves[c] + p * quarters[c], quarters[c])
        return pl.ds(at, quarters[c])

    for c in range(pairs + 1):
        n_half, n_quarter = halves[c], quarters[c]
        plan.add(f"ha{c}", [lambda c=c, r=n_half: (s1.at[c, 0:r], r1.at[c, 0:r], core())])
        plan.add(f"hb{c}", [
            lambda c=c, n=n, r=n_quarter: (s2.at[c, n, 0:r], r2.at[c, n, 0:r], same_plane(*steps[n]))
            for n in range(members - 1)
        ])
        plan.add(f"hz{c}", [
            lambda c=c, d=d, r=n_quarter: (s3.at[c, 0:r], r3.at[c, d - 1, 0:r], other_plane(d))
            for d in others
        ])

        def share(c, n):
            ref = fl.at[c, quarter_at(c, part), :]
            return ref, ref, same_plane(*steps[n])

        def side(c):
            ref = fl.at[c, rows_of(kind, halves[c]), :]
            return ref, ref, core()

        plan.add(f"hg{c}", [lambda c=c, n=n: share(c, n) for n in range(members - 1)])
        plan.add(f"hh{c}", [lambda c=c: side(c)])
    near = [(far, d) for far in (0, 1) for d in range(nb) if far or d]
    plan.add("sb", [lambda n=n: (few.at[0], rs.at[n], same_plane(*near[n])) for n in range(len(near))])
    plan.add("sz", [lambda d=d: (few.at[1], rs.at[len(near) + d - 1], other_plane(d)) for d in others])
    assert plan.count <= send_sem.shape[0]

    def chunk_start(c):
        s1[c, 0 : halves[c]] = held_sum(c)[rows_of(1 - kind, halves[c]), :].astype(BF)
        plan.start(f"ha{c}")

    def chunk_b(c):
        plan.arrived(f"ha{c}")
        at = rows_of(kind, halves[c])
        ref = held_sum(c)
        ref[at, :] = ref[at, :] + r1[c, 0 : halves[c]].astype(F32)
        for n, to in enumerate(steps):
            s2[c, n, 0 : quarters[c]] = ref[quarter_at(c, part_of(*to)), :].astype(BF)
        plan.start(f"hb{c}")

    def chunk_z(c):
        plan.arrived(f"hb{c}")
        r = quarters[c]
        total = pair_sum(
            [held_sum(c)[quarter_at(c, part), :]] + [r2[c, n, 0:r].astype(F32) for n in range(members - 1)]
        )
        s3[c, 0:r] = total.astype(BF)
        plan.start(f"hz{c}")

    def chunk_g(c):
        plan.arrived(f"hz{c}")
        r = quarters[c]
        total = pair_sum([s3[c, 0:r].astype(F32)] + [r3[c, d - 1, 0:r].astype(F32) for d in others])
        fl[c, quarter_at(c, part), :] = total.astype(BF)
        plan.start(f"hg{c}")

    def chunk_h(c):
        plan.arrived(f"hg{c}")
        plan.start(f"hh{c}")

    def out_copy(c):
        return pltpu.make_async_copy(fl.at[c], flat_ref.at[c], load_sem.at[4 + c])

    def chunk_done(c):
        plan.arrived(f"hh{c}")
        out_copy(c).start()

    def reduced(w):
        plan.arrived(f"rs{w}")
        total = pair_sum([ours[w, plane].astype(F32)] + [theirs[w, d - 1].astype(F32) for d in others])
        piece[w] = total.astype(BF)
        mine[w]().start()
        for name in ("z", "y0", "x0"):
            plan.start(f"{name}{w}")

    def own_y(w):
        plan.arrived(f"y0{w}")
        plan.start(f"yx0{w}")

    def whole_slice(w):
        mine[w]().wait()
        plan.arrived(f"z{w}")
        for name in ("y1", "x1", "co"):
            plan.start(f"{name}{w}")

    def slice_y(w):
        plan.arrived(f"y1{w}")
        for name in ("yx1", "cy"):
            plan.start(f"{name}{w}")

    def slice_x(w):
        plan.arrived(f"x0{w}")
        plan.arrived(f"x1{w}")
        plan.start(f"cx{w}")

    def slice_d(w):
        plan.arrived(f"yx0{w}")
        plan.arrived(f"yx1{w}")
        plan.start(f"cd{w}")

    stages = [chunk_start, chunk_b, chunk_z, chunk_g, chunk_h, chunk_done]

    @pl.when(now == 0)
    def _():
        for c in loads:
            c().start()
        partners = [peer("blk", blk, d) for d in range(1, nb)]
        partners += [same_plane(1, d) for d in range(nb)] + [other_plane(d) for d in others]
        arrive(partners)
        small[...] = jnp.zeros_like(small)
        go_acc[...] = jnp.zeros_like(go_acc)
        fill_bias(bias_own, None, False, 0)
        for c in loads:
            c().wait()
        mg, deo = factors[0], factors[1]
        act, slope = gelu_both(nn(mg, win[...]))
        du = (slope * nt(deo, wback[...])).astype(BF)
        g_in = tn(mg, du).astype(BF)
        for n in range(planes):
            ours[0, n] = g_in[n * rows : (n + 1) * rows]
        plan.start("rs0")
        g_back = tn(act.astype(BF), deo).astype(BF)
        for n in range(planes):
            ours[1, n] = g_back[n * rows : (n + 1) * rows]
        plan.start("rs1")

    gate_rows = gate_ref.shape[0]

    @pl.when(now < lead)
    def _():
        at = rows_of(step, BLOCK)
        h = h_ref[0]
        cot_b = cot_ref[0, 0]
        dout = cot_b.astype(F32)
        r2_ = rms(h)
        z = h * r2_
        n2 = (z * g2_ref[...]).astype(BF)
        gate = gate_ref[...]
        gate_b = gate.astype(BF)
        gate_low = (gate - gate_b.astype(F32)).astype(BF)
        eo = jnp.concatenate([eo_ref[j] for j in range(eo_ref.shape[0])], axis=0)
        dmg = jnp.concatenate([dmg_ref[j] for j in range(dmg_ref.shape[0])], axis=0).astype(BF)
        eo_b = eo.astype(BF)
        eo_low = (eo - eo_b.astype(F32)).astype(BF)
        mixed = tn(
            jnp.concatenate([gate_b, gate_low, gate_b], axis=0),
            jnp.concatenate([eo_b, eo_b, eo_low], axis=0),
        )
        act_buf[micro, step] = (h + mixed).astype(BF)
        for m in range(micros):
            pl.when(micro == m)(functools.partial(acts[m].start, step))
        dw2 = nt(jnp.concatenate([eo_b, eo_low], axis=0), cot_b)
        dw = dw2[:gate_rows] + dw2[gate_rows:] + nt(dmg, n2)
        wdw = gate * dw
        dlog = (wdw - gate * jnp.sum(wdw, axis=1, keepdims=True)).astype(BF)
        dn2 = tn(
            jnp.concatenate([gate_b, dlog], axis=0),
            jnp.concatenate([dmg, wc_ref[...]], axis=0),
        )
        small[0:gate_rows, :] += nn(dlog, n2)
        small[gate_rows : gate_rows + 1, :] += jnp.sum(dn2 * z, axis=0, keepdims=True)
        a = dn2 * g2_ref[...]
        dh = dout + r2_ * (a - z * jnp.mean(a * z, axis=-1, keepdims=True))
        dh_all[micro, at, :] = dh
        da = dh.astype(BF)
        dob_b = nt(da, wo_ref[...]).astype(BF)
        dob[micro, at, :] = dob_b
        ob = ob_ref[0]
        go_acc[...] += tn(ob, da)
        prod = dob_b.astype(F32) * ob.astype(F32)
        high = prod.astype(BF)
        low = (prod - high.astype(F32)).astype(BF)
        heads = head_rows(delta.shape[1], width)
        delta[micro, :, at] = nt(heads, high) + nt(heads, low)
        x = x_ref[0, step].astype(F32)
        n1_all[micro, at, :] = (x * rms(x) * g1_ref[...]).astype(BF)

    for m in range(1, micros):
        for i in range(blocks):
            pl.when(now == m * blocks + i)(
                functools.partial(fill_bias, bias.at[i], start_ref[i], True, i)
            )

    masks = head_masks()

    def attend(m):
        hp = step
        packed = m > 0
        lanes = rows_of(hp, pair_lanes)
        for i in range(blocks):
            low, count = key_range(packed, i)
            at = slice(i * BLOCK, (i + 1) * BLOCK)
            q_pair, dob_pair = q_ref[0, at, :], dob[m, at, lanes]
            k_pair, v_pair = k_ref[0, low : low + count, :], v_ref[0, low : low + count, :]
            dk_sum = dv_sum = None
            dqs = []
            for h in range(2):
                qm, dm = q_pair * masks[h], dob_pair * masks[h]
                scores = add_bias(nt(k_pair, qm), bias.at[i] if packed else bias_own, packed, count)
                p = jnp.exp(scores * SCALE - lse_ref[0, pl.ds(hp * 2 + h, 1), at])
                dp_ = nt(v_pair, dm)
                ds = (p * (dp_ - delta[m, pl.ds(hp * 2 + h, 1), at])).astype(BF)
                kt = kt_ref[0, h * HEAD_DIM : (h + 1) * HEAD_DIM, low : low + count]
                dqs.append(nn(kt, ds) * SCALE)
                dk_part, dv_part = nn(ds, qm), nn(p.astype(BF), dm)
                dk_sum = dk_part if dk_sum is None else dk_sum + dk_part
                dv_sum = dv_part if dv_sum is None else dv_sum + dv_part
            old = i * BLOCK - low
            dk_acc[at, :] = dk_sum[old:]
            dv_acc[at, :] = dv_sum[old:]
            if old:
                dk_acc[low : i * BLOCK, :] += dk_sum[:old]
                dv_acc[low : i * BLOCK, :] += dv_sum[:old]
            dq_all[at, lanes] = jnp.concatenate(dqs, axis=0).T.astype(BF)
        dk = (dk_acc[...] * SCALE).astype(BF)
        dv = dv_acc[...].astype(BF)
        dk_all[:, lanes] = dk
        dv_all[:, lanes] = dv
        g = tn(jnp.concatenate([dq_all[:, lanes], dk, dv], axis=1), n1_all[m])
        if packed:
            gacc[hp] += g
        else:
            gacc[hp] = g

    for m in range(micros):
        in_phase = (now >= lead) & (micro == m) & (step < pairs)
        pl.when(in_phase)(functools.partial(attend, m))

    in_third = (now >= lead) & (step >= pairs)
    i = blk ^ (nb - 1 - (step - pairs))

    @pl.when(in_third)
    def _():
        at = rows_of(i, BLOCK)
        x = x_ref[0, i].astype(F32)
        r1_ = rms(x)
        z1 = x * r1_
        dn1 = (
            nt(dq_all[at, :], wq_ref[...]) + nt(dk_all[at, :], wk_ref[...]) + nt(dv_all[at, :], wv_ref[...])
        )
        small[gate_rows + 8 : gate_rows + 9, :] += jnp.sum(dn1 * z1, axis=0, keepdims=True)
        b = dn1 * g1_ref[...]
        gi = dh_all[micro, at, :] + r1_ * (b - z1 * jnp.mean(b * z1, axis=-1, keepdims=True))
        gi_buf[micro, i] = gi.astype(BF)

    final = lead + micros * span - 1
    tasks = {}

    def after(at, task, *args):
        tasks.setdefault(min(at, final), []).append(functools.partial(task, *args))

    def far_block(d):
        gis[0].copy(d).start()

    for n, gap in enumerate((0, 2, 5, 8, 10, 12)):
        after(lead - 1 + gap, stages[n], 0)
    for c in range(1, pairs):
        for n, gap in enumerate((0, 1, 3, 5, 6, 7)):
            after(last + c - 1 + gap, stages[n], c)
    c = pairs
    after(last + c - 1, chunk_start, c)
    after(last + c, chunk_b, c)
    after(last + c + 2, chunk_z, c)
    after(blocks, reduced, 0)
    after(lead, reduced, 1)
    after(lead, own_y, 0)
    after(lead + 2, whole_slice, 0)
    after(lead + 2, own_y, 1)
    after(last - 1, slice_y, 0)
    after(last - 1, whole_slice, 1)
    after(last + pairs - 2, slice_y, 1)
    after(last + pairs - 2, slice_x, 0)
    after(final, slice_x, 1)
    after(final, slice_d, 0)
    for d in range(2, nb):
        after(last + 2 * (d - 2), far_block, d)
    for at, todo in tasks.items():
        if at < final:

            @pl.when(now == at)
            def _(todo=todo):
                for task in todo:
                    task()

    @pl.when(in_third)
    def _():
        for m in range(micros):
            pl.when(micro == m)(functools.partial(gis[m].start, i, 2 if m == 0 else nb))

    @pl.when(now == final)
    def _():
        per = gate_rows // 2
        few[0] = jnp.concatenate(
            [jnp.sum(small[n * per : (n + 1) * per, :], axis=0, keepdims=True) for n in range(2)]
            + [small[gate_rows : gate_rows + 1, :], small[gate_rows + 8 : gate_rows + 9, :]]
            + [jnp.zeros((4, width), F32)],
            axis=0,
        )
        plan.start("sb")
        for task in tasks[final]:
            task()
        chunk_g(c)
        plan.arrived("sb")
        few[1] = pair_sum([few[0]] + [rs[n] for n in range(len(near))])
        plan.start("sz")
        chunk_h(c)
        slice_d(1)
        chunk_done(c)
        plan.arrived("sz")
        small_ref[...] = pair_sum([few[1]] + [rs[len(near) + d - 1] for d in others])
        for w in both:
            for name in "oyxd":
                plan.arrived(f"c{name}{w}")
        for n in range(pairs + 1):
            out_copy(n).wait()
        for name in plan.sets:
            plan.sent(name)
        for r in acts + gis:
            r.wait()


def whole(shape):
    return pl.BlockSpec(shape, lambda *_: (0,) * len(shape))


def held(shape):
    return pl.BlockSpec(shape, lambda *_: (0,) * len(shape), pipeline_mode=pl.Buffered(1))


ANY = pl.BlockSpec(memory_space=pl.ANY)
DMA = pltpu.SemaphoreType.DMA


def shaped(shape, dtype):
    return jax.ShapeDtypeStruct(shape, dtype)


def params(number):
    return pltpu.CompilerParams(
        vmem_limit_bytes=VMEM_LIMIT, collective_id=number, has_side_effects=True
    )


def forward_call(x, seg, cot, g1, wq, wk, wv, wo, g2, wc):
    nb = lax.axis_size("blk")
    micros, _, rows_in, width = x.shape
    length = nb * rows_in
    blocks = length // BLOCK
    assert x.shape[1] == nb and rows_in == BLOCK
    rows = wc.shape[0]
    heads = width // HEAD_DIM
    per = BLOCK // GROUP
    experts = rows // per
    span = 2 * blocks
    phase = lambda s: jnp.maximum(s % span - blocks, 0)
    whole_micro = lambda a, b: pl.BlockSpec((1, a, b), lambda s: (s // span, 0, 0))
    flat = lambda s: (s // span) * blocks + phase(s)
    moves = 2 * micros + 1
    return pl.pallas_call(
        functools.partial(forward_kernel, micros, blocks, nb),
        grid=(micros * span,),
        in_specs=[ANY, ANY, ANY] + [held(a.shape) for a in (g1, wq, wk, wv, wo, g2, wc)],
        out_specs=[
            whole_micro(length, width), whole_micro(length, width), whole_micro(length, width),
            whole_micro(width, length),
            pl.BlockSpec((1, BLOCK, width), lambda s: (s // span, phase(s), 0)),
            pl.BlockSpec((1, heads, BLOCK), lambda s: (s // span, 0, phase(s))),
            pl.BlockSpec((1, BLOCK, width), lambda s: (s // span, phase(s), 0)),
            pl.BlockSpec((rows, BLOCK), lambda s: (0, flat(s))),
            pl.BlockSpec((experts, per, width), lambda s: (0, flat(s), 0)),
            whole((blocks, 1, BLOCK)), ANY, ANY,
        ],
        out_shape=[
            shaped((micros, length, width), BF), shaped((micros, length, width), BF),
            shaped((micros, length, width), BF), shaped((micros, width, length), BF),
            shaped((micros, length, width), BF), shaped((micros, heads, length), F32),
            shaped((micros, length, width), F32), shaped((rows, micros * length), F32),
            shaped((experts, micros * length // GROUP, width), F32),
            shaped((blocks, 1, BLOCK), jnp.int32), shaped(x.shape, BF), shaped(x.shape, BF),
        ],
        scratch_shapes=[
            pltpu.VMEM(x.shape, BF), pltpu.VMEM(seg.shape, seg.dtype),
            pltpu.VMEM((length, BLOCK), F32), pltpu.VMEM((BLOCK, width), F32),
            pltpu.VMEM((heads, BLOCK), F32), pltpu.VMEM((width, width), BF),
            DMA((moves + 1,)), DMA((moves * (nb - 1),)), DMA((moves * (nb - 1),)),
        ],
        compiler_params=params(1),
        name="attention_forward",
    )(x, seg, cot, g1, wq, wk, wv, wo, g2, wc)


def experts_call(mg, gate, cot, w_in, w_back):
    micros, nb, _, width = cot.shape
    experts, groups, _ = mg.shape
    ff = w_in.shape[2]
    blocks = gate.shape[1] // BLOCK // micros
    chunk = min(CHUNK, ff)
    by_expert = lambda n: pl.BlockSpec((1, n, width), lambda e, c: (e, 0, 0))
    members = 2 * nb
    return pl.pallas_call(
        functools.partial(experts_kernel, micros, blocks, nb),
        grid=(experts, ff // chunk),
        in_specs=[
            held(mg.shape), held(gate.shape), held(cot.shape),
            pl.BlockSpec((1, width, chunk), lambda e, c: (e, 0, c)),
            pl.BlockSpec((1, chunk, width), lambda e, c: (e, c, 0)),
        ],
        out_specs=[by_expert(groups)] * 2 + [whole((2, members * groups, width))],
        out_shape=[shaped((experts, groups, width), F32)] * 2
        + [shaped((2, members * groups, width), BF)],
        scratch_shapes=[
            pltpu.VMEM((experts, 2, groups, width), BF),
            pltpu.VMEM((members - 1, 2, groups, width), BF), DMA((members - 1,)), DMA((members - 1,)),
        ],
        compiler_params=params(2),
        name="experts",
    )(mg, gate, cot, w_in, w_back)


def backward_call(x, cot, h, gate, eo, dmg, ob, lse, q, k, v, kt, start, g1, g2, wc, wq, wk, wv, wo,
                  factors, w_in, w_back):
    micros, nb, _, width = x.shape
    planes = lax.axis_size("dp") // 2
    length = q.shape[1]
    blocks = length // BLOCK
    rows = wc.shape[0]
    per = BLOCK // GROUP
    experts = rows // per
    heads = width // HEAD_DIM
    pairs = heads // 2
    ff = w_in.shape[2]
    cut = ff // nb
    assert cut == width
    members = len(plane_steps(nb)) + 1
    lead, span = micros * blocks, blocks + pairs
    flat = lambda s: jnp.minimum(s, lead - 1)
    m_late = lambda s: jnp.maximum(s - lead, 0) // span
    m_of = lambda s: jnp.where(s < lead, s // blocks, m_late(s))
    pair_of = lambda s: jnp.minimum(jnp.maximum(s - lead, 0) % span, pairs - 1)
    row_block = pl.BlockSpec((1, BLOCK, width), lambda s: (flat(s) // blocks, flat(s) % blocks, 0))
    group_block = pl.BlockSpec((experts, per, width), lambda s: (0, flat(s), 0))
    pair_block = pl.BlockSpec((1, length, 2 * HEAD_DIM), lambda s: (m_late(s), 0, pair_of(s)))
    piece = (2, width // planes, cut)
    chunk = width
    chunks = pairs + 1
    half = chunk // 2
    quarter = half // members
    reach = max(key_range(True, i)[1] for i in range(blocks))
    small = (rows + 16, width)
    few = (8, width)
    vm = pltpu.VMEM
    copies = 96 + 16 * chunks + 32 * planes
    return pl.pallas_call(
        functools.partial(backward_kernel, micros, blocks, nb, planes),
        grid=(lead + micros * span,),
        in_specs=[
            pl.BlockSpec((1, nb, BLOCK, width), lambda s: (m_of(s), 0, 0, 0)),
            pl.BlockSpec((1, 1, BLOCK, width), lambda s: (flat(s) // blocks, flat(s) % blocks, 0, 0)),
            row_block,
            pl.BlockSpec((rows, BLOCK), lambda s: (0, flat(s))),
            group_block, group_block, row_block,
            pl.BlockSpec((1, heads, length), lambda s: (m_late(s), 0, 0)),
            pair_block, pair_block, pair_block,
            pl.BlockSpec((1, 2 * HEAD_DIM, length), lambda s: (m_late(s), pair_of(s), 0)),
        ] + [held(a.shape) for a in (start, g1, g2, wc, wq, wk, wv, wo, factors)] + [ANY, ANY],
        out_specs=[ANY, ANY, ANY, whole(few), ANY, ANY],
        out_shape=[
            shaped(x.shape, BF), shaped(x.shape, BF), shaped((chunks, chunk, width), BF),
            shaped(few, F32), shaped(w_in.shape, BF), shaped(w_back.shape, BF),
        ],
        scratch_shapes=[
            vm((micros, length, width), F32), vm((micros, length, width), BF),
            vm((micros, length, width), BF), vm((micros, heads, length), F32), vm((length, width), BF), vm((length, width), BF),
            vm((length, width), BF), vm((length, 2 * HEAD_DIM), F32), vm((length, 2 * HEAD_DIM), F32),
            vm((pairs, 6 * HEAD_DIM, width), F32), vm((width, width), F32), vm((BLOCK, BLOCK), F32),
            vm((blocks, reach, BLOCK), F32),
            vm(x.shape, BF), vm(x.shape, BF), vm((width, cut), BF), vm((cut, width), BF),
            vm((2, planes) + piece[1:], BF), vm((2, planes - 1) + piece[1:], BF), vm(piece, BF),
            vm((chunks, half, width), BF), vm((chunks, half, width), BF),
            vm((chunks, members - 1, quarter, width), BF), vm((chunks, members - 1, quarter, width), BF),
            vm((chunks, quarter, width), BF), vm((chunks, planes - 1, quarter, width), BF),
            vm((chunks, chunk, width), BF), vm(small, F32), vm((2,) + few, F32),
            vm((2 * nb + planes - 2,) + few, F32),
            DMA((2 * micros,)), DMA((5 + pairs,)), DMA((2 * micros * (nb - 1),)),
            DMA((2 * micros * (nb - 1),)), DMA((copies,)), DMA((copies,)),
        ],
        compiler_params=params(3),
        name="attention_backward",
    )(x, cot, h, gate, eo, dmg, ob, lse, q, k, v, kt, start, g1, g2, wc, wq, wk, wv, wo, factors, w_in,
      w_back)


def widen_kernel(flat_ref, one_ref, gin_ref, gback_ref, q_ref, k_ref, v_ref, o_ref, gin_out, gback_out):
    gin_out[...] = gin_ref[...].astype(F32)
    gback_out[...] = gback_ref[...].astype(F32)
    lanes = q_ref.shape[1]
    for n, ref in enumerate((q_ref, k_ref, v_ref)):
        ref[...] = flat_ref[0, n * lanes : (n + 1) * lanes, :].astype(F32).T
    o_ref[...] = one_ref[0].astype(F32)


def widen_call(flat, gin, gback):
    experts, width, ff = gin.shape
    lanes = 2 * HEAD_DIM
    pairs = width // lanes
    cuts = ff // width
    pair = lambda s: jnp.minimum(s, pairs - 1)
    tall = pl.BlockSpec((width, lanes), lambda s: (0, pair(s)))
    in_block = pl.BlockSpec((1, width, width), lambda s: (s // cuts, 0, s % cuts))
    back_block = pl.BlockSpec((1, width, width), lambda s: (s // cuts, s % cuts, 0))
    square = shaped((width, width), F32)
    return pl.pallas_call(
        widen_kernel,
        grid=(experts * cuts,),
        in_specs=[
            pl.BlockSpec((1,) + flat.shape[1:], lambda s: (1 + pair(s), 0, 0)),
            pl.BlockSpec((1, lanes, width), lambda s: (0, pair(s), 0)), in_block, back_block,
        ],
        out_specs=[tall, tall, tall, pl.BlockSpec((lanes, width), lambda s: (pair(s), 0)), in_block, back_block],
        out_shape=[square] * 4 + [shaped(gin.shape, F32), shaped(gback.shape, F32)],
        compiler_params=pltpu.CompilerParams(vmem_limit_bytes=VMEM_LIMIT),
        name="gradients_out",
    )(flat, flat, gin, gback)


def local(block_input, segment_ids, gain_one, w_query, w_key, w_value, w_out, gain_two, w_ctrl,
          w_in, w_back, cotangent):
    micros, seqs, rows, width = block_input.shape
    experts, _, ff = w_in.shape
    nb = lax.axis_size("blk")
    per = BLOCK // GROUP
    g1, g2 = gain_one.reshape(1, width), gain_two.reshape(1, width)
    wc = jnp.repeat(w_ctrl.T, per, axis=0)
    seg = segment_ids.reshape(nb, 2, rows // 2)
    q, k, v, kt, ob, lse, h, gate, mg, start, x, cot = forward_call(
        block_input, seg, cotangent, g1, w_query, w_key, w_value, w_out, g2, wc
    )
    eo, dmg, factors = experts_call(mg, gate, cot, w_in, w_back)
    acts, gis, flat, small, grad_in, grad_back = backward_call(
        x, cot, h, gate, eo, dmg, ob, lse, q, k, v, kt, start, g1, g2, wc, w_query, w_key, w_value,
        w_out, factors, w_in, w_back,
    )
    gq, gk, gv, go, grad_in, grad_back = widen_call(flat, grad_in, grad_back)
    return acts, gis, small[3], gq, gk, gv, go, small[2], small[:experts].T, grad_in, grad_back


def solution(mesh):
    data = P(None, "dp", "blk", None)
    in_specs = (data, P("dp", "blk")) + (P(),) * 9 + (data,)
    out_specs = (data, data) + (P(),) * 9
    return jax.shard_map(local, mesh=mesh, in_specs=in_specs, out_specs=out_specs, check_vma=False)
```

```python
import functools

import jax
import jax.numpy as jnp
from jax import lax
from jax.experimental import pallas as pl
from jax.experimental.pallas import tpu as pltpu
from jax.sharding import PartitionSpec as P

HEAD_DIM = 64
GROUP = 32
EPSILON = 1e-05
BLOCK = 256
CHUNK = 512
SCALE = 0.125
MASKED = -1e30
VMEM_LIMIT = 60 * 1024 * 1024
BF = jnp.bfloat16
F32 = jnp.float32
MESH = pl.DeviceIdType.MESH


def dot(a, b, ca, cb):
    return lax.dot_general(a, b, (((ca,), (cb,)), ((), ())), preferred_element_type=F32)


def nn(a, b):
    return dot(a, b, 1, 0)


def nt(a, b):
    return dot(a, b, 1, 1)


def tn(a, b):
    return dot(a, b, 0, 0)


def key_range(packed, i):
    low = max(0, i * BLOCK - BLOCK - BLOCK // 2) if packed else 0
    return low, (i + 1) * BLOCK - low


def head_masks():
    lane = lax.broadcasted_iota(jnp.int32, (1, 2 * HEAD_DIM), 1)
    first = (lane < HEAD_DIM).astype(F32).astype(BF)
    return first, (lane >= HEAD_DIM).astype(F32).astype(BF)


def group_match(rows, tokens):
    row = lax.broadcasted_iota(jnp.int32, (rows, tokens), 0)
    col = lax.broadcasted_iota(jnp.int32, (rows, tokens), 1)
    return (row % (tokens // GROUP)) == (col // GROUP)


def fill_bias(bias_ref, start_ref, packed, i):
    low, count = key_range(packed, i)
    q_pos = i * BLOCK + lax.broadcasted_iota(jnp.int32, (1, BLOCK), 1)
    if packed:
        k_pos = low + lax.broadcasted_iota(jnp.int32, (count, BLOCK), 0)
        allowed = (k_pos <= q_pos) & (k_pos >= start_ref[...])
        bias_ref[0:count, :] = jnp.where(allowed, 0.0, MASKED)
    else:
        k_pos = i * BLOCK + lax.broadcasted_iota(jnp.int32, (BLOCK, BLOCK), 0)
        bias_ref[0:BLOCK, :] = jnp.where(k_pos <= q_pos, 0.0, MASKED)


def add_bias(scores, bias_ref, packed, count):
    if packed:
        return scores + bias_ref[0:count, :]
    last = scores[count - BLOCK :, :] + bias_ref[0:BLOCK, :]
    if count == BLOCK:
        return last
    return jnp.concatenate([scores[: count - BLOCK, :], last], axis=0)


def rms(values):
    return lax.rsqrt(jnp.mean(values * values, axis=-1, keepdims=True) + EPSILON)


def peer(axis, me, d):
    return {axis: me ^ d}


def arrive(partners):
    barrier = pltpu.get_barrier_semaphore()
    for p in partners:
        pl.semaphore_signal(barrier, inc=1, device_id=p, device_id_type=MESH)
    pl.semaphore_wait(barrier, len(partners))


def remote(src, dst, sems, k, where):
    return pltpu.make_async_remote_copy(
        src_ref=src, dst_ref=dst, send_sem=sems[0].at[k], recv_sem=sems[1].at[k],
        device_id=where, device_id_type=MESH,
    )


class Exchange:
    def __init__(self, nb, src, dst, own, sems, base):
        self.nb, self.src, self.dst, self.own, self.sems, self.base = nb, src, dst, own, sems, base
        self.me = lax.axis_index("blk")

    def local(self):
        return pltpu.make_async_copy(
            self.src.at[self.me], self.dst.at[self.me], self.own.at[self.base]
        )

    def copy(self, d):
        return remote(
            self.src.at[self.me ^ d], self.dst.at[self.me], self.sems,
            self.base * (self.nb - 1) + d - 1, peer("blk", self.me, d),
        )

    def start(self):
        self.local().start()
        for d in range(1, self.nb):
            self.copy(d).start()

    def wait(self):
        self.local().wait()
        for d in range(1, self.nb):
            self.copy(d).wait()


def unit(n):
    row = lax.broadcasted_iota(jnp.int32, (n, n), 0)
    col = lax.broadcasted_iota(jnp.int32, (n, n), 1)
    return (row == col).astype(F32).astype(BF)


def split_three(a):
    high = a.astype(BF)
    rest = a - high.astype(F32)
    mid = rest.astype(BF)
    return [high, mid, (rest - mid.astype(F32)).astype(BF)]


def head_rows(heads, width):
    row = lax.broadcasted_iota(jnp.int32, (heads, width), 0)
    col = lax.broadcasted_iota(jnp.int32, (heads, width), 1)
    return (row == col // HEAD_DIM).astype(F32).astype(BF)


def forward_kernel(micros, blocks, nb, x_src, seg_src, cot_src, g1_ref, wq_ref, wk_ref, wv_ref, wo_ref,
                   g2_ref, wc_ref, q_ref, k_ref, v_ref, kt_ref, ob_ref, lse_ref, h_ref, gate_ref,
                   mg_ref, start_ref, x_out, cot_out, x_all, seg_all, bias, o_acc, sums, eye, own,
                   send_sem, recv_sem):
    sems = (send_sem, recv_sem)
    now = pl.program_id(0)
    span = 2 * blocks
    micro, step = now // span, now % span
    width = wo_ref.shape[0]
    pairs = width // (2 * HEAD_DIM)
    me = lax.axis_index("blk")
    xs = [Exchange(nb, x_src.at[m], x_all.at[m], own, sems, m) for m in range(micros)]
    segs = Exchange(nb, seg_src, seg_all, own, sems, micros)
    cots = [
        Exchange(nb, cot_src.at[m], cot_out.at[m], own, sems, micros + 1 + m) for m in range(micros)
    ]
    keep = pltpu.make_async_copy(x_all, x_out, own.at[2 * micros + 1])

    @pl.when(now == 0)
    def _():
        xs[0].local().start()
        eye[...] = unit(width)
        arrive([peer("blk", me, d) for d in range(1, nb)])
        for d in range(1, nb):
            xs[0].copy(d).start()

    @pl.when(step < blocks)
    def _():
        block = me ^ step
        for m in range(micros):
            pl.when((micro == m) & (step == 0))(xs[m].local().wait)
            for d in range(1, nb):
                pl.when((micro == m) & (step == d))(xs[m].copy(d).wait_recv)
        x = x_all[micro, block].astype(F32)
        n1 = (x * rms(x) * g1_ref[...]).astype(BF)
        at = pl.ds(pl.multiple_of(block * BLOCK, BLOCK), BLOCK)
        q_ref[0, at, :] = nn(n1, wq_ref[...]).astype(BF)
        k = nn(n1, wk_ref[...]).astype(BF)
        k_ref[0, at, :] = k
        v_ref[0, at, :] = nn(n1, wv_ref[...]).astype(BF)
        kt_ref[0, :, at] = nt(eye[...], k).astype(BF)

    @pl.when(now == nb - 1)
    def _():
        segs.start()
        for m in range(1, micros):
            xs[m].start()

    @pl.when(now == blocks)
    def _():
        for c in cots:
            c.start()

    @pl.when(now == span)
    def _():
        segs.wait()
        counts = [
            jnp.sum(jnp.sum((seg_all[...] < d).astype(F32), axis=0), keepdims=True)
            for d in range(1, nb * seg_all.shape[1] * seg_all.shape[2] // BLOCK)
        ]
        for b in range(blocks):
            seg = jnp.concatenate([seg_all[b, n : n + 1, :] for n in range(seg_all.shape[1])], axis=1)
            start = jnp.zeros(seg.shape, F32)
            for d, count in enumerate(counts):
                start = jnp.where(seg == d + 1, count, start)
            start_ref[b] = start.astype(jnp.int32)

    masks = head_masks()

    def attend(packed, i):
        low, count = key_range(packed, i)
        fill_bias(bias, start_ref[i], packed, i)
        for hp in range(pairs):
            lanes = slice(hp * 2 * HEAD_DIM, (hp + 1) * 2 * HEAD_DIM)
            q_pair = q_ref[0, i * BLOCK : (i + 1) * BLOCK, lanes]
            k_pair = k_ref[0, low : low + count, lanes]
            v_pair = v_ref[0, low : low + count, lanes]
            o_pair = None
            for h in range(2):
                scores = add_bias(nt(k_pair, q_pair * masks[h]), bias, packed, count)
                top = jnp.max(scores, axis=0, keepdims=True)
                p = jnp.exp((scores - top) * SCALE)
                total = jnp.sum(p, axis=0, keepdims=True)
                o = tn(p.astype(BF), v_pair * masks[h])
                o_pair = o if o_pair is None else o_pair + o
                sums[hp * 2 + h : hp * 2 + h + 1, :] = 1.0 / total
                lse_ref[0, hp * 2 + h : hp * 2 + h + 1, :] = top * SCALE + jnp.log(total)
            o_acc[:, lanes] = o_pair

    for m in range(micros):
        for i in range(blocks):
            pl.when(now == m * span + blocks + i)(functools.partial(attend, m > 0, i))

    @pl.when(step >= blocks)
    def _():
        heads = head_rows(sums.shape[0], width)
        scale = tn(
            jnp.concatenate(split_three(sums[...]), axis=0), jnp.concatenate([heads] * 3, axis=0)
        )
        ob = (o_acc[...] * scale).astype(BF)
        ob_ref[0] = ob
        h = x_all[micro, step - blocks].astype(F32) + nn(ob, wo_ref[...])
        h_ref[0] = h
        n2 = (h * rms(h) * g2_ref[...]).astype(BF)
        logits = nt(wc_ref[...], n2)
        rows = logits.shape[0]
        match = group_match(rows, BLOCK)
        logits = jnp.where(match, logits, MASKED)
        e = jnp.where(match, jnp.exp(logits - jnp.max(logits, axis=1, keepdims=True)), 0.0)
        gate = e / jnp.sum(e, axis=1, keepdims=True)
        gate_ref[...] = gate
        mg = nn(gate.astype(BF), n2).astype(BF).astype(F32)
        half = rows // mg_ref.shape[0]
        for j in range(mg_ref.shape[0]):
            mg_ref[j] = mg[j * half : (j + 1) * half]

    @pl.when(now == span + nb)
    def _():
        keep.start()

    @pl.when(now == micros * span - 1)
    def _():
        keep.wait()
        for x in xs:
            for d in range(1, nb):
                x.copy(d).wait_send()
        for c in cots:
            c.wait()


def gelu_both(u):
    c = 0.7978845608028654
    t = jnp.tanh(c * (u + 0.044715 * (u * u * u)))
    act = 0.5 * u * (1.0 + t)
    slope = 0.5 * (1.0 + t) + 0.5 * u * (1.0 - t * t) * (c * (1.0 + 3 * 0.044715 * (u * u)))
    return act, slope


def same_plane(far, d):
    return {"dp": lax.axis_index("dp") ^ far, "blk": lax.axis_index("blk") ^ d}


def plane_steps(nb):
    return [(far, d) for far in (0, 1) for d in range(0, nb, 2) if far or d]


def experts_kernel(micros, blocks, nb, *refs):
    mg_ref, gate_ref, cot_ref, win_ref, wback_ref = refs[:5]
    eo_ref, dmg_ref, all_ref, factors, gathered, send_sem, recv_sem = refs[5:]
    sems = (send_sem, recv_sem)
    e, c = pl.program_id(0), pl.program_id(1)
    at = e * pl.num_programs(1) + c
    last = pl.num_programs(0) * pl.num_programs(1) - 1
    per = BLOCK // GROUP
    n_exp = factors.shape[0]
    groups = micros * blocks * per
    blk = lax.axis_index("blk")
    kind = blk % n_exp
    steps = [(far, d) for far in (0, 1) for d in range(nb) if far or d]

    def plane_copy(n):
        far, d = steps[n]
        return remote(factors.at[kind ^ (d & 1)], gathered.at[n], sems, n, same_plane(far, d))

    @pl.when(at == 0)
    def _():
        deo = []
        for m in range(micros):
            for i in range(blocks):
                at_rows = (m * blocks + i) * BLOCK
                deo.append(nn(gate_ref[:, at_rows : at_rows + BLOCK].astype(BF), cot_ref[m, i]))
        for j in range(n_exp):
            factors[j, 0] = mg_ref[j].astype(BF)
            factors[j, 1] = jnp.concatenate(
                [d[j * per : (j + 1) * per] for d in deo], axis=0
            ).astype(BF)
        arrive([same_plane(*s) for s in steps])
        for n in range(len(steps)):
            plane_copy(n).start()

    mg, deo = factors[e, 0], factors[e, 1]
    act, slope = gelu_both(nn(mg, win_ref[0]))
    eo_part = nn(act.astype(BF), wback_ref[0])
    du = (slope * nt(deo, wback_ref[0])).astype(BF)
    dmg_part = nt(du, win_ref[0])

    @pl.when(c == 0)
    def _():
        eo_ref[0] = eo_part
        dmg_ref[0] = dmg_part

    @pl.when(c > 0)
    def _():
        eo_ref[0] += eo_part
        dmg_ref[0] += dmg_part

    @pl.when(at == last)
    def _():
        for n in range(len(steps)):
            plane_copy(n).wait()
        for n in range(len(steps) + 1):
            piece = factors[kind] if n == 0 else gathered[n - 1]
            for f in range(2):
                all_ref[f, n * groups : (n + 1) * groups, :] = piece[f]


class Return:
    def __init__(self, nb, buf, out, own, sems, base):
        self.nb, self.buf, self.out, self.own, self.sems, self.base = nb, buf, out, own, sems, base
        self.me = lax.axis_index("blk")

    def local(self):
        return pltpu.make_async_copy(
            self.buf.at[self.me], self.out.at[self.me], self.own.at[self.base]
        )

    def copy(self, d):
        return remote(
            self.buf.at[self.me ^ d], self.out.at[self.me], self.sems,
            self.base * (self.nb - 1) + d - 1, peer("blk", self.me, d),
        )

    def start(self, i, reach=None):
        pl.when(i == self.me)(lambda: self.local().start())
        for d in range(1, reach or self.nb):
            pl.when(i == (self.me ^ d))(lambda d=d: self.copy(d).start())

    def wait(self):
        self.local().wait()
        for d in range(1, self.nb):
            self.copy(d).wait()


class Plan:
    def __init__(self, sems):
        self.sems, self.count, self.sets = sems, 0, {}

    def add(self, name, makers):
        self.sets[name] = list(enumerate(makers, self.count))
        self.count += len(makers)

    def each(self, name):
        for k, maker in self.sets[name]:
            src, dst, where = maker()
            yield remote(src, dst, self.sems, k, where)

    def start(self, name):
        for c in self.each(name):
            c.start()

    def arrived(self, name):
        for c in self.each(name):
            c.wait_recv()

    def sent(self, name):
        for c in self.each(name):
            c.wait_send()


def other_plane(d):
    return {"dp": lax.axis_index("dp") ^ (2 * d)}


def pair_sum(parts):
    while len(parts) > 1:
        parts = [parts[n] + parts[n + 1] for n in range(0, len(parts), 2)]
    return parts[0]


def rows_of(n, size):
    return pl.ds(pl.multiple_of(n * size, size), size)


def backward_kernel(micros, blocks, nb, planes, x_ref, cot_ref, h_ref, gate_ref, eo_ref, dmg_ref, ob_ref,
                    lse_ref, q_ref, k_ref, v_ref, kt_ref, start_ref, g1_ref, g2_ref, wc_ref, wq_ref,
                    wk_ref, wv_ref, wo_ref, factors, win_hbm, wback_hbm, act_ref, gi_ref, flat_ref,
                    small_ref, gin, gback, dh_all, n1_all, dob, delta, dq_all, dk_all, dv_all, dk_acc,
                    dv_acc, gacc, go_acc, bias_own, bias, act_buf, gi_buf, win, wback, ours, theirs, piece, s1,
                    r1, s2, r2, s3, r3, fl, small, few, rs, own, load_sem, ret_send, ret_recv, send_sem,
                    recv_sem):
    now = pl.program_id(0)
    width = wo_ref.shape[0]
    pairs = width // (2 * HEAD_DIM)
    pair_lanes = 2 * HEAD_DIM
    lead, span = micros * blocks, blocks + pairs
    micro = jnp.where(now < lead, now // blocks, (now - lead) // span)
    step = jnp.where(now < lead, now % blocks, (now - lead) % span)
    last = lead + (micros - 1) * span
    blk, dp = lax.axis_index("blk"), lax.axis_index("dp")
    kind, plane = blk % 2, dp // 2
    steps = plane_steps(nb)
    members = len(steps) + 1
    core = lambda: peer("blk", lax.axis_index("blk"), 1)

    def part_of(far, d):
        return ((blk ^ d) // 2) + (nb // 2) * ((dp % 2) ^ far)

    part = part_of(0, 0)
    cut = win.shape[1]
    rets = (ret_send, ret_recv)
    acts = [Return(nb, act_buf.at[m], act_ref.at[m], own, rets, 2 * m) for m in range(micros)]
    gis = [Return(nb, gi_buf.at[m], gi_ref.at[m], own, rets, 2 * m + 1) for m in range(micros)]
    columns = rows_of(part, cut)
    loads = [
        lambda: pltpu.make_async_copy(win_hbm.at[kind, :, columns], win, load_sem.at[0]),
        lambda: pltpu.make_async_copy(wback_hbm.at[kind, columns, :], wback, load_sem.at[1]),
    ]
    rows = width // planes

    def window(which, p, z):
        if which == 0:
            return gin.at[kind, rows_of(z, rows), rows_of(p, cut)]
        at = pl.multiple_of(p * cut + z * rows, rows)
        return gback.at[kind, pl.ds(at, rows), :]

    def slab(which, p):
        if which == 0:
            return gin.at[kind, :, rows_of(p, cut)]
        return gback.at[kind, rows_of(p, cut), :]

    mine = [
        lambda w=w: pltpu.make_async_copy(piece.at[w], window(w, part, plane), load_sem.at[2 + w])
        for w in range(2)
    ]
    y_peer, x_peer = steps[0], steps[1]
    others = range(1, planes)
    both = range(2)
    plan = Plan((send_sem, recv_sem))
    for w in both:
        plan.add(f"rs{w}", [
            lambda d=d, w=w: (ours.at[w, plane ^ d], theirs.at[w, d - 1], other_plane(d)) for d in others
        ])
        plan.add(f"z{w}", [
            lambda d=d, w=w: (piece.at[w], window(w, part, plane), other_plane(d)) for d in others
        ])
        for name, to in ((f"y0{w}", y_peer), (f"x0{w}", x_peer)):
            plan.add(name, [
                lambda w=w, to=to: (piece.at[w], window(w, part, plane), same_plane(*to))
            ])

    def onward(p, z, w, to):
        return window(w, p, z), window(w, p, z), same_plane(*to)

    part_y = part_of(*y_peer)
    for w in both:
        plan.add(f"yx0{w}", [lambda w=w: onward(part_y, plane, w, x_peer)])
        for name, p, to in ((f"y1{w}", part, y_peer), (f"x1{w}", part, x_peer), (f"yx1{w}", part_y, x_peer)):
            plan.add(name, [
                lambda d=d, w=w, p=p, to=to: onward(p, plane ^ d, w, to) for d in others
            ])
        for name, p in zip("oyxd", [part] + [part_of(*t) for t in steps]):
            plan.add(f"c{name}{w}", [lambda w=w, p=p: (slab(w, p), slab(w, p), core())])

    sizes = [width] + [3 * pair_lanes] * pairs
    halves = [n // 2 for n in sizes]
    quarters = [n // 2 // members for n in sizes]

    def held_sum(c):
        return go_acc if c == 0 else gacc.at[c - 1]

    def quarter_at(c, p):
        at = pl.multiple_of(kind * halves[c] + p * quarters[c], quarters[c])
        return pl.ds(at, quarters[c])

    for c in range(pairs + 1):
        n_half, n_quarter = halves[c], quarters[c]
        plan.add(f"ha{c}", [lambda c=c, r=n_half: (s1.at[c, 0:r], r1.at[c, 0:r], core())])
        plan.add(f"hb{c}", [
            lambda c=c, n=n, r=n_quarter: (s2.at[c, n, 0:r], r2.at[c, n, 0:r], same_plane(*steps[n]))
            for n in range(members - 1)
        ])
        plan.add(f"hz{c}", [
            lambda c=c, d=d, r=n_quarter: (s3.at[c, 0:r], r3.at[c, d - 1, 0:r], other_plane(d))
            for d in others
        ])

        def share(c, n):
            ref = fl.at[c, quarter_at(c, part), :]
            return ref, ref, same_plane(*steps[n])

        def side(c):
            ref = fl.at[c, rows_of(kind, halves[c]), :]
            return ref, ref, core()

        plan.add(f"hg{c}", [lambda c=c, n=n: share(c, n) for n in range(members - 1)])
        plan.add(f"hh{c}", [lambda c=c: side(c)])
    near = [(far, d) for far in (0, 1) for d in range(nb) if far or d]
    plan.add("sb", [lambda n=n: (few.at[0], rs.at[n], same_plane(*near[n])) for n in range(len(near))])
    plan.add("sz", [lambda d=d: (few.at[1], rs.at[len(near) + d - 1], other_plane(d)) for d in others])
    assert plan.count <= send_sem.shape[0]

    def chunk_start(c):
        s1[c, 0 : halves[c]] = held_sum(c)[rows_of(1 - kind, halves[c]), :].astype(BF)
        plan.start(f"ha{c}")

    def chunk_b(c):
        plan.arrived(f"ha{c}")
        at = rows_of(kind, halves[c])
        ref = held_sum(c)
        ref[at, :] = ref[at, :] + r1[c, 0 : halves[c]].astype(F32)
        for n, to in enumerate(steps):
            s2[c, n, 0 : quarters[c]] = ref[quarter_at(c, part_of(*to)), :].astype(BF)
        plan.start(f"hb{c}")

    def chunk_z(c):
        plan.arrived(f"hb{c}")
        r = quarters[c]
        total = pair_sum(
            [held_sum(c)[quarter_at(c, part), :]] + [r2[c, n, 0:r].astype(F32) for n in range(members - 1)]
        )
        s3[c, 0:r] = total.astype(BF)
        plan.start(f"hz{c}")

    def chunk_g(c):
        plan.arrived(f"hz{c}")
        r = quarters[c]
        total = pair_sum([s3[c, 0:r].astype(F32)] + [r3[c, d - 1, 0:r].astype(F32) for d in others])
        fl[c, quarter_at(c, part), :] = total.astype(BF)
        plan.start(f"hg{c}")

    def chunk_h(c):
        plan.arrived(f"hg{c}")
        plan.start(f"hh{c}")

    def out_copy(c):
        return pltpu.make_async_copy(fl.at[c], flat_ref.at[c], load_sem.at[4 + c])

    def chunk_done(c):
        plan.arrived(f"hh{c}")
        out_copy(c).start()

    def reduced(w):
        plan.arrived(f"rs{w}")
        total = pair_sum([ours[w, plane].astype(F32)] + [theirs[w, d - 1].astype(F32) for d in others])
        piece[w] = total.astype(BF)
        mine[w]().start()
        for name in ("z", "y0", "x0"):
            plan.start(f"{name}{w}")

    def own_y(w):
        plan.arrived(f"y0{w}")
        plan.start(f"yx0{w}")

    def whole_slice(w):
        mine[w]().wait()
        plan.arrived(f"z{w}")
        for name in ("y1", "x1", "co"):
            plan.start(f"{name}{w}")

    def slice_y(w):
        plan.arrived(f"y1{w}")
        for name in ("yx1", "cy"):
            plan.start(f"{name}{w}")

    def slice_x(w):
        plan.arrived(f"x0{w}")
        plan.arrived(f"x1{w}")
        plan.start(f"cx{w}")

    def slice_d(w):
        plan.arrived(f"yx0{w}")
        plan.arrived(f"yx1{w}")
        plan.start(f"cd{w}")

    stages = [chunk_start, chunk_b, chunk_z, chunk_g, chunk_h, chunk_done]

    @pl.when(now == 0)
    def _():
        for c in loads:
            c().start()
        partners = [peer("blk", blk, d) for d in range(1, nb)]
        partners += [same_plane(1, d) for d in range(nb)] + [other_plane(d) for d in others]
        arrive(partners)
        small[...] = jnp.zeros_like(small)
        go_acc[...] = jnp.zeros_like(go_acc)
        fill_bias(bias_own, None, False, 0)
        for c in loads:
            c().wait()
        mg, deo = factors[0], factors[1]
        act, slope = gelu_both(nn(mg, win[...]))
        du = (slope * nt(deo, wback[...])).astype(BF)
        g_in = tn(mg, du).astype(BF)
        for n in range(planes):
            ours[0, n] = g_in[n * rows : (n + 1) * rows]
        plan.start("rs0")
        g_back = tn(act.astype(BF), deo).astype(BF)
        for n in range(planes):
            ours[1, n] = g_back[n * rows : (n + 1) * rows]
        plan.start("rs1")

    gate_rows = gate_ref.shape[0]

    @pl.when(now < lead)
    def _():
        at = rows_of(step, BLOCK)
        h = h_ref[0]
        cot_b = cot_ref[0, 0]
        dout = cot_b.astype(F32)
        r2_ = rms(h)
        z = h * r2_
        n2 = (z * g2_ref[...]).astype(BF)
        gate = gate_ref[...]
        gate_b = gate.astype(BF)
        gate_low = (gate - gate_b.astype(F32)).astype(BF)
        eo = jnp.concatenate([eo_ref[j] for j in range(eo_ref.shape[0])], axis=0)
        dmg = jnp.concatenate([dmg_ref[j] for j in range(dmg_ref.shape[0])], axis=0).astype(BF)
        eo_b = eo.astype(BF)
        eo_low = (eo - eo_b.astype(F32)).astype(BF)
        mixed = tn(
            jnp.concatenate([gate_b, gate_low, gate_b], axis=0),
            jnp.concatenate([eo_b, eo_b, eo_low], axis=0),
        )
        act_buf[micro, step] = (h + mixed).astype(BF)
        for m in range(micros):
            pl.when(micro == m)(functools.partial(acts[m].start, step))
        dw2 = nt(jnp.concatenate([eo_b, eo_low], axis=0), cot_b)
        dw = dw2[:gate_rows] + dw2[gate_rows:] + nt(dmg, n2)
        wdw = gate * dw
        dlog = (wdw - gate * jnp.sum(wdw, axis=1, keepdims=True)).astype(BF)
        dn2 = tn(
            jnp.concatenate([gate_b, dlog], axis=0),
            jnp.concatenate([dmg, wc_ref[...]], axis=0),
        )
        small[0:gate_rows, :] += nn(dlog, n2)
        small[gate_rows : gate_rows + 1, :] += jnp.sum(dn2 * z, axis=0, keepdims=True)
        a = dn2 * g2_ref[...]
        dh = dout + r2_ * (a - z * jnp.mean(a * z, axis=-1, keepdims=True))
        dh_all[micro, at, :] = dh
        da = dh.astype(BF)
        dob_b = nt(da, wo_ref[...]).astype(BF)
        dob[micro, at, :] = dob_b
        ob = ob_ref[0]
        go_acc[...] += tn(ob, da)
        prod = dob_b.astype(F32) * ob.astype(F32)
        high = prod.astype(BF)
        low = (prod - high.astype(F32)).astype(BF)
        heads = head_rows(delta.shape[1], width)
        delta[micro, :, at] = nt(heads, high) + nt(heads, low)
        x = x_ref[0, step].astype(F32)
        n1_all[micro, at, :] = (x * rms(x) * g1_ref[...]).astype(BF)

    for m in range(1, micros):
        for i in range(blocks):
            pl.when(now == m * blocks + i)(
                functools.partial(fill_bias, bias.at[i], start_ref[i], True, i)
            )

    masks = head_masks()

    def attend(m):
        hp = step
        packed = m > 0
        lanes = rows_of(hp, pair_lanes)
        for i in range(blocks):
            low, count = key_range(packed, i)
            at = slice(i * BLOCK, (i + 1) * BLOCK)
            q_pair, dob_pair = q_ref[0, at, :], dob[m, at, lanes]
            k_pair, v_pair = k_ref[0, low : low + count, :], v_ref[0, low : low + count, :]
            dk_sum = dv_sum = None
            dqs = []
            for h in range(2):
                qm, dm = q_pair * masks[h], dob_pair * masks[h]
                scores = add_bias(nt(k_pair, qm), bias.at[i] if packed else bias_own, packed, count)
                p = jnp.exp(scores * SCALE - lse_ref[0, pl.ds(hp * 2 + h, 1), at])
                dp_ = nt(v_pair, dm)
                ds = (p * (dp_ - delta[m, pl.ds(hp * 2 + h, 1), at])).astype(BF)
                kt = kt_ref[0, h * HEAD_DIM : (h + 1) * HEAD_DIM, low : low + count]
                dqs.append(nn(kt, ds) * SCALE)
                dk_part, dv_part = nn(ds, qm), nn(p.astype(BF), dm)
                dk_sum = dk_part if dk_sum is None else dk_sum + dk_part
                dv_sum = dv_part if dv_sum is None else dv_sum + dv_part
            old = i * BLOCK - low
            dk_acc[at, :] = dk_sum[old:]
            dv_acc[at, :] = dv_sum[old:]
            if old:
                dk_acc[low : i * BLOCK, :] += dk_sum[:old]
                dv_acc[low : i * BLOCK, :] += dv_sum[:old]
            dq_all[at, lanes] = jnp.concatenate(dqs, axis=0).T.astype(BF)
        dk = (dk_acc[...] * SCALE).astype(BF)
        dv = dv_acc[...].astype(BF)
        dk_all[:, lanes] = dk
        dv_all[:, lanes] = dv
        g = tn(jnp.concatenate([dq_all[:, lanes], dk, dv], axis=1), n1_all[m])
        if packed:
            gacc[hp] += g
        else:
            gacc[hp] = g

    for m in range(micros):
        in_phase = (now >= lead) & (micro == m) & (step < pairs)
        pl.when(in_phase)(functools.partial(attend, m))

    in_third = (now >= lead) & (step >= pairs)
    i = blk ^ (nb - 1 - (step - pairs))

    @pl.when(in_third)
    def _():
        at = rows_of(i, BLOCK)
        x = x_ref[0, i].astype(F32)
        r1_ = rms(x)
        z1 = x * r1_
        dn1 = (
            nt(dq_all[at, :], wq_ref[...]) + nt(dk_all[at, :], wk_ref[...]) + nt(dv_all[at, :], wv_ref[...])
        )
        small[gate_rows + 8 : gate_rows + 9, :] += jnp.sum(dn1 * z1, axis=0, keepdims=True)
        b = dn1 * g1_ref[...]
        gi = dh_all[micro, at, :] + r1_ * (b - z1 * jnp.mean(b * z1, axis=-1, keepdims=True))
        gi_buf[micro, i] = gi.astype(BF)

    final = lead + micros * span - 1
    tasks = {}

    def after(at, task, *args):
        tasks.setdefault(min(at, final), []).append(functools.partial(task, *args))

    def far_block(d):
        gis[0].copy(d).start()

    for n, gap in enumerate((0, 2, 5, 8, 10, 12)):
        after(lead - 1 + gap, stages[n], 0)
    for c in range(1, pairs):
        for n, gap in enumerate((0, 1, 3, 5, 6, 7)):
            after(last + c - 1 + gap, stages[n], c)
    c = pairs
    after(last + c - 1, chunk_start, c)
    after(last + c, chunk_b, c)
    after(last + c + 2, chunk_z, c)
    after(blocks, reduced, 0)
    after(lead, reduced, 1)
    after(lead, own_y, 0)
    after(lead + 2, whole_slice, 0)
    after(lead + 2, own_y, 1)
    after(last - 1, slice_y, 0)
    after(last - 1, whole_slice, 1)
    after(last + pairs - 2, slice_y, 1)
    after(last + pairs - 2, slice_x, 0)
    after(final, slice_x, 1)
    after(final, slice_d, 0)
    for d in range(2, nb):
        after(last + 2 * (d - 2), far_block, d)
    for at, todo in tasks.items():
        if at < final:

            @pl.when(now == at)
            def _(todo=todo):
                for task in todo:
                    task()

    @pl.when(in_third)
    def _():
        for m in range(micros):
            pl.when(micro == m)(functools.partial(gis[m].start, i, 2 if m == 0 else nb))

    @pl.when(now == final)
    def _():
        per = gate_rows // 2
        few[0] = jnp.concatenate(
            [jnp.sum(small[n * per : (n + 1) * per, :], axis=0, keepdims=True) for n in range(2)]
            + [small[gate_rows : gate_rows + 1, :], small[gate_rows + 8 : gate_rows + 9, :]]
            + [jnp.zeros((4, width), F32)],
            axis=0,
        )
        plan.start("sb")
        for task in tasks[final]:
            task()
        chunk_g(c)
        plan.arrived("sb")
        few[1] = pair_sum([few[0]] + [rs[n] for n in range(len(near))])
        plan.start("sz")
        chunk_h(c)
        slice_d(1)
        chunk_done(c)
        plan.arrived("sz")
        small_ref[...] = pair_sum([few[1]] + [rs[len(near) + d - 1] for d in others])
        for w in both:
            for name in "oyxd":
                plan.arrived(f"c{name}{w}")
        for n in range(pairs + 1):
            out_copy(n).wait()
        for name in plan.sets:
            plan.sent(name)
        for r in acts + gis:
            r.wait()


def whole(shape):
    return pl.BlockSpec(shape, lambda *_: (0,) * len(shape))


def held(shape):
    return pl.BlockSpec(shape, lambda *_: (0,) * len(shape), pipeline_mode=pl.Buffered(1))


ANY = pl.BlockSpec(memory_space=pl.ANY)
DMA = pltpu.SemaphoreType.DMA


def shaped(shape, dtype):
    return jax.ShapeDtypeStruct(shape, dtype)


def params(number):
    return pltpu.CompilerParams(
        vmem_limit_bytes=VMEM_LIMIT, collective_id=number, has_side_effects=True
    )


def forward_call(x, seg, cot, g1, wq, wk, wv, wo, g2, wc):
    nb = lax.axis_size("blk")
    micros, _, rows_in, width = x.shape
    length = nb * rows_in
    blocks = length // BLOCK
    assert x.shape[1] == nb and rows_in == BLOCK
    rows = wc.shape[0]
    heads = width // HEAD_DIM
    per = BLOCK // GROUP
    experts = rows // per
    span = 2 * blocks
    phase = lambda s: jnp.maximum(s % span - blocks, 0)
    whole_micro = lambda a, b: pl.BlockSpec((1, a, b), lambda s: (s // span, 0, 0))
    flat = lambda s: (s // span) * blocks + phase(s)
    moves = 2 * micros + 1
    return pl.pallas_call(
        functools.partial(forward_kernel, micros, blocks, nb),
        grid=(micros * span,),
        in_specs=[ANY, ANY, ANY] + [held(a.shape) for a in (g1, wq, wk, wv, wo, g2, wc)],
        out_specs=[
            whole_micro(length, width), whole_micro(length, width), whole_micro(length, width),
            whole_micro(width, length),
            pl.BlockSpec((1, BLOCK, width), lambda s: (s // span, phase(s), 0)),
            pl.BlockSpec((1, heads, BLOCK), lambda s: (s // span, 0, phase(s))),
            pl.BlockSpec((1, BLOCK, width), lambda s: (s // span, phase(s), 0)),
            pl.BlockSpec((rows, BLOCK), lambda s: (0, flat(s))),
            pl.BlockSpec((experts, per, width), lambda s: (0, flat(s), 0)),
            whole((blocks, 1, BLOCK)), ANY, ANY,
        ],
        out_shape=[
            shaped((micros, length, width), BF), shaped((micros, length, width), BF),
            shaped((micros, length, width), BF), shaped((micros, width, length), BF),
            shaped((micros, length, width), BF), shaped((micros, heads, length), F32),
            shaped((micros, length, width), F32), shaped((rows, micros * length), F32),
            shaped((experts, micros * length // GROUP, width), F32),
            shaped((blocks, 1, BLOCK), jnp.int32), shaped(x.shape, BF), shaped(x.shape, BF),
        ],
        scratch_shapes=[
            pltpu.VMEM(x.shape, BF), pltpu.VMEM(seg.shape, seg.dtype),
            pltpu.VMEM((length, BLOCK), F32), pltpu.VMEM((BLOCK, width), F32),
            pltpu.VMEM((heads, BLOCK), F32), pltpu.VMEM((width, width), BF),
            DMA((moves + 1,)), DMA((moves * (nb - 1),)), DMA((moves * (nb - 1),)),
        ],
        compiler_params=params(1),
        name="attention_forward",
    )(x, seg, cot, g1, wq, wk, wv, wo, g2, wc)


def experts_call(mg, gate, cot, w_in, w_back):
    micros, nb, _, width = cot.shape
    experts, groups, _ = mg.shape
    ff = w_in.shape[2]
    blocks = gate.shape[1] // BLOCK // micros
    chunk = min(CHUNK, ff)
    by_expert = lambda n: pl.BlockSpec((1, n, width), lambda e, c: (e, 0, 0))
    members = 2 * nb
    return pl.pallas_call(
        functools.partial(experts_kernel, micros, blocks, nb),
        grid=(experts, ff // chunk),
        in_specs=[
            held(mg.shape), held(gate.shape), held(cot.shape),
            pl.BlockSpec((1, width, chunk), lambda e, c: (e, 0, c)),
            pl.BlockSpec((1, chunk, width), lambda e, c: (e, c, 0)),
        ],
        out_specs=[by_expert(groups)] * 2 + [whole((2, members * groups, width))],
        out_shape=[shaped((experts, groups, width), F32)] * 2
        + [shaped((2, members * groups, width), BF)],
        scratch_shapes=[
            pltpu.VMEM((experts, 2, groups, width), BF),
            pltpu.VMEM((members - 1, 2, groups, width), BF), DMA((members - 1,)), DMA((members - 1,)),
        ],
        compiler_params=params(2),
        name="experts",
    )(mg, gate, cot, w_in, w_back)


def backward_call(x, cot, h, gate, eo, dmg, ob, lse, q, k, v, kt, start, g1, g2, wc, wq, wk, wv, wo,
                  factors, w_in, w_back):
    micros, nb, _, width = x.shape
    planes = lax.axis_size("dp") // 2
    length = q.shape[1]
    blocks = length // BLOCK
    rows = wc.shape[0]
    per = BLOCK // GROUP
    experts = rows // per
    heads = width // HEAD_DIM
    pairs = heads // 2
    ff = w_in.shape[2]
    cut = ff // nb
    assert cut == width
    members = len(plane_steps(nb)) + 1
    lead, span = micros * blocks, blocks + pairs
    flat = lambda s: jnp.minimum(s, lead - 1)
    m_late = lambda s: jnp.maximum(s - lead, 0) // span
    m_of = lambda s: jnp.where(s < lead, s // blocks, m_late(s))
    pair_of = lambda s: jnp.minimum(jnp.maximum(s - lead, 0) % span, pairs - 1)
    row_block = pl.BlockSpec((1, BLOCK, width), lambda s: (flat(s) // blocks, flat(s) % blocks, 0))
    group_block = pl.BlockSpec((experts, per, width), lambda s: (0, flat(s), 0))
    pair_block = pl.BlockSpec((1, length, 2 * HEAD_DIM), lambda s: (m_late(s), 0, pair_of(s)))
    piece = (2, width // planes, cut)
    chunk = width
    chunks = pairs + 1
    half = chunk // 2
    quarter = half // members
    reach = max(key_range(True, i)[1] for i in range(blocks))
    small = (rows + 16, width)
    few = (8, width)
    vm = pltpu.VMEM
    copies = 96 + 16 * chunks + 32 * planes
    return pl.pallas_call(
        functools.partial(backward_kernel, micros, blocks, nb, planes),
        grid=(lead + micros * span,),
        in_specs=[
            pl.BlockSpec((1, nb, BLOCK, width), lambda s: (m_of(s), 0, 0, 0)),
            pl.BlockSpec((1, 1, BLOCK, width), lambda s: (flat(s) // blocks, flat(s) % blocks, 0, 0)),
            row_block,
            pl.BlockSpec((rows, BLOCK), lambda s: (0, flat(s))),
            group_block, group_block, row_block,
            pl.BlockSpec((1, heads, length), lambda s: (m_late(s), 0, 0)),
            pair_block, pair_block, pair_block,
            pl.BlockSpec((1, 2 * HEAD_DIM, length), lambda s: (m_late(s), pair_of(s), 0)),
        ] + [held(a.shape) for a in (start, g1, g2, wc, wq, wk, wv, wo, factors)] + [ANY, ANY],
        out_specs=[ANY, ANY, ANY, whole(few), ANY, ANY],
        out_shape=[
            shaped(x.shape, BF), shaped(x.shape, BF), shaped((chunks, chunk, width), BF),
            shaped(few, F32), shaped(w_in.shape, BF), shaped(w_back.shape, BF),
        ],
        scratch_shapes=[
            vm((micros, length, width), F32), vm((micros, length, width), BF),
            vm((micros, length, width), BF), vm((micros, heads, length), F32), vm((length, width), BF), vm((length, width), BF),
            vm((length, width), BF), vm((length, 2 * HEAD_DIM), F32), vm((length, 2 * HEAD_DIM), F32),
            vm((pairs, 6 * HEAD_DIM, width), F32), vm((width, width), F32), vm((BLOCK, BLOCK), F32),
            vm((blocks, reach, BLOCK), F32),
            vm(x.shape, BF), vm(x.shape, BF), vm((width, cut), BF), vm((cut, width), BF),
            vm((2, planes) + piece[1:], BF), vm((2, planes - 1) + piece[1:], BF), vm(piece, BF),
            vm((chunks, half, width), BF), vm((chunks, half, width), BF),
            vm((chunks, members - 1, quarter, width), BF), vm((chunks, members - 1, quarter, width), BF),
            vm((chunks, quarter, width), BF), vm((chunks, planes - 1, quarter, width), BF),
            vm((chunks, chunk, width), BF), vm(small, F32), vm((2,) + few, F32),
            vm((2 * nb + planes - 2,) + few, F32),
            DMA((2 * micros,)), DMA((5 + pairs,)), DMA((2 * micros * (nb - 1),)),
            DMA((2 * micros * (nb - 1),)), DMA((copies,)), DMA((copies,)),
        ],
        compiler_params=params(3),
        name="attention_backward",
    )(x, cot, h, gate, eo, dmg, ob, lse, q, k, v, kt, start, g1, g2, wc, wq, wk, wv, wo, factors, w_in,
      w_back)


def local(block_input, segment_ids, gain_one, w_query, w_key, w_value, w_out, gain_two, w_ctrl,
          w_in, w_back, cotangent):
    micros, seqs, rows, width = block_input.shape
    experts, _, ff = w_in.shape
    nb = lax.axis_size("blk")
    per = BLOCK // GROUP
    g1, g2 = gain_one.reshape(1, width), gain_two.reshape(1, width)
    wc = jnp.repeat(w_ctrl.T, per, axis=0)
    seg = segment_ids.reshape(nb, 2, rows // 2)
    q, k, v, kt, ob, lse, h, gate, mg, start, x, cot = forward_call(
        block_input, seg, cotangent, g1, w_query, w_key, w_value, w_out, g2, wc
    )
    eo, dmg, factors = experts_call(mg, gate, cot, w_in, w_back)
    acts, gis, flat, small, grad_in, grad_back = backward_call(
        x, cot, h, gate, eo, dmg, ob, lse, q, k, v, kt, start, g1, g2, wc, w_query, w_key, w_value,
        w_out, factors, w_in, w_back,
    )
    lanes = 2 * HEAD_DIM
    one = lambda n: flat[1:, n * lanes : (n + 1) * lanes].reshape(width, width).astype(F32).T
    return (
        acts, gis, small[3], one(0), one(1), one(2), flat[0].astype(F32), small[2], small[:experts].T,
        grad_in.astype(F32), grad_back.astype(F32),
    )


def solution(mesh):
    data = P(None, "dp", "blk", None)
    in_specs = (data, P("dp", "blk")) + (P(),) * 9 + (data,)
    out_specs = (data, data) + (P(),) * 9
    return jax.shard_map(local, mesh=mesh, in_specs=in_specs, out_specs=out_specs, check_vma=False)
```

```python
import functools

import jax
import jax.numpy as jnp
from jax import lax
from jax.experimental import pallas as pl
from jax.experimental.pallas import tpu as pltpu
from jax.sharding import PartitionSpec as P

HEAD_DIM = 64
GROUP = 32
EPSILON = 1e-05
BLOCK = 256
CHUNK = 512
SCALE = 0.125
MASKED = -1e30
VMEM_LIMIT = 60 * 1024 * 1024
BF = jnp.bfloat16
F32 = jnp.float32
MESH = pl.DeviceIdType.MESH


def dot(a, b, ca, cb):
    return lax.dot_general(a, b, (((ca,), (cb,)), ((), ())), preferred_element_type=F32)


def nn(a, b):
    return dot(a, b, 1, 0)


def nt(a, b):
    return dot(a, b, 1, 1)


def tn(a, b):
    return dot(a, b, 0, 0)


def key_range(packed, i):
    low = max(0, i * BLOCK - BLOCK - BLOCK // 2) if packed else 0
    return low, (i + 1) * BLOCK - low


def head_masks():
    lane = lax.broadcasted_iota(jnp.int32, (1, 2 * HEAD_DIM), 1)
    first = (lane < HEAD_DIM).astype(F32).astype(BF)
    return first, (lane >= HEAD_DIM).astype(F32).astype(BF)


def group_match(rows, tokens):
    row = lax.broadcasted_iota(jnp.int32, (rows, tokens), 0)
    col = lax.broadcasted_iota(jnp.int32, (rows, tokens), 1)
    return (row % (tokens // GROUP)) == (col // GROUP)


def fill_bias(bias_ref, start_ref, packed, i):
    low, count = key_range(packed, i)
    q_pos = i * BLOCK + lax.broadcasted_iota(jnp.int32, (1, BLOCK), 1)
    if packed:
        k_pos = low + lax.broadcasted_iota(jnp.int32, (count, BLOCK), 0)
        allowed = (k_pos <= q_pos) & (k_pos >= start_ref[...])
        bias_ref[0:count, :] = jnp.where(allowed, 0.0, MASKED)
    else:
        k_pos = i * BLOCK + lax.broadcasted_iota(jnp.int32, (BLOCK, BLOCK), 0)
        bias_ref[0:BLOCK, :] = jnp.where(k_pos <= q_pos, 0.0, MASKED)


def add_bias(scores, bias_ref, packed, count):
    if packed:
        return scores + bias_ref[0:count, :]
    last = scores[count - BLOCK :, :] + bias_ref[0:BLOCK, :]
    if count == BLOCK:
        return last
    return jnp.concatenate([scores[: count - BLOCK, :], last], axis=0)


def rms(values):
    return lax.rsqrt(jnp.mean(values * values, axis=-1, keepdims=True) + EPSILON)


def peer(axis, me, d):
    return {axis: me ^ d}


def arrive(partners):
    barrier = pltpu.get_barrier_semaphore()
    for p in partners:
        pl.semaphore_signal(barrier, inc=1, device_id=p, device_id_type=MESH)
    pl.semaphore_wait(barrier, len(partners))


def remote(src, dst, sems, k, where):
    return pltpu.make_async_remote_copy(
        src_ref=src, dst_ref=dst, send_sem=sems[0].at[k], recv_sem=sems[1].at[k],
        device_id=where, device_id_type=MESH,
    )


class Exchange:
    def __init__(self, nb, src, dst, own, sems, base):
        self.nb, self.src, self.dst, self.own, self.sems, self.base = nb, src, dst, own, sems, base
        self.me = lax.axis_index("blk")

    def local(self):
        return pltpu.make_async_copy(
            self.src.at[self.me], self.dst.at[self.me], self.own.at[self.base]
        )

    def copy(self, d):
        return remote(
            self.src.at[self.me ^ d], self.dst.at[self.me], self.sems,
            self.base * (self.nb - 1) + d - 1, peer("blk", self.me, d),
        )

    def start(self):
        self.local().start()
        for d in range(1, self.nb):
            self.copy(d).start()

    def wait(self):
        self.local().wait()
        for d in range(1, self.nb):
            self.copy(d).wait()


def unit(n):
    row = lax.broadcasted_iota(jnp.int32, (n, n), 0)
    col = lax.broadcasted_iota(jnp.int32, (n, n), 1)
    return (row == col).astype(F32).astype(BF)


def split_three(a):
    high = a.astype(BF)
    rest = a - high.astype(F32)
    mid = rest.astype(BF)
    return [high, mid, (rest - mid.astype(F32)).astype(BF)]


def head_rows(heads, width):
    row = lax.broadcasted_iota(jnp.int32, (heads, width), 0)
    col = lax.broadcasted_iota(jnp.int32, (heads, width), 1)
    return (row == col // HEAD_DIM).astype(F32).astype(BF)


def forward_kernel(micros, blocks, nb, x_src, seg_src, cot_src, g1_ref, wq_ref, wk_ref, wv_ref, wo_ref,
                   g2_ref, wc_ref, q_ref, k_ref, v_ref, kt_ref, ob_ref, lse_ref, h_ref, gate_ref,
                   mg_ref, start_ref, x_out, cot_out, x_all, seg_all, bias, o_acc, sums, eye, own,
                   send_sem, recv_sem):
    sems = (send_sem, recv_sem)
    now = pl.program_id(0)
    span = 2 * blocks
    micro, step = now // span, now % span
    width = wo_ref.shape[0]
    pairs = width // (2 * HEAD_DIM)
    me = lax.axis_index("blk")
    xs = [Exchange(nb, x_src.at[m], x_all.at[m], own, sems, m) for m in range(micros)]
    segs = Exchange(nb, seg_src, seg_all, own, sems, micros)
    cots = [
        Exchange(nb, cot_src.at[m], cot_out.at[m], own, sems, micros + 1 + m) for m in range(micros)
    ]
    keep = pltpu.make_async_copy(x_all, x_out, own.at[2 * micros + 1])

    @pl.when(now == 0)
    def _():
        xs[0].local().start()
        eye[...] = unit(width)
        arrive([peer("blk", me, d) for d in range(1, nb)])
        for d in range(1, nb):
            xs[0].copy(d).start()

    @pl.when(step < blocks)
    def _():
        block = me ^ step
        for m in range(micros):
            pl.when((micro == m) & (step == 0))(xs[m].local().wait)
            for d in range(1, nb):
                pl.when((micro == m) & (step == d))(xs[m].copy(d).wait_recv)
        x = x_all[micro, block].astype(F32)
        n1 = (x * rms(x) * g1_ref[...]).astype(BF)
        at = pl.ds(pl.multiple_of(block * BLOCK, BLOCK), BLOCK)
        q_ref[0, at, :] = nn(n1, wq_ref[...]).astype(BF)
        k = nn(n1, wk_ref[...]).astype(BF)
        k_ref[0, at, :] = k
        v_ref[0, at, :] = nn(n1, wv_ref[...]).astype(BF)
        kt_ref[0, :, at] = nt(eye[...], k).astype(BF)

    @pl.when(now == nb - 1)
    def _():
        segs.start()
        for m in range(1, micros):
            xs[m].start()

    @pl.when(now == blocks)
    def _():
        for c in cots:
            c.start()

    @pl.when(now == span)
    def _():
        segs.wait()
        counts = [
            jnp.sum(jnp.sum((seg_all[...] < d).astype(F32), axis=0), keepdims=True)
            for d in range(1, nb * seg_all.shape[1] * seg_all.shape[2] // BLOCK)
        ]
        for b in range(blocks):
            seg = jnp.concatenate([seg_all[b, n : n + 1, :] for n in range(seg_all.shape[1])], axis=1)
            start = jnp.zeros(seg.shape, F32)
            for d, count in enumerate(counts):
                start = jnp.where(seg == d + 1, count, start)
            start_ref[b] = start.astype(jnp.int32)

    masks = head_masks()

    def attend(packed, i):
        low, count = key_range(packed, i)
        fill_bias(bias, start_ref[i], packed, i)
        for hp in range(pairs):
            lanes = slice(hp * 2 * HEAD_DIM, (hp + 1) * 2 * HEAD_DIM)
            q_pair = q_ref[0, i * BLOCK : (i + 1) * BLOCK, lanes]
            k_pair = k_ref[0, low : low + count, lanes]
            v_pair = v_ref[0, low : low + count, lanes]
            o_pair = None
            for h in range(2):
                scores = add_bias(nt(k_pair, q_pair * masks[h]), bias, packed, count)
                top = jnp.max(scores, axis=0, keepdims=True)
                p = jnp.exp((scores - top) * SCALE)
                total = jnp.sum(p, axis=0, keepdims=True)
                o = tn(p.astype(BF), v_pair * masks[h])
                o_pair = o if o_pair is None else o_pair + o
                sums[hp * 2 + h : hp * 2 + h + 1, :] = 1.0 / total
                lse_ref[0, hp * 2 + h : hp * 2 + h + 1, :] = top * SCALE + jnp.log(total)
            o_acc[:, lanes] = o_pair

    for m in range(micros):
        for i in range(blocks):
            pl.when(now == m * span + blocks + i)(functools.partial(attend, m > 0, i))

    @pl.when(step >= blocks)
    def _():
        heads = head_rows(sums.shape[0], width)
        scale = tn(
            jnp.concatenate(split_three(sums[...]), axis=0), jnp.concatenate([heads] * 3, axis=0)
        )
        ob = (o_acc[...] * scale).astype(BF)
        ob_ref[0] = ob
        h = x_all[micro, step - blocks].astype(F32) + nn(ob, wo_ref[...])
        h_ref[0] = h
        n2 = (h * rms(h) * g2_ref[...]).astype(BF)
        logits = nt(wc_ref[...], n2)
        rows = logits.shape[0]
        match = group_match(rows, BLOCK)
        logits = jnp.where(match, logits, MASKED)
        e = jnp.where(match, jnp.exp(logits - jnp.max(logits, axis=1, keepdims=True)), 0.0)
        gate = e / jnp.sum(e, axis=1, keepdims=True)
        gate_ref[...] = gate
        mg = nn(gate.astype(BF), n2).astype(BF).astype(F32)
        half = rows // mg_ref.shape[0]
        for j in range(mg_ref.shape[0]):
            mg_ref[j] = mg[j * half : (j + 1) * half]

    @pl.when(now == span + nb)
    def _():
        keep.start()

    @pl.when(now == micros * span - 1)
    def _():
        keep.wait()
        for x in xs:
            for d in range(1, nb):
                x.copy(d).wait_send()
        for c in cots:
            c.wait()


def gelu_both(u):
    c = 0.7978845608028654
    t = jnp.tanh(c * (u + 0.044715 * (u * u * u)))
    act = 0.5 * u * (1.0 + t)
    slope = 0.5 * (1.0 + t) + 0.5 * u * (1.0 - t * t) * (c * (1.0 + 3 * 0.044715 * (u * u)))
    return act, slope


def same_plane(far, d):
    return {"dp": lax.axis_index("dp") ^ far, "blk": lax.axis_index("blk") ^ d}


def plane_steps(nb):
    return [(far, d) for far in (0, 1) for d in range(0, nb, 2) if far or d]


def experts_kernel(micros, blocks, nb, *refs):
    mg_ref, gate_ref, cot_ref, win_ref, wback_ref = refs[:5]
    eo_ref, dmg_ref, all_ref, factors, gathered, send_sem, recv_sem = refs[5:]
    sems = (send_sem, recv_sem)
    e, c = pl.program_id(0), pl.program_id(1)
    at = e * pl.num_programs(1) + c
    last = pl.num_programs(0) * pl.num_programs(1) - 1
    per = BLOCK // GROUP
    n_exp = factors.shape[0]
    groups = micros * blocks * per
    blk = lax.axis_index("blk")
    kind = blk % n_exp
    steps = [(far, d) for far in (0, 1) for d in range(nb) if far or d]

    def plane_copy(n):
        far, d = steps[n]
        return remote(factors.at[kind ^ (d & 1)], gathered.at[n], sems, n, same_plane(far, d))

    @pl.when(at == 0)
    def _():
        deo = []
        for m in range(micros):
            for i in range(blocks):
                at_rows = (m * blocks + i) * BLOCK
                deo.append(nn(gate_ref[:, at_rows : at_rows + BLOCK].astype(BF), cot_ref[m, i]))
        for j in range(n_exp):
            factors[j, 0] = mg_ref[j].astype(BF)
            factors[j, 1] = jnp.concatenate(
                [d[j * per : (j + 1) * per] for d in deo], axis=0
            ).astype(BF)
        arrive([same_plane(*s) for s in steps])
        for n in range(len(steps)):
            plane_copy(n).start()

    mg, deo = factors[e, 0], factors[e, 1]
    act, slope = gelu_both(nn(mg, win_ref[0]))
    eo_part = nn(act.astype(BF), wback_ref[0])
    du = (slope * nt(deo, wback_ref[0])).astype(BF)
    dmg_part = nt(du, win_ref[0])

    @pl.when(c == 0)
    def _():
        eo_ref[0] = eo_part
        dmg_ref[0] = dmg_part

    @pl.when(c > 0)
    def _():
        eo_ref[0] += eo_part
        dmg_ref[0] += dmg_part

    @pl.when(at == last)
    def _():
        for n in range(len(steps)):
            plane_copy(n).wait()
        for n in range(len(steps) + 1):
            piece = factors[kind] if n == 0 else gathered[n - 1]
            for f in range(2):
                all_ref[f, n * groups : (n + 1) * groups, :] = piece[f]


class Return:
    def __init__(self, nb, buf, out, own, sems, base):
        self.nb, self.buf, self.out, self.own, self.sems, self.base = nb, buf, out, own, sems, base
        self.me = lax.axis_index("blk")

    def local(self):
        return pltpu.make_async_copy(
            self.buf.at[self.me], self.out.at[self.me], self.own.at[self.base]
        )

    def copy(self, d):
        return remote(
            self.buf.at[self.me ^ d], self.out.at[self.me], self.sems,
            self.base * (self.nb - 1) + d - 1, peer("blk", self.me, d),
        )

    def start(self, i, reach=None):
        pl.when(i == self.me)(lambda: self.local().start())
        for d in range(1, reach or self.nb):
            pl.when(i == (self.me ^ d))(lambda d=d: self.copy(d).start())

    def wait(self):
        self.local().wait()
        for d in range(1, self.nb):
            self.copy(d).wait()


class Plan:
    def __init__(self, sems):
        self.sems, self.count, self.sets = sems, 0, {}

    def add(self, name, makers):
        self.sets[name] = list(enumerate(makers, self.count))
        self.count += len(makers)

    def each(self, name):
        for k, maker in self.sets[name]:
            src, dst, where = maker()
            yield remote(src, dst, self.sems, k, where)

    def start(self, name):
        for c in self.each(name):
            c.start()

    def arrived(self, name):
        for c in self.each(name):
            c.wait_recv()

    def sent(self, name):
        for c in self.each(name):
            c.wait_send()


def other_plane(d):
    return {"dp": lax.axis_index("dp") ^ (2 * d)}


def pair_sum(parts):
    while len(parts) > 1:
        parts = [parts[n] + parts[n + 1] for n in range(0, len(parts), 2)]
    return parts[0]


def rows_of(n, size):
    return pl.ds(pl.multiple_of(n * size, size), size)


def backward_kernel(micros, blocks, nb, planes, x_ref, cot_ref, h_ref, gate_ref, eo_ref, dmg_ref, ob_ref,
                    lse_ref, q_ref, k_ref, v_ref, kt_ref, start_ref, g1_ref, g2_ref, wc_ref, wq_ref,
                    wk_ref, wv_ref, wo_ref, factors, win_hbm, wback_hbm, act_ref, gi_ref, flat_ref,
                    small_ref, gin, gback, dh_all, n1_all, dob, delta, dq_all, dk_all, dv_all, dk_acc,
                    dv_acc, gacc, go_acc, bias_own, bias, act_buf, gi_buf, win, wback, ours, theirs, piece, s1,
                    r1, s2, r2, s3, r3, fl, small, few, rs, own, load_sem, ret_send, ret_recv, send_sem,
                    recv_sem):
    now = pl.program_id(0)
    width = wo_ref.shape[0]
    pairs = width // (2 * HEAD_DIM)
    pair_lanes = 2 * HEAD_DIM
    lead, span = micros * blocks, blocks + pairs
    micro = jnp.where(now < lead, now // blocks, (now - lead) // span)
    step = jnp.where(now < lead, now % blocks, (now - lead) % span)
    last = lead + (micros - 1) * span
    blk, dp = lax.axis_index("blk"), lax.axis_index("dp")
    kind, plane = blk % 2, dp // 2
    steps = plane_steps(nb)
    members = len(steps) + 1
    core = lambda: peer("blk", lax.axis_index("blk"), 1)

    def part_of(far, d):
        return ((blk ^ d) // 2) + (nb // 2) * ((dp % 2) ^ far)

    part = part_of(0, 0)
    cut = win.shape[1]
    rets = (ret_send, ret_recv)
    acts = [Return(nb, act_buf.at[m], act_ref.at[m], own, rets, 2 * m) for m in range(micros)]
    gis = [Return(nb, gi_buf.at[m], gi_ref.at[m], own, rets, 2 * m + 1) for m in range(micros)]
    columns = rows_of(part, cut)
    loads = [
        lambda: pltpu.make_async_copy(win_hbm.at[kind, :, columns], win, load_sem.at[0]),
        lambda: pltpu.make_async_copy(wback_hbm.at[kind, columns, :], wback, load_sem.at[1]),
    ]
    rows = width // planes

    def window(which, p, z):
        if which == 0:
            return gin.at[kind, rows_of(z, rows), rows_of(p, cut)]
        at = pl.multiple_of(p * cut + z * rows, rows)
        return gback.at[kind, pl.ds(at, rows), :]

    def slab(which, p):
        if which == 0:
            return gin.at[kind, :, rows_of(p, cut)]
        return gback.at[kind, rows_of(p, cut), :]

    mine = [
        lambda w=w: pltpu.make_async_copy(piece.at[w], window(w, part, plane), load_sem.at[2 + w])
        for w in range(2)
    ]
    y_peer, x_peer = steps[0], steps[1]
    others = range(1, planes)
    both = range(2)
    plan = Plan((send_sem, recv_sem))
    for w in both:
        plan.add(f"rs{w}", [
            lambda d=d, w=w: (ours.at[w, plane ^ d], theirs.at[w, d - 1], other_plane(d)) for d in others
        ])
        plan.add(f"z{w}", [
            lambda d=d, w=w: (piece.at[w], window(w, part, plane), other_plane(d)) for d in others
        ])
        for name, to in ((f"y0{w}", y_peer), (f"x0{w}", x_peer)):
            plan.add(name, [
                lambda w=w, to=to: (piece.at[w], window(w, part, plane), same_plane(*to))
            ])

    def onward(p, z, w, to):
        return window(w, p, z), window(w, p, z), same_plane(*to)

    part_y = part_of(*y_peer)
    for w in both:
        plan.add(f"yx0{w}", [lambda w=w: onward(part_y, plane, w, x_peer)])
        for name, p, to in ((f"y1{w}", part, y_peer), (f"x1{w}", part, x_peer), (f"yx1{w}", part_y, x_peer)):
            plan.add(name, [
                lambda d=d, w=w, p=p, to=to: onward(p, plane ^ d, w, to) for d in others
            ])
        for name, p in zip("oyxd", [part] + [part_of(*t) for t in steps]):
            plan.add(f"c{name}{w}", [lambda w=w, p=p: (slab(w, p), slab(w, p), core())])

    wides = [width] + [3 * pair_lanes] * pairs
    half, quarter = width // 2, width // 2 // members

    def held_sum(c):
        return go_acc if c == 0 else gacc.at[c - 1]

    def quarter_at(p):
        at = pl.multiple_of(kind * half + p * quarter, quarter)
        return pl.ds(at, quarter)

    for c in range(pairs + 1):
        wide = wides[c]
        plan.add(f"ha{c}", [lambda c=c, w=wide: (s1.at[c, :, 0:w], r1.at[c, :, 0:w], core())])
        plan.add(f"hb{c}", [
            lambda c=c, n=n, w=wide: (s2.at[c, n, :, 0:w], r2.at[c, n, :, 0:w], same_plane(*steps[n]))
            for n in range(members - 1)
        ])
        plan.add(f"hz{c}", [
            lambda c=c, d=d, w=wide: (s3.at[c, :, 0:w], r3.at[c, d - 1, :, 0:w], other_plane(d))
            for d in others
        ])

        def share(c, n):
            ref = fl.at[c, quarter_at(part), 0 : wides[c]]
            return ref, ref, same_plane(*steps[n])

        def side(c):
            ref = fl.at[c, rows_of(kind, half), 0 : wides[c]]
            return ref, ref, core()

        plan.add(f"hg{c}", [lambda c=c, n=n: share(c, n) for n in range(members - 1)])
        plan.add(f"hh{c}", [lambda c=c: side(c)])
    near = [(far, d) for far in (0, 1) for d in range(nb) if far or d]
    plan.add("sb", [lambda n=n: (few.at[0], rs.at[n], same_plane(*near[n])) for n in range(len(near))])
    plan.add("sz", [lambda d=d: (few.at[1], rs.at[len(near) + d - 1], other_plane(d)) for d in others])
    assert plan.count <= send_sem.shape[0]

    def chunk_start(c):
        s1[c, :, 0 : wides[c]] = held_sum(c)[rows_of(1 - kind, half), :].astype(BF)
        plan.start(f"ha{c}")

    def chunk_b(c):
        plan.arrived(f"ha{c}")
        at = rows_of(kind, half)
        ref = held_sum(c)
        ref[at, :] = ref[at, :] + r1[c, :, 0 : wides[c]].astype(F32)
        for n, to in enumerate(steps):
            s2[c, n, :, 0 : wides[c]] = ref[quarter_at(part_of(*to)), :].astype(BF)
        plan.start(f"hb{c}")

    def chunk_z(c):
        plan.arrived(f"hb{c}")
        w = wides[c]
        total = pair_sum(
            [held_sum(c)[quarter_at(part), :]] + [r2[c, n, :, 0:w].astype(F32) for n in range(members - 1)]
        )
        s3[c, :, 0:w] = total.astype(BF)
        plan.start(f"hz{c}")

    def chunk_g(c):
        plan.arrived(f"hz{c}")
        w = wides[c]
        total = pair_sum([s3[c, :, 0:w].astype(F32)] + [r3[c, d - 1, :, 0:w].astype(F32) for d in others])
        fl[c, quarter_at(part), 0:w] = total.astype(BF)
        plan.start(f"hg{c}")

    def chunk_h(c):
        plan.arrived(f"hg{c}")
        plan.start(f"hh{c}")

    def out_copy(c):
        return pltpu.make_async_copy(fl.at[c], flat_ref.at[c], load_sem.at[4 + c])

    def chunk_done(c):
        plan.arrived(f"hh{c}")
        out_copy(c).start()

    def reduced(w):
        plan.arrived(f"rs{w}")
        total = pair_sum([ours[w, plane].astype(F32)] + [theirs[w, d - 1].astype(F32) for d in others])
        piece[w] = total.astype(BF)
        mine[w]().start()
        for name in ("z", "y0", "x0"):
            plan.start(f"{name}{w}")

    def own_y(w):
        plan.arrived(f"y0{w}")
        plan.start(f"yx0{w}")

    def whole_slice(w):
        mine[w]().wait()
        plan.arrived(f"z{w}")
        for name in ("y1", "x1", "co"):
            plan.start(f"{name}{w}")

    def slice_y(w):
        plan.arrived(f"y1{w}")
        for name in ("yx1", "cy"):
            plan.start(f"{name}{w}")

    def slice_x(w):
        plan.arrived(f"x0{w}")
        plan.arrived(f"x1{w}")
        plan.start(f"cx{w}")

    def slice_d(w):
        plan.arrived(f"yx0{w}")
        plan.arrived(f"yx1{w}")
        plan.start(f"cd{w}")

    stages = [chunk_start, chunk_b, chunk_z, chunk_g, chunk_h, chunk_done]

    @pl.when(now == 0)
    def _():
        for c in loads:
            c().start()
        partners = [peer("blk", blk, d) for d in range(1, nb)]
        partners += [same_plane(1, d) for d in range(nb)] + [other_plane(d) for d in others]
        arrive(partners)
        small[...] = jnp.zeros_like(small)
        go_acc[...] = jnp.zeros_like(go_acc)
        fill_bias(bias_own, None, False, 0)
        for c in loads:
            c().wait()
        mg, deo = factors[0], factors[1]
        act, slope = gelu_both(nn(mg, win[...]))
        du = (slope * nt(deo, wback[...])).astype(BF)
        g_in = tn(mg, du).astype(BF)
        for n in range(planes):
            ours[0, n] = g_in[n * rows : (n + 1) * rows]
        plan.start("rs0")
        g_back = tn(act.astype(BF), deo).astype(BF)
        for n in range(planes):
            ours[1, n] = g_back[n * rows : (n + 1) * rows]
        plan.start("rs1")

    gate_rows = gate_ref.shape[0]

    @pl.when(now < lead)
    def _():
        at = rows_of(step, BLOCK)
        h = h_ref[0]
        cot_b = cot_ref[0, 0]
        dout = cot_b.astype(F32)
        r2_ = rms(h)
        z = h * r2_
        n2 = (z * g2_ref[...]).astype(BF)
        gate = gate_ref[...]
        gate_b = gate.astype(BF)
        gate_low = (gate - gate_b.astype(F32)).astype(BF)
        eo = jnp.concatenate([eo_ref[j] for j in range(eo_ref.shape[0])], axis=0)
        dmg = jnp.concatenate([dmg_ref[j] for j in range(dmg_ref.shape[0])], axis=0).astype(BF)
        eo_b = eo.astype(BF)
        eo_low = (eo - eo_b.astype(F32)).astype(BF)
        mixed = tn(
            jnp.concatenate([gate_b, gate_low, gate_b], axis=0),
            jnp.concatenate([eo_b, eo_b, eo_low], axis=0),
        )
        act_buf[micro, step] = (h + mixed).astype(BF)
        for m in range(micros):
            pl.when(micro == m)(functools.partial(acts[m].start, step))
        dw2 = nt(jnp.concatenate([eo_b, eo_low], axis=0), cot_b)
        dw = dw2[:gate_rows] + dw2[gate_rows:] + nt(dmg, n2)
        wdw = gate * dw
        dlog = (wdw - gate * jnp.sum(wdw, axis=1, keepdims=True)).astype(BF)
        dn2 = tn(
            jnp.concatenate([gate_b, dlog], axis=0),
            jnp.concatenate([dmg, wc_ref[...]], axis=0),
        )
        small[0:gate_rows, :] += nn(dlog, n2)
        small[gate_rows : gate_rows + 1, :] += jnp.sum(dn2 * z, axis=0, keepdims=True)
        a = dn2 * g2_ref[...]
        dh = dout + r2_ * (a - z * jnp.mean(a * z, axis=-1, keepdims=True))
        dh_all[micro, at, :] = dh
        da = dh.astype(BF)
        dob_b = nt(da, wo_ref[...]).astype(BF)
        dob[micro, at, :] = dob_b
        ob = ob_ref[0]
        go_acc[...] += tn(ob, da)
        prod = dob_b.astype(F32) * ob.astype(F32)
        high = prod.astype(BF)
        low = (prod - high.astype(F32)).astype(BF)
        heads = head_rows(delta.shape[1], width)
        delta[micro, :, at] = nt(heads, high) + nt(heads, low)
        x = x_ref[0, step].astype(F32)
        n1_all[micro, at, :] = (x * rms(x) * g1_ref[...]).astype(BF)

    for m in range(1, micros):
        for i in range(blocks):
            pl.when(now == m * blocks + i)(
                functools.partial(fill_bias, bias.at[i], start_ref[i], True, i)
            )

    masks = head_masks()

    def attend(m):
        hp = step
        packed = m > 0
        lanes = rows_of(hp, pair_lanes)
        for i in range(blocks):
            low, count = key_range(packed, i)
            at = slice(i * BLOCK, (i + 1) * BLOCK)
            q_pair, dob_pair = q_ref[0, at, :], dob[m, at, lanes]
            k_pair, v_pair = k_ref[0, low : low + count, :], v_ref[0, low : low + count, :]
            dk_sum = dv_sum = None
            dqs = []
            for h in range(2):
                qm, dm = q_pair * masks[h], dob_pair * masks[h]
                scores = add_bias(nt(k_pair, qm), bias.at[i] if packed else bias_own, packed, count)
                p = jnp.exp(scores * SCALE - lse_ref[0, pl.ds(hp * 2 + h, 1), at])
                dp_ = nt(v_pair, dm)
                ds = (p * (dp_ - delta[m, pl.ds(hp * 2 + h, 1), at])).astype(BF)
                kt = kt_ref[0, h * HEAD_DIM : (h + 1) * HEAD_DIM, low : low + count]
                dqs.append(nn(kt, ds) * SCALE)
                dk_part, dv_part = nn(ds, qm), nn(p.astype(BF), dm)
                dk_sum = dk_part if dk_sum is None else dk_sum + dk_part
                dv_sum = dv_part if dv_sum is None else dv_sum + dv_part
            old = i * BLOCK - low
            dk_acc[at, :] = dk_sum[old:]
            dv_acc[at, :] = dv_sum[old:]
            if old:
                dk_acc[low : i * BLOCK, :] += dk_sum[:old]
                dv_acc[low : i * BLOCK, :] += dv_sum[:old]
            dq_all[at, lanes] = jnp.concatenate(dqs, axis=0).T.astype(BF)
        dk = (dk_acc[...] * SCALE).astype(BF)
        dv = dv_acc[...].astype(BF)
        dk_all[:, lanes] = dk
        dv_all[:, lanes] = dv
        g = tn(n1_all[m], jnp.concatenate([dq_all[:, lanes], dk, dv], axis=1))
        if packed:
            gacc[hp] += g
        else:
            gacc[hp] = g

    for m in range(micros):
        in_phase = (now >= lead) & (micro == m) & (step < pairs)
        pl.when(in_phase)(functools.partial(attend, m))

    in_third = (now >= lead) & (step >= pairs)
    i = blk ^ (nb - 1 - (step - pairs))

    @pl.when(in_third)
    def _():
        at = rows_of(i, BLOCK)
        x = x_ref[0, i].astype(F32)
        r1_ = rms(x)
        z1 = x * r1_
        dn1 = (
            nt(dq_all[at, :], wq_ref[...]) + nt(dk_all[at, :], wk_ref[...]) + nt(dv_all[at, :], wv_ref[...])
        )
        small[gate_rows + 8 : gate_rows + 9, :] += jnp.sum(dn1 * z1, axis=0, keepdims=True)
        b = dn1 * g1_ref[...]
        gi = dh_all[micro, at, :] + r1_ * (b - z1 * jnp.mean(b * z1, axis=-1, keepdims=True))
        gi_buf[micro, i] = gi.astype(BF)

    final = lead + micros * span - 1
    tasks = {}

    def after(at, task, *args):
        tasks.setdefault(min(at, final), []).append(functools.partial(task, *args))

    def far_block(d):
        gis[0].copy(d).start()

    for n, gap in enumerate((0, 2, 5, 8, 10, 12)):
        after(lead - 1 + gap, stages[n], 0)
    for c in range(1, pairs):
        for n, gap in enumerate((0, 1, 3, 5, 6, 7)):
            after(last + c - 1 + gap, stages[n], c)
    c = pairs
    after(last + c - 1, chunk_start, c)
    after(last + c, chunk_b, c)
    after(last + c + 2, chunk_z, c)
    after(blocks, reduced, 0)
    after(lead, reduced, 1)
    after(lead, own_y, 0)
    after(lead + 2, whole_slice, 0)
    after(lead + 2, own_y, 1)
    after(last - 1, slice_y, 0)
    after(last - 1, whole_slice, 1)
    after(last + pairs - 2, slice_y, 1)
    after(last + pairs - 2, slice_x, 0)
    after(final, slice_x, 1)
    after(final, slice_d, 0)
    for d in range(2, nb):
        after(last + 2 * (d - 2), far_block, d)
    for at, todo in tasks.items():
        if at < final:

            @pl.when(now == at)
            def _(todo=todo):
                for task in todo:
                    task()

    @pl.when(in_third)
    def _():
        for m in range(micros):
            pl.when(micro == m)(functools.partial(gis[m].start, i, 2 if m == 0 else nb))

    @pl.when(now == final)
    def _():
        per = gate_rows // 2
        few[0] = jnp.concatenate(
            [jnp.sum(small[n * per : (n + 1) * per, :], axis=0, keepdims=True) for n in range(2)]
            + [small[gate_rows : gate_rows + 1, :], small[gate_rows + 8 : gate_rows + 9, :]]
            + [jnp.zeros((4, width), F32)],
            axis=0,
        )
        plan.start("sb")
        for task in tasks[final]:
            task()
        chunk_g(c)
        plan.arrived("sb")
        few[1] = pair_sum([few[0]] + [rs[n] for n in range(len(near))])
        plan.start("sz")
        chunk_h(c)
        slice_d(1)
        chunk_done(c)
        plan.arrived("sz")
        small_ref[...] = pair_sum([few[1]] + [rs[len(near) + d - 1] for d in others])
        for w in both:
            for name in "oyxd":
                plan.arrived(f"c{name}{w}")
        for n in range(pairs + 1):
            out_copy(n).wait()
        for name in plan.sets:
            plan.sent(name)
        for r in acts + gis:
            r.wait()


def whole(shape):
    return pl.BlockSpec(shape, lambda *_: (0,) * len(shape))


def held(shape):
    return pl.BlockSpec(shape, lambda *_: (0,) * len(shape), pipeline_mode=pl.Buffered(1))


ANY = pl.BlockSpec(memory_space=pl.ANY)
DMA = pltpu.SemaphoreType.DMA


def shaped(shape, dtype):
    return jax.ShapeDtypeStruct(shape, dtype)


def params(number):
    return pltpu.CompilerParams(
        vmem_limit_bytes=VMEM_LIMIT, collective_id=number, has_side_effects=True
    )


def forward_call(x, seg, cot, g1, wq, wk, wv, wo, g2, wc):
    nb = lax.axis_size("blk")
    micros, _, rows_in, width = x.shape
    length = nb * rows_in
    blocks = length // BLOCK
    assert x.shape[1] == nb and rows_in == BLOCK
    rows = wc.shape[0]
    heads = width // HEAD_DIM
    per = BLOCK // GROUP
    experts = rows // per
    span = 2 * blocks
    phase = lambda s: jnp.maximum(s % span - blocks, 0)
    whole_micro = lambda a, b: pl.BlockSpec((1, a, b), lambda s: (s // span, 0, 0))
    flat = lambda s: (s // span) * blocks + phase(s)
    moves = 2 * micros + 1
    return pl.pallas_call(
        functools.partial(forward_kernel, micros, blocks, nb),
        grid=(micros * span,),
        in_specs=[ANY, ANY, ANY] + [held(a.shape) for a in (g1, wq, wk, wv, wo, g2, wc)],
        out_specs=[
            whole_micro(length, width), whole_micro(length, width), whole_micro(length, width),
            whole_micro(width, length),
            pl.BlockSpec((1, BLOCK, width), lambda s: (s // span, phase(s), 0)),
            pl.BlockSpec((1, heads, BLOCK), lambda s: (s // span, 0, phase(s))),
            pl.BlockSpec((1, BLOCK, width), lambda s: (s // span, phase(s), 0)),
            pl.BlockSpec((rows, BLOCK), lambda s: (0, flat(s))),
            pl.BlockSpec((experts, per, width), lambda s: (0, flat(s), 0)),
            whole((blocks, 1, BLOCK)), ANY, ANY,
        ],
        out_shape=[
            shaped((micros, length, width), BF), shaped((micros, length, width), BF),
            shaped((micros, length, width), BF), shaped((micros, width, length), BF),
            shaped((micros, length, width), BF), shaped((micros, heads, length), F32),
            shaped((micros, length, width), F32), shaped((rows, micros * length), F32),
            shaped((experts, micros * length // GROUP, width), F32),
            shaped((blocks, 1, BLOCK), jnp.int32), shaped(x.shape, BF), shaped(x.shape, BF),
        ],
        scratch_shapes=[
            pltpu.VMEM(x.shape, BF), pltpu.VMEM(seg.shape, seg.dtype),
            pltpu.VMEM((length, BLOCK), F32), pltpu.VMEM((BLOCK, width), F32),
            pltpu.VMEM((heads, BLOCK), F32), pltpu.VMEM((width, width), BF),
            DMA((moves + 1,)), DMA((moves * (nb - 1),)), DMA((moves * (nb - 1),)),
        ],
        compiler_params=params(1),
        name="attention_forward",
    )(x, seg, cot, g1, wq, wk, wv, wo, g2, wc)


def experts_call(mg, gate, cot, w_in, w_back):
    micros, nb, _, width = cot.shape
    experts, groups, _ = mg.shape
    ff = w_in.shape[2]
    blocks = gate.shape[1] // BLOCK // micros
    chunk = min(CHUNK, ff)
    by_expert = lambda n: pl.BlockSpec((1, n, width), lambda e, c: (e, 0, 0))
    members = 2 * nb
    return pl.pallas_call(
        functools.partial(experts_kernel, micros, blocks, nb),
        grid=(experts, ff // chunk),
        in_specs=[
            held(mg.shape), held(gate.shape), held(cot.shape),
            pl.BlockSpec((1, width, chunk), lambda e, c: (e, 0, c)),
            pl.BlockSpec((1, chunk, width), lambda e, c: (e, c, 0)),
        ],
        out_specs=[by_expert(groups)] * 2 + [whole((2, members * groups, width))],
        out_shape=[shaped((experts, groups, width), F32)] * 2
        + [shaped((2, members * groups, width), BF)],
        scratch_shapes=[
            pltpu.VMEM((experts, 2, groups, width), BF),
            pltpu.VMEM((members - 1, 2, groups, width), BF), DMA((members - 1,)), DMA((members - 1,)),
        ],
        compiler_params=params(2),
        name="experts",
    )(mg, gate, cot, w_in, w_back)


def backward_call(x, cot, h, gate, eo, dmg, ob, lse, q, k, v, kt, start, g1, g2, wc, wq, wk, wv, wo,
                  factors, w_in, w_back):
    micros, nb, _, width = x.shape
    planes = lax.axis_size("dp") // 2
    length = q.shape[1]
    blocks = length // BLOCK
    rows = wc.shape[0]
    per = BLOCK // GROUP
    experts = rows // per
    heads = width // HEAD_DIM
    pairs = heads // 2
    ff = w_in.shape[2]
    cut = ff // nb
    assert cut == width
    members = len(plane_steps(nb)) + 1
    lead, span = micros * blocks, blocks + pairs
    flat = lambda s: jnp.minimum(s, lead - 1)
    m_late = lambda s: jnp.maximum(s - lead, 0) // span
    m_of = lambda s: jnp.where(s < lead, s // blocks, m_late(s))
    pair_of = lambda s: jnp.minimum(jnp.maximum(s - lead, 0) % span, pairs - 1)
    row_block = pl.BlockSpec((1, BLOCK, width), lambda s: (flat(s) // blocks, flat(s) % blocks, 0))
    group_block = pl.BlockSpec((experts, per, width), lambda s: (0, flat(s), 0))
    pair_block = pl.BlockSpec((1, length, 2 * HEAD_DIM), lambda s: (m_late(s), 0, pair_of(s)))
    piece = (2, width // planes, cut)
    chunk = width
    chunks = pairs + 1
    half = chunk // 2
    quarter = half // members
    reach = max(key_range(True, i)[1] for i in range(blocks))
    small = (rows + 16, width)
    few = (8, width)
    vm = pltpu.VMEM
    copies = 96 + 16 * chunks + 32 * planes
    return pl.pallas_call(
        functools.partial(backward_kernel, micros, blocks, nb, planes),
        grid=(lead + micros * span,),
        in_specs=[
            pl.BlockSpec((1, nb, BLOCK, width), lambda s: (m_of(s), 0, 0, 0)),
            pl.BlockSpec((1, 1, BLOCK, width), lambda s: (flat(s) // blocks, flat(s) % blocks, 0, 0)),
            row_block,
            pl.BlockSpec((rows, BLOCK), lambda s: (0, flat(s))),
            group_block, group_block, row_block,
            pl.BlockSpec((1, heads, length), lambda s: (m_late(s), 0, 0)),
            pair_block, pair_block, pair_block,
            pl.BlockSpec((1, 2 * HEAD_DIM, length), lambda s: (m_late(s), pair_of(s), 0)),
        ] + [held(a.shape) for a in (start, g1, g2, wc, wq, wk, wv, wo, factors)] + [ANY, ANY],
        out_specs=[ANY, ANY, ANY, whole(few), ANY, ANY],
        out_shape=[
            shaped(x.shape, BF), shaped(x.shape, BF), shaped((chunks, chunk, width), BF),
            shaped(few, F32), shaped(w_in.shape, BF), shaped(w_back.shape, BF),
        ],
        scratch_shapes=[
            vm((micros, length, width), F32), vm((micros, length, width), BF),
            vm((micros, length, width), BF), vm((micros, heads, length), F32), vm((length, width), BF), vm((length, width), BF),
            vm((length, width), BF), vm((length, 2 * HEAD_DIM), F32), vm((length, 2 * HEAD_DIM), F32),
            vm((pairs, width, 6 * HEAD_DIM), F32), vm((width, width), F32), vm((BLOCK, BLOCK), F32),
            vm((blocks, reach, BLOCK), F32),
            vm(x.shape, BF), vm(x.shape, BF), vm((width, cut), BF), vm((cut, width), BF),
            vm((2, planes) + piece[1:], BF), vm((2, planes - 1) + piece[1:], BF), vm(piece, BF),
            vm((chunks, half, width), BF), vm((chunks, half, width), BF),
            vm((chunks, members - 1, quarter, width), BF), vm((chunks, members - 1, quarter, width), BF),
            vm((chunks, quarter, width), BF), vm((chunks, planes - 1, quarter, width), BF),
            vm((chunks, chunk, width), BF), vm(small, F32), vm((2,) + few, F32),
            vm((2 * nb + planes - 2,) + few, F32),
            DMA((2 * micros,)), DMA((5 + pairs,)), DMA((2 * micros * (nb - 1),)),
            DMA((2 * micros * (nb - 1),)), DMA((copies,)), DMA((copies,)),
        ],
        compiler_params=params(3),
        name="attention_backward",
    )(x, cot, h, gate, eo, dmg, ob, lse, q, k, v, kt, start, g1, g2, wc, wq, wk, wv, wo, factors, w_in,
      w_back)


def local(block_input, segment_ids, gain_one, w_query, w_key, w_value, w_out, gain_two, w_ctrl,
          w_in, w_back, cotangent):
    micros, seqs, rows, width = block_input.shape
    experts, _, ff = w_in.shape
    nb = lax.axis_size("blk")
    per = BLOCK // GROUP
    g1, g2 = gain_one.reshape(1, width), gain_two.reshape(1, width)
    wc = jnp.repeat(w_ctrl.T, per, axis=0)
    seg = segment_ids.reshape(nb, 2, rows // 2)
    q, k, v, kt, ob, lse, h, gate, mg, start, x, cot = forward_call(
        block_input, seg, cotangent, g1, w_query, w_key, w_value, w_out, g2, wc
    )
    eo, dmg, factors = experts_call(mg, gate, cot, w_in, w_back)
    acts, gis, flat, small, grad_in, grad_back = backward_call(
        x, cot, h, gate, eo, dmg, ob, lse, q, k, v, kt, start, g1, g2, wc, w_query, w_key, w_value,
        w_out, factors, w_in, w_back,
    )
    lanes = 2 * HEAD_DIM
    one = lambda n: jnp.concatenate(
        [flat[c, :, n * lanes : (n + 1) * lanes] for c in range(1, flat.shape[0])], axis=1
    ).astype(F32)
    return (
        acts, gis, small[3], one(0), one(1), one(2), flat[0].astype(F32), small[2], small[:experts].T,
        grad_in.astype(F32), grad_back.astype(F32),
    )


def solution(mesh):
    data = P(None, "dp", "blk", None)
    in_specs = (data, P("dp", "blk")) + (P(),) * 9 + (data,)
    out_specs = (data, data) + (P(),) * 9
    return jax.shard_map(local, mesh=mesh, in_specs=in_specs, out_specs=out_specs, check_vma=False)
```
